32 devices in a mesh: case: 2 (over y), gx: 4 (over z), gy: 4 (over x, core).
Axes of the slice: x: 2, y: 2, z: 4, core: 2. Of those that a mesh axis runs over, the one named last changes fastest.
Arguments:
- features: bfloat16 [10, 512, 1024], P(None, ('case', 'gx'), 'gy'), parts along dimension 1, may hold values from -6 to 6
- source: bfloat16 [5, 512, 1024], P(None, ('case', 'gx'), 'gy'), parts along dimension 1, may hold values from -4.2 to 5.6
- coupling: bfloat16 [4, 512, 1024], P(None, ('case', 'gx'), 'gy'), parts along dimension 1, may hold values from 0.16992188 to 0.33984375
- diagonal: float32 [512, 1024], P(('case', 'gx'), 'gy'), parts along dimension 0, may hold values from 0.8 to 1
- production: float32 [512, 1024], P(('case', 'gx'), 'gy'), parts along dimension 0, may hold values from -6 to 6
- bc_code: int32 [512, 1024], P(('case', 'gx'), 'gy'), parts along dimension 0, may hold values from 0 to 2, as said below
- mixing: float32 [5, 5], replicated, may hold values from -0.15 to 0.9
- weight_in: bfloat16 [10, 64], replicated, may hold values from -2 to 2
- weight_mid: bfloat16 [64, 64], replicated, may hold values from -0.75 to 0.75
- weight_top: bfloat16 [64, 64], replicated, may hold values from -0.75 to 0.75
- weight_out: float32 [64], replicated, may hold values from -0.75 to 0.75
- biases: float32 [3, 64], replicated, may hold values from -3 to 3
Outputs:
- adjoint: float32 [5, 512, 1024], P(None, ('case', 'gx'), 'gy'), parts along dimension 1
- beta_field: float32 [512, 1024], P(('case', 'gx'), 'gy'), parts along dimension 0
- grad_in: float32 [20, 64], P('case'), parts along dimension 0
- grad_mid: float32 [128, 64], P('case'), parts along dimension 0
- grad_top: float32 [128, 64], P('case'), parts along dimension 0
- grad_out: float32 [128], P('case'), parts along dimension 0
- grad_bias: float32 [6, 64], P('case'), parts along dimension 0
The draws below stay inside these ranges and needn't reach their ends.
There are 2 independent parts, one for each index of `case`. The reference program is written for one: setup_inputs(seed, part) draws one part's arguments, and reference() takes and returns one part's arrays. A program takes and returns all parts, laid end to end along the dimension named above; an argument that names none is the same for every part. Nothing has to cross between parts.
Inputs may be any that keep to these rules, and one draw needn't show every extreme that they name: `bc_code`: 0 marks an interior cell, 1 a wall cell, 2 a far-field cell.
All inputs are finite; a program needn't handle non-finite values.
Results may differ from the reference program's by a relative error of at most 0.0038.
Values sent between devices are 32-bit elements; how exact they have to be, the bound alone decides.
No kernel may reach another device: no remote copies, remote signals or barrier semaphores. Data moves between devices by JAX's collectives and lax.ppermute only.
A program may use at most 64 MiB of HBM per device.

```python
import math
import jax
import jax.numpy as jnp
from jax import lax

NF = 10
H = 64
NV = 5
SWEEPS = 6
NX = 256
NY = 1024


def draw_source(key, part):
    key = jax.random.fold_in(key, 11)
    key_rough = jax.random.fold_in(key, 0)
    rough = jax.random.truncated_normal(key_rough, -6.0, 6.0, (NV, NX, NY), jnp.float32)
    values = 0.8 * rough + 0.6
    return values.astype(jnp.bfloat16)


def draw_mixing(key, part):
    key = jax.random.fold_in(key, 7)
    key_off, key_main = jax.random.split(key)
    off_diag = jax.random.uniform(key_off, (NV, NV), jnp.float32, -0.15, 0.15)
    main_diag = jax.random.uniform(key_main, (NV, NV), jnp.float32, 0.75, 0.9)
    rows_iota = lax.broadcasted_iota(jnp.int32, (NV, NV), 0)
    cols_iota = lax.broadcasted_iota(jnp.int32, (NV, NV), 1)
    return jnp.where(rows_iota == cols_iota, main_diag, off_diag)


def draw_bc_code(key, part):
    key = jax.random.fold_in(key, 5)
    rolls = jax.random.randint(key, (NX, NY), 0, 16)
    codes = jnp.where(rolls == 15, 2, jnp.where(rolls == 14, 1, 0))
    return codes.astype(jnp.int32)


def block_scale(stream_key, dims, pieces, least, high):
    def one(axis_at, shards_of):
        draws = jax.random.uniform(jax.random.fold_in(jax.random.fold_in(stream_key, 6), axis_at), (shards_of,), jnp.float32, least / len(pieces), high / len(pieces))
        return jnp.repeat(jnp.exp(draws), dims[axis_at] // shards_of).reshape((-1,) + (1,) * (len(dims) - axis_at - 1))

    factor_of = one(*pieces[0])
    for cut in pieces[1:]:
        factor_of = factor_of * one(*cut)
    return factor_of


def centred(rng, shape, scale, most, cuts=(), held_as=jnp.bfloat16):
    entries = jax.random.normal(rng, shape, jnp.float32) * scale
    if len(cuts) > 0:
        entries = block_scale(rng, shape, cuts, -0.22, 0.18) * entries
    return jnp.clip(entries, min=-most, max=most).astype(held_as)


def setup_inputs(seed: int = 0, part: int = 0) -> dict:
    arg_keys = jax.random.split(jax.random.key(seed), 13)
    part_keys = jax.random.split(jax.random.fold_in(arg_keys[12], part), 13)
    return {
        "features": centred(part_keys[0], (NF, NX, NY), 1.0, 6.0, ((1, 4), (2, 4))),
        "source": draw_source(jax.random.fold_in(jax.random.fold_in(arg_keys[12], part), 71), part),
        "coupling": jnp.clip(jnp.exp(math.log(0.33984375) - 0.6931472 * jax.random.uniform(part_keys[2], (4, NX, NY), jnp.float32) ** block_scale(part_keys[2], (4, NX, NY), ((1, 4), (2, 4)), -0.2, 0.2)), 0.16992188, 0.33984375).astype(jnp.bfloat16),
        "diagonal": jnp.clip(0.8 + 0.19999999 * jax.random.uniform(part_keys[3], (NX, NY), jnp.float32) ** block_scale(part_keys[3], (NX, NY), ((0, 4), (1, 4)), -0.2, 0.2), 0.8, 1.0),
        "production": centred(part_keys[4], (NX, NY), 1.0, 6.0, ((0, 4), (1, 4)), jnp.float32),
        "bc_code": draw_bc_code(jax.random.fold_in(jax.random.fold_in(arg_keys[12], part), 71), part),
        "mixing": draw_mixing(jax.random.fold_in(arg_keys[12], 71), part),
        "weight_in": centred(arg_keys[7], (NF, H), NF ** -0.5, 2.0),
        "weight_mid": centred(arg_keys[8], (H, H), H ** -0.5, 0.75),
        "weight_top": centred(arg_keys[9], (H, H), H ** -0.5, 0.75),
        "weight_out": centred(arg_keys[10], (H,), H ** -0.5, 0.75, (), jnp.float32),
        "biases": centred(arg_keys[11], (3, H), 0.5, 3.0, (), jnp.float32),
    }


WALL_EXTRA = 0.2
FAR_EXTRA = 0.6
REG_WEIGHT = 0.5
CLIP_NORM = 64.0
HIGHEST_PREC = lax.Precision.HIGHEST

def total_diagonal(diagonal, bc_code):
    return diagonal + jnp.where(bc_code == 1, WALL_EXTRA, 0.0) + jnp.where(bc_code == 2, FAR_EXTRA, 0.0)

def mix_vars(mixing, values):
    return jnp.einsum('ba,bxy->axy', mixing, values, precision=HIGHEST_PREC)

def incoming(couple_f, adjoint):
    flux_east = couple_f[0][None] * adjoint
    flux_west = couple_f[1][None] * adjoint
    flux_north = couple_f[2][None] * adjoint
    flux_south = couple_f[3][None] * adjoint
    total = jnp.pad(flux_east, ((0, 0), (1, 0), (0, 0)))[:, :-1, :]
    total = total + jnp.pad(flux_west, ((0, 0), (0, 1), (0, 0)))[:, 1:, :]
    total = total + jnp.pad(flux_north, ((0, 0), (0, 0), (1, 0)))[:, :, :-1]
    total = total + jnp.pad(flux_south, ((0, 0), (0, 0), (0, 1)))[:, :, 1:]
    return total

def forward(block_in, weight_in, weight_mid, weight_top, weight_out, biases):
    first = jnp.dot(weight_in.T, block_in, preferred_element_type=jnp.float32)
    layer_one = jnp.tanh(first + biases[0][:, None]).astype(jnp.bfloat16)
    second = jnp.dot(weight_mid.T, layer_one, preferred_element_type=jnp.float32)
    layer_two = jnp.tanh(second + biases[1][:, None]).astype(jnp.bfloat16)
    third = jnp.dot(weight_top.T, layer_two, preferred_element_type=jnp.float32)
    layer_three = jnp.tanh(third + biases[2][:, None]).astype(jnp.bfloat16)
    beta_vals = 1.0 + jnp.dot(weight_out, layer_three.astype(jnp.float32), precision=HIGHEST_PREC)
    return (layer_one, layer_two, layer_three, beta_vals)

def backward(block_in, layer_one, layer_two, layer_three, beta_vals, adj_last, prod_blk, weight_mid, weight_top, weight_out):
    sens = adj_last * prod_blk + REG_WEIGHT * (beta_vals - 1.0)
    three_f = layer_three.astype(jnp.float32)
    two_f = layer_two.astype(jnp.float32)
    one_f = layer_one.astype(jnp.float32)
    grad_out = jnp.dot(three_f, sens, precision=HIGHEST_PREC)
    delta_three = sens[None, :] * weight_out[:, None] * (1.0 - three_f * three_f)
    bias_three = lax.optimization_barrier(jnp.sum(delta_three, axis=1))
    delta_three = delta_three.astype(jnp.bfloat16)
    grad_top = jnp.dot(layer_two, delta_three.T, preferred_element_type=jnp.float32)
    delta_two = jnp.dot(weight_top, delta_three, preferred_element_type=jnp.float32) * (1.0 - two_f * two_f)
    bias_two = lax.optimization_barrier(jnp.sum(delta_two, axis=1))
    delta_two = delta_two.astype(jnp.bfloat16)
    grad_mid = jnp.dot(layer_one, delta_two.T, preferred_element_type=jnp.float32)
    delta_one = jnp.dot(weight_mid, delta_two, preferred_element_type=jnp.float32) * (1.0 - one_f * one_f)
    bias_one = lax.optimization_barrier(jnp.sum(delta_one, axis=1))
    delta_one = delta_one.astype(jnp.bfloat16)
    grad_in = jnp.dot(block_in, delta_one.T, preferred_element_type=jnp.float32)
    return (grad_in, grad_mid, grad_top, grad_out, jnp.stack([bias_one, bias_two, bias_three]))

def clip_all(grads):
    squares = sum((jnp.sum(item * item) for item in grads))
    factor = CLIP_NORM / jnp.maximum(jnp.sqrt(squares), CLIP_NORM)
    return tuple((item * factor for item in grads))

def reference(features, source, coupling, diagonal, production, bc_code, mixing, weight_in, weight_mid, weight_top, weight_out, biases):
    diag_total = total_diagonal(diagonal, bc_code)
    source_f = source.astype(jnp.float32)
    couple_f = coupling.astype(jnp.float32)
    adjoint = source_f / diag_total[None]
    for sweep_idx in range(SWEEPS):
        adjoint = (source_f + mix_vars(mixing, incoming(couple_f, adjoint))) / diag_total[None]
    rows_blk = math.gcd(NX, 16)
    blocks = NX // rows_blk
    width = rows_blk * NY
    feats = features.reshape(NF, blocks, width).transpose(1, 0, 2)
    adj_last = adjoint[NV - 1].reshape(blocks, width)
    prods = production.reshape(blocks, width)

    def step(carry, items):
        block_in, adj_blk, prod_blk = items
        layer_one, layer_two, layer_three, beta_vals = forward(block_in, weight_in, weight_mid, weight_top, weight_out, biases)
        grads = backward(block_in, layer_one, layer_two, layer_three, beta_vals, adj_blk, prod_blk, weight_mid, weight_top, weight_out)
        return (tuple((a + b for a, b in zip(carry, grads))), beta_vals)
    init = (jnp.zeros((NF, H), jnp.float32), jnp.zeros((H, H), jnp.float32), jnp.zeros((H, H), jnp.float32), jnp.zeros((H,), jnp.float32), jnp.zeros((3, H), jnp.float32))
    totals, betas = lax.scan(step, init, (feats, adj_last, prods))
    beta_field = betas.reshape(NX, NY)
    grad_in, grad_mid, grad_top, grad_out, grad_bias = clip_all(totals)
    return (adjoint, beta_field, grad_in, grad_mid, grad_top, grad_out, grad_bias)
```

```python
import functools

import jax
import jax.numpy as jnp
from jax import lax
from jax.experimental import pallas as pl
from jax.experimental.pallas import tpu as pltpu
from jax.sharding import PartitionSpec as P

SWEEPS = 6
WALL_EXTRA = 0.2
FAR_EXTRA = 0.6
REG_WEIGHT = 0.5
CLIP_NORM = 64.0
EDGE = 8
SUB, LANE = 8, 128
F32, BF16 = jnp.float32, jnp.bfloat16
NT = (((1,), (1,)), ((), ()))
TN = (((0,), (0,)), ((), ()))
VMEM_BYTES = 48 * 1024 * 1024


def whole(shape):
    return pl.BlockSpec(shape, lambda *_: (0,) * len(shape))


def params():
    return pltpu.CompilerParams(vmem_limit_bytes=VMEM_BYTES)


def inverse_diag(diag, code):
    total = diag + jnp.where(code == 1, WALL_EXTRA, 0.0) + jnp.where(code == 2, FAR_EXTRA, 0.0)
    return 1.0 / total


def rows_kernel(src_t, src_b, cpl_t, cpl_b, dia_t, dia_b, bc_t, bc_b, top_ref, bottom_ref):
    nv, nc = src_t.shape[0], cpl_t.shape[0]
    last = src_b.shape[1] - EDGE
    for v in range(nv):
        top_ref[v] = src_t[v].astype(F32)[:EDGE]
        bottom_ref[v] = src_b[v].astype(F32)[last:]
    for d in range(nc):
        top_ref[nv + d] = cpl_t[d].astype(F32)[:EDGE]
        bottom_ref[nv + d] = cpl_b[d].astype(F32)[last:]
    top_ref[nv + nc] = inverse_diag(dia_t[...], bc_t[...])
    bottom_ref[nv + nc] = inverse_diag(dia_b[...], bc_b[...])


def row_slabs(source, coupling, diagonal, bc_code):
    nv, rows, cols = source.shape
    nc = coupling.shape[0]
    slab = jax.ShapeDtypeStruct((nv + nc + 1, EDGE, cols), F32)
    tall = rows // 16 - 1

    def pair(count):
        return [
            pl.BlockSpec((count, 16, cols), lambda i: (0, 0, 0)),
            pl.BlockSpec((count, 16, cols), lambda i: (0, tall, 0)),
        ]

    flat = [
        pl.BlockSpec((EDGE, cols), lambda i: (0, 0)),
        pl.BlockSpec((EDGE, cols), lambda i: (rows // EDGE - 1, 0)),
    ]
    return pl.pallas_call(
        rows_kernel,
        grid=(1,),
        in_specs=pair(nv) + pair(nc) + flat + flat,
        out_specs=[whole(slab.shape)] * 2,
        out_shape=[slab, slab],
        compiler_params=params(),
        name="row_slabs",
    )(source, source, coupling, coupling, diagonal, diagonal, bc_code, bc_code)


def cols_kernel(src_w, src_e, cpl_w, cpl_e, dia_w, dia_e, bc_w, bc_e, north, south, west_ref, east_ref):
    nv, rows, _ = src_w.shape
    nc = cpl_w.shape[0]
    cols = north.shape[2]
    lane = lax.broadcasted_iota(jnp.int32, (rows, LANE), 1) // EDGE
    lane_h = lane[:EDGE]
    sides = (
        (west_ref, src_w, cpl_w, dia_w, bc_w, slice(0, LANE), 0),
        (east_ref, src_e, cpl_e, dia_e, bc_e, slice(cols - LANE, cols), EDGE),
    )
    for out, src, cpl, dia, bc, window, extra in sides:
        mid = jnp.zeros((rows, LANE), F32)
        up = jnp.zeros((EDGE, LANE), F32)
        down = jnp.zeros((EDGE, LANE), F32)
        for f in range(nv + nc + 1):
            if f < nv:
                x = src[f].astype(F32)
            elif f < nv + nc:
                x = cpl[f - nv].astype(F32)
            else:
                x = inverse_diag(dia[...], bc[...])
            shift = (EDGE * f + extra) % LANE
            mid = jnp.where(lane == f, pltpu.roll(x, shift, 1), mid)
            up = jnp.where(lane_h == f, pltpu.roll(north[f, :, window], shift, 1), up)
            down = jnp.where(lane_h == f, pltpu.roll(south[f, :, window], shift, 1), down)
        out[0:EDGE] = up
        out[EDGE : EDGE + rows] = mid
        out[EDGE + rows :] = down


def col_slabs(source, coupling, diagonal, bc_code, north, south):
    nv, rows, cols = source.shape
    nc = coupling.shape[0]
    slab = jax.ShapeDtypeStruct((rows + 2 * EDGE, LANE), F32)
    wide = cols // LANE - 1

    def pair(count):
        return [
            pl.BlockSpec((count, rows, LANE), lambda i: (0, 0, 0)),
            pl.BlockSpec((count, rows, LANE), lambda i: (0, 0, wide)),
        ]

    flat = [
        pl.BlockSpec((rows, LANE), lambda i: (0, 0)),
        pl.BlockSpec((rows, LANE), lambda i: (0, wide)),
    ]
    return pl.pallas_call(
        cols_kernel,
        grid=(1,),
        in_specs=pair(nv) + pair(nc) + flat + flat + [whole(north.shape)] * 2,
        out_specs=[whole(slab.shape)] * 2,
        out_shape=[slab, slab],
        compiler_params=params(),
        name="col_slabs",
    )(source, source, coupling, coupling, diagonal, diagonal, bc_code, bc_code, north, south)


def column_of(row):
    hidden = row.shape[1]
    wide = jnp.concatenate([row, jnp.zeros((1, LANE - hidden), F32)], axis=1)
    return jnp.transpose(jnp.broadcast_to(wide, (LANE, LANE)))[:hidden]


def across(block, width):
    return jnp.concatenate([block] * (width // LANE), axis=1)


def forward_kernel(
    feat_ref, win_ref, wmid_ref, wtop_ref, wout_ref, bias_ref,
    acts_ref, beta_ref,
    w1, x1, w2, w3, cst,
):
    nf, rows, cols = feat_ref.shape
    hidden = wmid_ref.shape[0]
    step_rows = hidden + 16

    @pl.when(pl.program_id(0) == 0)
    def _():
        depth = x1.shape[0]
        x1[...] = jnp.zeros(x1.shape, BF16)
        feat_of = lax.broadcasted_iota(jnp.int32, (nf, depth), 1) // rows
        pick = (feat_of == lax.broadcasted_iota(jnp.int32, (nf, depth), 0)).astype(F32).astype(BF16)
        spread = lax.dot_general(win_ref[...], pick, TN, preferred_element_type=F32)
        col = lax.broadcasted_iota(jnp.int32, (hidden, depth), 1)
        col_f = lax.broadcasted_iota(jnp.int32, (16, depth), 1)
        row_f = lax.broadcasted_iota(jnp.int32, (16, depth), 0)
        for r in range(rows):
            base = r * step_rows
            w1[base : base + hidden] = jnp.where(col % rows == r, spread, 0.0).astype(BF16)
            same = jnp.logical_and(col_f == row_f * rows + r, row_f < nf)
            w1[base + hidden : base + step_rows] = jnp.where(same, 1.0, 0.0).astype(BF16)
        w2[...] = jnp.transpose(wmid_ref[...].astype(F32)).astype(BF16)
        w3[...] = jnp.transpose(wtop_ref[...].astype(F32)).astype(BF16)
        for k in range(3):
            cst[k] = column_of(bias_ref[k : k + 1, :])
        cst[3] = column_of(wout_ref[...])

    x1[0 : nf * rows] = feat_ref[...].reshape(nf * rows, cols)
    per = 2
    b1, b2, b3, wo = (across(cst[k], cols) for k in range(4))
    for g in range(rows // per):
        lo = g * per * step_rows
        first = jnp.dot(w1[lo : lo + per * step_rows], x1[...], preferred_element_type=F32)
        ones = []
        for q in range(per):
            part = first[q * step_rows : (q + 1) * step_rows]
            one = jnp.tanh(part[:hidden] + b1).astype(BF16)
            acts_ref[g * per + q, 0:hidden] = one
            acts_ref[g * per + q, 3 * hidden :] = part[hidden:].astype(BF16)
            ones.append(one)
        second = jnp.dot(w2[...], jnp.concatenate(ones, axis=1), preferred_element_type=F32)
        twos = []
        for q in range(per):
            two = jnp.tanh(second[:, q * cols : (q + 1) * cols] + b2).astype(BF16)
            acts_ref[g * per + q, hidden : 2 * hidden] = two
            twos.append(two)
        third = jnp.dot(w3[...], jnp.concatenate(twos, axis=1), preferred_element_type=F32)
        for q in range(per):
            three = jnp.tanh(third[:, q * cols : (q + 1) * cols] + b3).astype(BF16)
            acts_ref[g * per + q, 2 * hidden : 3 * hidden] = three
            total = jnp.sum(three.astype(F32) * wo, axis=0, keepdims=True)
            beta_ref[g * per + q : g * per + q + 1, :] = 1.0 + total


def forward(features, weight_in, weight_mid, weight_top, weight_out, biases):
    nf, rows, cols = features.shape
    hidden = weight_mid.shape[0]
    blk = 16
    high = 3 * hidden + 16
    depth = -(-nf * blk // LANE) * LANE
    return pl.pallas_call(
        forward_kernel,
        grid=(rows // blk,),
        in_specs=[
            pl.BlockSpec((nf, blk, cols), lambda i: (0, i, 0)),
            whole(weight_in.shape),
            whole(weight_mid.shape),
            whole(weight_top.shape),
            whole(weight_out.shape),
            whole(biases.shape),
        ],
        out_specs=[
            pl.BlockSpec((blk, high, cols), lambda i: (i, 0, 0)),
            pl.BlockSpec((blk, cols), lambda i: (i, 0)),
        ],
        out_shape=[
            jax.ShapeDtypeStruct((rows, high, cols), BF16),
            jax.ShapeDtypeStruct((rows, cols), F32),
        ],
        scratch_shapes=[
            pltpu.VMEM((blk * (hidden + 16), depth), BF16),
            pltpu.VMEM((depth, cols), BF16),
            pltpu.VMEM((hidden, hidden), BF16),
            pltpu.VMEM((hidden, hidden), BF16),
            pltpu.VMEM((4, hidden, LANE), F32),
        ],
        compiler_params=params(),
        cost_estimate=pl.CostEstimate(
            flops=2 * rows * cols * (nf + 2 * hidden) * hidden,
            bytes_accessed=2 * rows * cols * (high + nf),
            transcendentals=3 * rows * cols * hidden,
        ),
        name="network_forward",
    )(features, weight_in, weight_mid, weight_top, weight_out, biases)


def tile_at(ref, lead, t, k):
    return ref[lead + (slice(t * SUB, (t + 1) * SUB), slice(k * LANE, (k + 1) * LANE))]


class Shifts:
    def __init__(self, tiles, lanes):
        self.tiles, self.lanes = tiles, lanes
        sub = lax.broadcasted_iota(jnp.int32, (SUB, LANE), 0)
        lane = lax.broadcasted_iota(jnp.int32, (SUB, LANE), 1)
        self.first_sub, self.last_sub = sub == 0, sub == SUB - 1
        self.first_lane, self.last_lane = lane == 0, lane == LANE - 1

    def above(self, ref, lead, t, k):
        here, other = tile_at(ref, lead, t, k), tile_at(ref, lead, max(t - 1, 0), k)
        return pltpu.roll(jnp.where(self.last_sub, other, here), 1, 0)

    def below(self, ref, lead, t, k):
        here, other = tile_at(ref, lead, t, k), tile_at(ref, lead, min(t + 1, self.tiles - 1), k)
        return pltpu.roll(jnp.where(self.first_sub, other, here), SUB - 1, 0)

    def left(self, ref, lead, t, k):
        here, other = tile_at(ref, lead, t, k), tile_at(ref, lead, t, (k - 1) % self.lanes)
        return pltpu.roll(jnp.where(self.last_lane, other, here), 1, 1)

    def right(self, ref, lead, t, k):
        here, other = tile_at(ref, lead, t, k), tile_at(ref, lead, t, (k + 1) % self.lanes)
        return pltpu.roll(jnp.where(self.first_lane, other, here), LANE - 1, 1)


def sweep_all(src, cpl, dia, bc, north, south, west, east, mix, adj_out, raw, src_x, cpl_x, adj_a, adj_b):
    nv, rows, cols = src.shape
    nc = cpl.shape[0]
    tall = rows + 2 * EDGE
    tiles, lanes = tall // SUB, cols // LANE + 1
    shifts = Shifts(tiles, lanes)
    inner = slice(EDGE, EDGE + rows)
    lane = lax.broadcasted_iota(jnp.int32, (tall, LANE), 1)
    from_east, from_west = lane < EDGE, lane >= LANE - EDGE
    for f in range(nv + nc + 1):
        if f < nv:
            raw[f, inner, 0:cols] = src[f].astype(F32)
        elif f < nv + nc:
            raw[f, inner, 0:cols] = cpl[f - nv].astype(F32)
        else:
            raw[f, inner, 0:cols] = inverse_diag(dia[...], bc[...])
        raw[f, 0:EDGE, 0:cols] = north[f]
        raw[f, EDGE + rows :, 0:cols] = south[f]
        e = pltpu.roll(east[...], (LANE - EDGE * f) % LANE, 1)
        w = pltpu.roll(west[...], (LANE - EDGE - EDGE * f) % LANE, 1)
        raw[f, :, cols:] = jnp.where(from_east, e, jnp.where(from_west, w, 0.0))

    moves = (shifts.above, shifts.below, shifts.left, shifts.right)
    for t in range(tiles):
        for k in range(lanes):
            at = (slice(t * SUB, (t + 1) * SUB), slice(k * LANE, (k + 1) * LANE))
            inv = tile_at(raw, (nv + nc,), t, k)
            for v in range(nv):
                src_x[(v,) + at] = inv * tile_at(raw, (v,), t, k)
            for d in range(nc):
                cpl_x[(d,) + at] = inv * moves[d](raw, (nv + d,), t, k)

    def sweep(old, new, last):
        for t in range(1, tiles - 1) if last else range(tiles):
            for k in range(lanes - 1) if last else range(lanes):
                at = (slice(t * SUB, (t + 1) * SUB), slice(k * LANE, (k + 1) * LANE))
                couple = [cpl_x[(d,) + at] for d in range(nc)]
                total = [src_x[(a,) + at] for a in range(nv)]
                for b in range(nv):
                    inc = couple[0] * moves[0](old, (b,), t, k)
                    for d in range(1, nc):
                        inc = inc + couple[d] * moves[d](old, (b,), t, k)
                    total = [total[a] + mix[b, a] * inc for a in range(nv)]
                if last:
                    at = (slice((t - 1) * SUB, t * SUB), at[1])
                for a in range(nv):
                    new[(a,) + at] = total[a]

    sweep(src_x, adj_a, False)

    @pl.loop(0, (SWEEPS - 2) // 2)
    def _(i):
        sweep(adj_a, adj_b, False)
        sweep(adj_b, adj_a, False)

    sweep(adj_a, adj_out, True)


def backward_kernel(
    src, cpl, dia, bc, prod, beta, north, south, west, east, mix, wmid, wtop, wout, acts,
    adj_out, packed,
    raw, src_x, cpl_x, adj_a, adj_b, sens, sums, g_mid, g_top, g_in,
):
    step = pl.program_id(0)
    nv = src.shape[0]
    blk, _, cols = acts.shape
    hidden = wmid.shape[0]

    @pl.when(step == 0)
    def _():
        sweep_all(
            src, cpl, dia, bc, north, south, west, east, mix, adj_out, raw, src_x, cpl_x, adj_a, adj_b
        )
        sens[...] = adj_out[nv - 1] * prod[...] + REG_WEIGHT * (beta[...] - 1.0)
        sums[...] = jnp.zeros(sums.shape, F32)
        sums[4] = column_of(wout[...])
        g_mid[...] = jnp.zeros(g_mid.shape, F32)
        g_top[...] = jnp.zeros(g_top.shape, F32)
        g_in[...] = jnp.zeros(g_in.shape, F32)

    rows_sens = sens[pl.ds(pl.multiple_of(step * blk, blk), blk), :]
    wo = across(sums[4], cols)

    def fold(x):
        parts = [x[:, k * LANE : (k + 1) * LANE] for k in range(cols // LANE)]
        return functools.reduce(jnp.add, parts)

    ones, twos, feats, d1s, d2s, d3s = [], [], [], [], [], []
    acc = [jnp.zeros((hidden, LANE), F32) for _ in range(4)]
    for q in range(blk):
        one, two = acts[q, 0:hidden], acts[q, hidden : 2 * hidden]
        three_f = acts[q, 2 * hidden : 3 * hidden].astype(F32)
        sen = jnp.broadcast_to(rows_sens[q : q + 1], (hidden, cols))
        acc[0] = acc[0] + fold(three_f * sen)
        d3 = sen * wo * (1.0 - three_f * three_f)
        acc[3] = acc[3] + fold(d3)
        d3 = d3.astype(BF16)
        two_f = two.astype(F32)
        d2 = jnp.dot(wtop[...], d3, preferred_element_type=F32) * (1.0 - two_f * two_f)
        acc[2] = acc[2] + fold(d2)
        d2 = d2.astype(BF16)
        one_f = one.astype(F32)
        d1 = jnp.dot(wmid[...], d2, preferred_element_type=F32) * (1.0 - one_f * one_f)
        acc[1] = acc[1] + fold(d1)
        d1 = d1.astype(BF16)
        ones.append(one)
        twos.append(two)
        feats.append(acts[q, 3 * hidden :])
        d1s.append(d1)
        d2s.append(d2)
        d3s.append(d3)

    def outer(xs, ds):
        return lax.dot_general(
            jnp.concatenate(xs, axis=1), jnp.concatenate(ds, axis=1), NT, preferred_element_type=F32
        )

    g_mid[...] += outer(ones, d2s)
    g_top[...] += outer(twos, d3s)
    g_in[...] += outer(feats, d1s)
    for k in range(4):
        sums[k] += acc[k]

    @pl.when(step == pl.num_programs(0) - 1)
    def _():
        packed[0:hidden, :] = jnp.concatenate([g_mid[...], g_top[...]], axis=1)
        tail = g_in[SUB : 2 * SUB]
        row = lax.broadcasted_iota(jnp.int32, (SUB, hidden), 0)
        for k in range(4):
            line = jnp.sum(jnp.transpose(sums[k]), axis=0, keepdims=True)
            tail = tail + jnp.where(row == k + 2, jnp.broadcast_to(line, (SUB, hidden)), 0.0)
        packed[hidden : hidden + SUB, :] = jnp.concatenate([g_in[0:SUB], tail], axis=1)


def sweeps_and_backward(source, coupling, diagonal, bc_code, production, beta, halos, mixing, weights, acts):
    nv, rows, cols = source.shape
    nc = coupling.shape[0]
    weight_mid, weight_top, weight_out = weights
    hidden = weight_mid.shape[0]
    blk = 8
    tall, wide = rows + 2 * EDGE, cols + LANE
    operands = [source, coupling, diagonal, bc_code, production, beta, *halos]
    return pl.pallas_call(
        backward_kernel,
        grid=(rows // blk,),
        in_specs=[whole(x.shape) for x in operands]
        + [pl.BlockSpec(memory_space=pltpu.SMEM)]
        + [whole(x.shape) for x in weights]
        + [pl.BlockSpec((blk,) + acts.shape[1:], lambda i: (i, 0, 0))],
        out_specs=[whole((nv, rows, cols)), whole((hidden + SUB, LANE))],
        out_shape=[
            jax.ShapeDtypeStruct((nv, rows, cols), F32),
            jax.ShapeDtypeStruct((hidden + SUB, LANE), F32),
        ],
        scratch_shapes=[
            pltpu.VMEM((nv + nc + 1, tall, wide), F32),
            pltpu.VMEM((nv, tall, wide), F32),
            pltpu.VMEM((nc, tall, wide), F32),
            pltpu.VMEM((nv, tall, wide), F32),
            pltpu.VMEM((nv, tall, wide), F32),
            pltpu.VMEM((rows, cols), F32),
            pltpu.VMEM((5, hidden, LANE), F32),
            pltpu.VMEM((hidden, hidden), F32),
            pltpu.VMEM((hidden, hidden), F32),
            pltpu.VMEM((16, hidden), F32),
        ],
        compiler_params=params(),
        name="sweeps_backward",
    )(*operands, mixing, *weights, acts)


def clip_kernel(parts, gin, gmid, gtop, gout, gbias):
    hidden = gmid.shape[0]
    total = parts[0]
    for k in range(1, parts.shape[0]):
        total = total + parts[k]
    squares = jnp.sum(jnp.sum(total * total, axis=0, keepdims=True), axis=1, keepdims=True)
    total = total * (CLIP_NORM / jnp.maximum(jnp.sqrt(squares), CLIP_NORM))
    gmid[...] = total[:hidden, :hidden]
    gtop[...] = total[:hidden, hidden:]
    low, high = total[hidden:, :hidden], total[hidden:, hidden:]
    gin[0:SUB] = low
    gin[SUB:] = high[: gin.shape[0] - SUB]
    gout[...] = high[2:3]
    gbias[...] = high[3:6]


def clip_all(parts, num_feat, hidden):
    shapes = [(num_feat, hidden), (hidden, hidden), (hidden, hidden), (1, hidden), (3, hidden)]
    return pl.pallas_call(
        clip_kernel,
        grid=(1,),
        in_specs=[whole(parts.shape)],
        out_specs=[whole(s) for s in shapes],
        out_shape=[jax.ShapeDtypeStruct(s, F32) for s in shapes],
        compiler_params=params(),
        name="clip",
    )(parts)


def sum_parts(packed):
    for axis in ("gy", "gx"):
        count = lax.axis_size(axis)
        step = 1
        while step < count:
            packed = packed + lax.ppermute(packed, axis, [(i, i ^ step) for i in range(count)])
            step *= 2
    return packed[None]


def shift_pair(low_edge, high_edge, axis):
    count = lax.axis_size(axis)
    up = [(i, i + 1) for i in range(count - 1)]
    down = [(b, a) for a, b in up]
    return lax.ppermute(high_edge, axis, up), lax.ppermute(low_edge, axis, down)


def shards(
    features, source, coupling, diagonal, production, bc_code, mixing,
    weight_in, weight_mid, weight_top, weight_out, biases,
):
    num_feat = features.shape[0]
    hidden = weight_mid.shape[0]
    wout = weight_out.reshape(1, hidden)
    top, bottom = row_slabs(source, coupling, diagonal, bc_code)
    north, south = shift_pair(top, bottom, "gx")
    first, last = col_slabs(source, coupling, diagonal, bc_code, north, south)
    west, east = shift_pair(first, last, "gy")
    acts, beta = forward(features, weight_in, weight_mid, weight_top, wout, biases)
    adjoint, packed = sweeps_and_backward(
        source, coupling, diagonal, bc_code, production, beta, (north, south, west, east), mixing,
        (weight_mid, weight_top, wout), acts,
    )
    grad_in, grad_mid, grad_top, grad_out, grad_bias = clip_all(sum_parts(packed), num_feat, hidden)
    return (adjoint, beta, grad_in, grad_mid, grad_top, grad_out.reshape(hidden), grad_bias)


def solution(mesh):
    cells3 = P(None, ("case", "gx"), "gy")
    cells2 = P(("case", "gx"), "gy")
    return jax.shard_map(
        shards,
        mesh=mesh,
        in_specs=(cells3,) * 3 + (cells2,) * 3 + (P(),) * 6,
        out_specs=(cells3, cells2, P("case"), P("case"), P("case"), P("case"), P("case")),
        check_vma=False,
    )
```

```python
import functools

import jax
import jax.numpy as jnp
from jax import lax
from jax.experimental import pallas as pl
from jax.experimental.pallas import tpu as pltpu
from jax.sharding import PartitionSpec as P

SWEEPS = 6
WALL_EXTRA = 0.2
FAR_EXTRA = 0.6
REG_WEIGHT = 0.5
CLIP_NORM = 64.0
EDGE = 8
SUB, LANE = 8, 128
F32, BF16 = jnp.float32, jnp.bfloat16
NT = (((1,), (1,)), ((), ()))
TN = (((0,), (0,)), ((), ()))
VMEM_BYTES = 16 * 1024 * 1024


def whole(shape):
    return pl.BlockSpec(shape, lambda *_: (0,) * len(shape))


def in_hbm(x):
    return pltpu.with_memory_space_constraint(x, pltpu.HBM)


def on_chip(kernel, operands, outs, scratch=(), far=(), far_outs=(), **kwargs):
    here, there = pl.BlockSpec(memory_space=pltpu.VMEM), pl.BlockSpec(memory_space=pltpu.HBM)
    return pl.pallas_call(
        kernel,
        in_specs=[here] * len(operands) + [there] * len(far),
        out_specs=[here] * len(outs) + [there] * len(far_outs),
        out_shape=[pltpu.VMEM(*o) for o in outs] + [pltpu.HBM(*o) for o in far_outs],
        scratch_shapes=list(scratch),
        compiler_params=params(),
        **kwargs,
    )(*operands, *[in_hbm(x) for x in far])


def like(x):
    return (x.shape, x.dtype)


def params():
    return pltpu.CompilerParams(vmem_limit_bytes=VMEM_BYTES)


def inverse_diag(diag, code):
    total = diag + jnp.where(code == 1, WALL_EXTRA, 0.0) + jnp.where(code == 2, FAR_EXTRA, 0.0)
    return 1.0 / total


def load_kernel(count, *refs):
    far, near = refs[:count], refs[count : 2 * count]
    inv, top, bottom, sems = refs[2 * count :]
    copies = [pltpu.make_async_copy(far[k], near[k], sems.at[k]) for k in range(count)]
    for copy in copies:
        copy.start()
    src, cpl, dia, bc = near[:4]
    for copy in copies[:4]:
        copy.wait()
    nv, rows, _ = src.shape
    nc = cpl.shape[0]
    inv[...] = inverse_diag(dia[...], bc[...])
    for v in range(nv):
        top[v] = src[v, 0:16].astype(F32)[:EDGE]
        bottom[v] = src[v, rows - 16 :].astype(F32)[16 - EDGE :]
    for d in range(nc):
        top[nv + d] = cpl[d, 0:16].astype(F32)[:EDGE]
        bottom[nv + d] = cpl[d, rows - 16 :].astype(F32)[16 - EDGE :]
    top[nv + nc] = inv[0:EDGE]
    bottom[nv + nc] = inv[rows - EDGE :]
    for copy in copies[4:]:
        copy.wait()


def load(arrays):
    source, coupling = arrays[:2]
    nv, rows, cols = source.shape
    slab = ((nv + coupling.shape[0] + 1, EDGE, cols), F32)
    return on_chip(
        functools.partial(load_kernel, len(arrays)),
        [],
        [like(x) for x in arrays] + [((rows, cols), F32), slab, slab],
        [pltpu.SemaphoreType.DMA((len(arrays),))],
        far=arrays,
        name="load",
    )


def cols_kernel(src, cpl, inv, north, south, west_ref, east_ref):
    nv, rows, cols = src.shape
    nc = cpl.shape[0]
    lane = lax.broadcasted_iota(jnp.int32, (rows, LANE), 1) // EDGE
    lane_h = lane[:EDGE]
    sides = ((west_ref, slice(0, LANE), 0), (east_ref, slice(cols - LANE, cols), EDGE))
    for out, window, extra in sides:
        mid = jnp.zeros((rows, LANE), F32)
        up = jnp.zeros((EDGE, LANE), F32)
        down = jnp.zeros((EDGE, LANE), F32)
        for f in range(nv + nc + 1):
            if f < nv:
                x = src[f, :, window].astype(F32)
            elif f < nv + nc:
                x = cpl[f - nv, :, window].astype(F32)
            else:
                x = inv[:, window]
            shift = (EDGE * f + extra) % LANE
            mid = jnp.where(lane == f, pltpu.roll(x, shift, 1), mid)
            up = jnp.where(lane_h == f, pltpu.roll(north[f, :, window], shift, 1), up)
            down = jnp.where(lane_h == f, pltpu.roll(south[f, :, window], shift, 1), down)
        out[0:EDGE] = up
        out[EDGE : EDGE + rows] = mid
        out[EDGE + rows :] = down


def col_slabs(source, coupling, inv, north, south):
    slab = ((source.shape[1] + 2 * EDGE, LANE), F32)
    return on_chip(cols_kernel, [source, coupling, inv, north, south], [slab, slab], name="col_slabs")


def column_of(row):
    hidden = row.shape[1]
    wide = jnp.concatenate([row, jnp.zeros((1, LANE - hidden), F32)], axis=1)
    return jnp.transpose(jnp.broadcast_to(wide, (LANE, LANE)))[:hidden]


def across(block, width):
    return jnp.concatenate([block] * (width // LANE), axis=1)


def weights_kernel(win, wmid, wtop, wout, bias, w1, w2, w3, cst):
    nf, hidden = win.shape
    step_rows, blk = hidden + 16, 16
    depth = w1.shape[1]
    feat_of = lax.broadcasted_iota(jnp.int32, (nf, depth), 1) // blk
    pick = (feat_of == lax.broadcasted_iota(jnp.int32, (nf, depth), 0)).astype(F32).astype(BF16)
    spread = lax.dot_general(win[...], pick, TN, preferred_element_type=F32)
    col = lax.broadcasted_iota(jnp.int32, (hidden, depth), 1)
    col_f = lax.broadcasted_iota(jnp.int32, (16, depth), 1)
    row_f = lax.broadcasted_iota(jnp.int32, (16, depth), 0)
    for r in range(blk):
        base = r * step_rows
        w1[base : base + hidden] = jnp.where(col % blk == r, spread, 0.0).astype(BF16)
        same = jnp.logical_and(col_f == row_f * blk + r, row_f < nf)
        w1[base + hidden : base + step_rows] = jnp.where(same, 1.0, 0.0).astype(BF16)
    w2[...] = jnp.transpose(wmid[...].astype(F32)).astype(BF16)
    w3[...] = jnp.transpose(wtop[...].astype(F32)).astype(BF16)
    for k in range(3):
        cst[k] = column_of(bias[k : k + 1, :])
    cst[3] = column_of(wout[...])


def prepare(weight_in, weight_mid, weight_top, weight_out, biases):
    nf, hidden = weight_in.shape
    depth = -(-nf * 16 // LANE) * LANE
    return on_chip(
        weights_kernel,
        [weight_in, weight_mid, weight_top, weight_out, biases],
        [
            ((16 * (hidden + 16), depth), BF16),
            ((hidden, hidden), BF16),
            ((hidden, hidden), BF16),
            ((4, hidden, LANE), F32),
        ],
        name="weights",
    )


def forward_kernel(first_row, feat, w1, w2, w3, cst, acts, beta, x1):
    nf, _, cols = feat.shape
    hidden = w2.shape[0]
    step_rows, blk, per = hidden + 16, 16, 4
    x1[...] = jnp.zeros(x1.shape, BF16)

    @pl.loop(0, acts.shape[0] // blk)
    def _(block):
        start = pl.multiple_of(block * blk, blk)
        x1[0 : nf * blk] = feat[:, pl.ds(first_row + start, blk), :].reshape(nf * blk, cols)
        b1, b2, b3, wo = (across(cst[k], cols) for k in range(4))
        lines = []
        for g in range(blk // per):
            lo = g * per * step_rows
            first = jnp.dot(w1[lo : lo + per * step_rows], x1[...], preferred_element_type=F32)
            ones = []
            for q in range(per):
                part = first[q * step_rows : (q + 1) * step_rows]
                one = jnp.tanh(part[:hidden] + b1).astype(BF16)
                acts[start + (g * per + q), 0:hidden] = one
                acts[start + (g * per + q), 3 * hidden :] = part[hidden:].astype(BF16)
                ones.append(one)
            second = jnp.dot(w2[...], jnp.concatenate(ones, axis=1), preferred_element_type=F32)
            twos = []
            for q in range(per):
                two = jnp.tanh(second[:, q * cols : (q + 1) * cols] + b2).astype(BF16)
                acts[start + (g * per + q), hidden : 2 * hidden] = two
                twos.append(two)
            third = jnp.dot(w3[...], jnp.concatenate(twos, axis=1), preferred_element_type=F32)
            for q in range(per):
                three = jnp.tanh(third[:, q * cols : (q + 1) * cols] + b3).astype(BF16)
                acts[start + (g * per + q), 2 * hidden : 3 * hidden] = three
                lines.append(1.0 + jnp.sum(three.astype(F32) * wo, axis=0, keepdims=True))
        beta[pl.ds(start, blk), :] = jnp.concatenate(lines, axis=0)


def forward(features, prepared, first_row, count):
    nf, _, cols = features.shape
    w1, w2 = prepared[:2]
    hidden = w2.shape[0]
    high = 3 * hidden + 16
    return on_chip(
        functools.partial(forward_kernel, first_row),
        [features, *prepared],
        [((count, high, cols), BF16), ((count, cols), F32)],
        [pltpu.VMEM((w1.shape[1], cols), BF16)],
        cost_estimate=pl.CostEstimate(
            flops=2 * count * cols * (nf + 2 * hidden) * hidden,
            bytes_accessed=2 * count * cols * (high + nf),
            transcendentals=3 * count * cols * hidden,
        ),
        name="network_forward",
    )


def tile_at(ref, lead, t, k):
    return ref[lead + (slice(t * SUB, (t + 1) * SUB), slice(k * LANE, (k + 1) * LANE))]


class Shifts:
    def __init__(self, tiles, lanes):
        self.tiles, self.lanes = tiles, lanes
        sub = lax.broadcasted_iota(jnp.int32, (SUB, LANE), 0)
        lane = lax.broadcasted_iota(jnp.int32, (SUB, LANE), 1)
        self.first_sub, self.last_sub = sub == 0, sub == SUB - 1
        self.first_lane, self.last_lane = lane == 0, lane == LANE - 1

    def above(self, ref, lead, t, k):
        here, other = tile_at(ref, lead, t, k), tile_at(ref, lead, max(t - 1, 0), k)
        return pltpu.roll(jnp.where(self.last_sub, other, here), 1, 0)

    def below(self, ref, lead, t, k):
        here, other = tile_at(ref, lead, t, k), tile_at(ref, lead, min(t + 1, self.tiles - 1), k)
        return pltpu.roll(jnp.where(self.first_sub, other, here), SUB - 1, 0)

    def left(self, ref, lead, t, k):
        here, other = tile_at(ref, lead, t, k), tile_at(ref, lead, t, (k - 1) % self.lanes)
        return pltpu.roll(jnp.where(self.last_lane, other, here), 1, 1)

    def right(self, ref, lead, t, k):
        here, other = tile_at(ref, lead, t, k), tile_at(ref, lead, t, (k + 1) % self.lanes)
        return pltpu.roll(jnp.where(self.first_lane, other, here), LANE - 1, 1)


def sweep_kernel(
    src, cpl, inverse, prod, beta_a, beta_b, north, south, west, east, mix,
    adj_out, sens, beta,
    raw, src_x, cpl_x, adj_a, adj_b,
):
    nv, rows, cols = src.shape
    nc = cpl.shape[0]
    tall = rows + 2 * EDGE
    tiles, lanes = tall // SUB, cols // LANE + 1
    shifts = Shifts(tiles, lanes)
    inner = slice(EDGE, EDGE + rows)
    lane = lax.broadcasted_iota(jnp.int32, (tall, LANE), 1)
    from_east, from_west = lane < EDGE, lane >= LANE - EDGE
    for f in range(nv + nc + 1):
        if f < nv:
            raw[f, inner, 0:cols] = src[f].astype(F32)
        elif f < nv + nc:
            raw[f, inner, 0:cols] = cpl[f - nv].astype(F32)
        else:
            raw[f, inner, 0:cols] = inverse[...]
        raw[f, 0:EDGE, 0:cols] = north[f]
        raw[f, EDGE + rows :, 0:cols] = south[f]
        e = pltpu.roll(east[...], (LANE - EDGE * f) % LANE, 1)
        w = pltpu.roll(west[...], (LANE - EDGE - EDGE * f) % LANE, 1)
        raw[f, :, cols:] = jnp.where(from_east, e, jnp.where(from_west, w, 0.0))

    moves = (shifts.above, shifts.below, shifts.left, shifts.right)
    for t in range(tiles):
        for k in range(lanes):
            at = (slice(t * SUB, (t + 1) * SUB), slice(k * LANE, (k + 1) * LANE))
            inv = tile_at(raw, (nv + nc,), t, k)
            for v in range(nv):
                src_x[(v,) + at] = inv * tile_at(raw, (v,), t, k)
            for d in range(nc):
                cpl_x[(d,) + at] = inv * moves[d](raw, (nv + d,), t, k)

    def sweep(old, new, last):
        for t in range(1, tiles - 1) if last else range(tiles):
            for k in range(lanes - 1) if last else range(lanes):
                at = (slice(t * SUB, (t + 1) * SUB), slice(k * LANE, (k + 1) * LANE))
                couple = [cpl_x[(d,) + at] for d in range(nc)]
                total = [src_x[(a,) + at] for a in range(nv)]
                for b in range(nv):
                    inc = couple[0] * moves[0](old, (b,), t, k)
                    for d in range(1, nc):
                        inc = inc + couple[d] * moves[d](old, (b,), t, k)
                    total = [total[a] + mix[b, a] * inc for a in range(nv)]
                if last:
                    at = (slice((t - 1) * SUB, t * SUB), at[1])
                for a in range(nv):
                    new[(a,) + at] = total[a]

    sweep(src_x, adj_a, False)

    @pl.loop(0, (SWEEPS - 2) // 2)
    def _(i):
        sweep(adj_a, adj_b, False)
        sweep(adj_b, adj_a, False)

    sweep(adj_a, adj_out, True)
    half = beta_a.shape[0]
    beta[0:half] = beta_a[...]
    beta[half:] = beta_b[...]
    sens[...] = adj_out[nv - 1] * prod[...] + REG_WEIGHT * (beta[...] - 1.0)


def sweeps(source, coupling, inverse, production, betas, halos, mixing):
    nv, rows, cols = source.shape
    nc = coupling.shape[0]
    tall, wide = rows + 2 * EDGE, cols + LANE
    near = pl.BlockSpec(memory_space=pltpu.VMEM)
    operands = [source, coupling, inverse, production, *betas, *halos]
    flat = ((rows, cols), F32)
    return pl.pallas_call(
        sweep_kernel,
        in_specs=[near] * len(operands) + [pl.BlockSpec(memory_space=pltpu.SMEM)],
        out_specs=[near] * 3,
        out_shape=[pltpu.VMEM((nv, rows, cols), F32), pltpu.VMEM(*flat), pltpu.VMEM(*flat)],
        scratch_shapes=[
            pltpu.VMEM((nv + nc + 1, tall, wide), F32),
            pltpu.VMEM((nv, tall, wide), F32),
            pltpu.VMEM((nc, tall, wide), F32),
            pltpu.VMEM((nv, tall, wide), F32),
            pltpu.VMEM((nv, tall, wide), F32),
        ],
        compiler_params=params(),
        name="sweeps",
    )(*operands, mixing)


def backward_kernel(
    adj, beta, sens, wmid, wtop, cst, acts_a, acts_b,
    packed, adj_out, beta_out,
    sums, g_mid, g_top, g_in, sems,
):
    out_copies = [
        pltpu.make_async_copy(adj, adj_out, sems.at[0]),
        pltpu.make_async_copy(beta, beta_out, sems.at[1]),
    ]
    for copy in out_copies:
        copy.start()
    blk, cols = 8, sens.shape[1]
    hidden = wmid.shape[0]
    sums[...] = jnp.zeros(sums.shape, F32)
    g_mid[...] = jnp.zeros(g_mid.shape, F32)
    g_top[...] = jnp.zeros(g_top.shape, F32)
    g_in[...] = jnp.zeros(g_in.shape, F32)

    def fold(x):
        parts = [x[:, k * LANE : (k + 1) * LANE] for k in range(cols // LANE)]
        return functools.reduce(jnp.add, parts)

    def outer(xs, ds):
        return lax.dot_general(
            jnp.concatenate(xs, axis=1), jnp.concatenate(ds, axis=1), NT, preferred_element_type=F32
        )

    def block(acts, start, first_row):
        rows_sens = sens[pl.ds(pl.multiple_of(first_row + start, blk), blk), :]
        wo = across(cst[3], cols)
        ones, twos, feats, d1s, d2s, d3s = [], [], [], [], [], []
        acc = [jnp.zeros((hidden, LANE), F32) for _ in range(4)]
        for q in range(blk):
            one, two = acts[start + q, 0:hidden], acts[start + q, hidden : 2 * hidden]
            three_f = acts[start + q, 2 * hidden : 3 * hidden].astype(F32)
            sen = jnp.broadcast_to(rows_sens[q : q + 1], (hidden, cols))
            acc[0] = acc[0] + fold(three_f * sen)
            d3 = sen * wo * (1.0 - three_f * three_f)
            acc[3] = acc[3] + fold(d3)
            d3 = d3.astype(BF16)
            two_f = two.astype(F32)
            d2 = jnp.dot(wtop[...], d3, preferred_element_type=F32) * (1.0 - two_f * two_f)
            acc[2] = acc[2] + fold(d2)
            d2 = d2.astype(BF16)
            one_f = one.astype(F32)
            d1 = jnp.dot(wmid[...], d2, preferred_element_type=F32) * (1.0 - one_f * one_f)
            acc[1] = acc[1] + fold(d1)
            d1 = d1.astype(BF16)
            ones.append(one)
            twos.append(two)
            feats.append(acts[start + q, 3 * hidden :])
            d1s.append(d1)
            d2s.append(d2)
            d3s.append(d3)
        g_mid[...] += outer(ones, d2s)
        g_top[...] += outer(twos, d3s)
        g_in[...] += outer(feats, d1s)
        for k in range(4):
            sums[k] += acc[k]

    half = acts_a.shape[0]
    for acts, first_row in ((acts_a, 0), (acts_b, half)):

        @pl.loop(0, acts.shape[0] // blk)
        def _(i, acts=acts, first_row=first_row):
            block(acts, pl.multiple_of(i * blk, blk), first_row)

    packed[0:hidden, :] = jnp.concatenate([g_mid[...], g_top[...]], axis=1)
    tail = g_in[SUB : 2 * SUB]
    row = lax.broadcasted_iota(jnp.int32, (SUB, hidden), 0)
    for k in range(4):
        line = jnp.sum(jnp.transpose(sums[k]), axis=0, keepdims=True)
        tail = tail + jnp.where(row == k + 2, jnp.broadcast_to(line, (SUB, hidden)), 0.0)
    packed[hidden : hidden + SUB, :] = jnp.concatenate([g_in[0:SUB], tail], axis=1)
    for copy in out_copies:
        copy.wait()


def backward(adj, beta, sens, weight_mid, weight_top, cst, acts):
    hidden = weight_mid.shape[0]
    return on_chip(
        backward_kernel,
        [adj, beta, sens, weight_mid, weight_top, cst, *acts],
        [((hidden + SUB, LANE), F32)],
        [
            pltpu.VMEM((4, hidden, LANE), F32),
            pltpu.VMEM((hidden, hidden), F32),
            pltpu.VMEM((hidden, hidden), F32),
            pltpu.VMEM((16, hidden), F32),
            pltpu.SemaphoreType.DMA((2,)),
        ],
        far_outs=[like(adj), like(beta)],
        name="backward",
    )


def clip_kernel(parts, gin, gmid, gtop, gout, gbias):
    hidden = gmid.shape[0]
    total = parts[0]
    for k in range(1, parts.shape[0]):
        total = total + parts[k]
    squares = jnp.sum(jnp.sum(total * total, axis=0, keepdims=True), axis=1, keepdims=True)
    total = total * (CLIP_NORM / jnp.maximum(jnp.sqrt(squares), CLIP_NORM))
    gmid[...] = total[:hidden, :hidden]
    gtop[...] = total[:hidden, hidden:]
    low, high = total[hidden:, :hidden], total[hidden:, hidden:]
    gin[0:SUB] = low
    gin[SUB:] = high[: gin.shape[0] - SUB]
    gout[...] = high[2:3]
    gbias[...] = high[3:6]


def clip_all(parts, num_feat, hidden):
    shapes = [(num_feat, hidden), (hidden, hidden), (hidden, hidden), (1, hidden), (3, hidden)]
    return pl.pallas_call(
        clip_kernel,
        grid=(1,),
        in_specs=[whole(parts.shape)],
        out_specs=[whole(s) for s in shapes],
        out_shape=[jax.ShapeDtypeStruct(s, F32) for s in shapes],
        compiler_params=params(),
        name="clip",
    )(parts)


def sum_parts(packed):
    return lax.all_gather(packed, ("gx", "gy"))


def shift_pair(low_edge, high_edge, axis):
    count = lax.axis_size(axis)
    up = [(i, i + 1) for i in range(count - 1)]
    down = [(b, a) for a, b in up]
    return lax.ppermute(high_edge, axis, up), lax.ppermute(low_edge, axis, down)


def shards(
    features, source, coupling, diagonal, production, bc_code, mixing,
    weight_in, weight_mid, weight_top, weight_out, biases,
):
    num_feat, rows, _ = features.shape
    hidden = weight_mid.shape[0]
    loaded = load([
        source, coupling, diagonal, bc_code, production, features,
        weight_in, weight_mid, weight_top, weight_out.reshape(1, hidden), biases,
    ])
    source, coupling, _, _, production, features, weight_in, weight_mid, weight_top, wout, biases = loaded[:11]
    inverse, top, bottom = loaded[11:]
    north, south = shift_pair(top, bottom, "gx")
    prepared = prepare(weight_in, weight_mid, weight_top, wout, biases)
    half = rows // 32 * 16
    acts_a, beta_a = forward(features, prepared, 0, half)
    north, south, beta_a = lax.optimization_barrier((north, south, beta_a))
    first, last = col_slabs(source, coupling, inverse, north, south)
    west, east = shift_pair(first, last, "gy")
    acts_b, beta_b = forward(features, prepared, half, rows - half)
    adj, sens, beta = sweeps(
        source, coupling, inverse, production, (beta_a, beta_b), (north, south, west, east), mixing
    )
    packed, adjoint, beta = backward(adj, beta, sens, weight_mid, weight_top, prepared[3], (acts_a, acts_b))
    grad_in, grad_mid, grad_top, grad_out, grad_bias = clip_all(sum_parts(packed), num_feat, hidden)
    return (adjoint, beta, grad_in, grad_mid, grad_top, grad_out.reshape(hidden), grad_bias)


def solution(mesh):
    cells3 = P(None, ("case", "gx"), "gy")
    cells2 = P(("case", "gx"), "gy")
    return jax.shard_map(
        shards,
        mesh=mesh,
        in_specs=(cells3,) * 3 + (cells2,) * 3 + (P(),) * 6,
        out_specs=(cells3, cells2, P("case"), P("case"), P("case"), P("case"), P("case")),
        check_vma=False,
    )
```

```python
import functools

import jax
import jax.numpy as jnp
from jax import lax
from jax.experimental import pallas as pl
from jax.experimental.pallas import tpu as pltpu
from jax.sharding import PartitionSpec as P

SWEEPS = 6
WALL_EXTRA = 0.2
FAR_EXTRA = 0.6
REG_WEIGHT = 0.5
CLIP_NORM = 64.0
EDGE = 8
SUB, LANE = 8, 128
F32, BF16 = jnp.float32, jnp.bfloat16
NT = (((1,), (1,)), ((), ()))
TN = (((0,), (0,)), ((), ()))
VMEM_BYTES = 16 * 1024 * 1024


def whole(shape):
    return pl.BlockSpec(shape, lambda *_: (0,) * len(shape))


def in_hbm(x):
    return pltpu.with_memory_space_constraint(x, pltpu.HBM)


def on_chip(kernel, operands, outs, scratch=(), far=(), far_outs=(), **kwargs):
    here, there = pl.BlockSpec(memory_space=pltpu.VMEM), pl.BlockSpec(memory_space=pltpu.HBM)
    return pl.pallas_call(
        kernel,
        in_specs=[here] * len(operands) + [there] * len(far),
        out_specs=[here] * len(outs) + [there] * len(far_outs),
        out_shape=[pltpu.VMEM(*o) for o in outs] + [pltpu.HBM(*o) for o in far_outs],
        scratch_shapes=list(scratch),
        compiler_params=params(),
        **kwargs,
    )(*operands, *[in_hbm(x) for x in far])


def like(x):
    return (x.shape, x.dtype)


def params():
    return pltpu.CompilerParams(vmem_limit_bytes=VMEM_BYTES)


def inverse_diag(diag, code):
    total = diag + jnp.where(code == 1, WALL_EXTRA, 0.0) + jnp.where(code == 2, FAR_EXTRA, 0.0)
    return 1.0 / total


def is_odd(axis):
    return lax.axis_index(axis) % 2 == 1


def load_kernel(count, *refs):
    far, near = refs[:count], refs[count : 2 * count]
    inv, first, second, sems = refs[2 * count :]
    copies = [pltpu.make_async_copy(far[k], near[k], sems.at[k]) for k in range(count)]
    for copy in copies:
        copy.start()
    src, cpl, dia, bc = near[:4]
    for copy in copies[:4]:
        copy.wait()
    nv, rows, _ = src.shape
    nc = cpl.shape[0]
    inv[...] = inverse_diag(dia[...], bc[...])
    odd = is_odd("gx")
    for f in range(nv + nc + 1):
        if f < nv + nc:
            ref, k = (src, f) if f < nv else (cpl, f - nv)
            top, bottom = ref[k, 0:16].astype(F32)[:EDGE], ref[k, rows - 16 :].astype(F32)[16 - EDGE :]
        else:
            top, bottom = inv[0:EDGE], inv[rows - EDGE :]
        first[f] = jnp.where(odd, top, bottom)
        second[f] = jnp.where(odd, bottom, top)
    for copy in copies[4:]:
        copy.wait()


def load(arrays):
    source, coupling = arrays[:2]
    nv, rows, cols = source.shape
    slab = ((nv + coupling.shape[0] + 1, EDGE, cols), F32)
    return on_chip(
        functools.partial(load_kernel, len(arrays)),
        [],
        [like(x) for x in arrays] + [((rows, cols), F32), slab, slab],
        [pltpu.SemaphoreType.DMA((len(arrays),))],
        far=arrays,
        name="load",
    )


def ordered(axis, first, second):
    odd = is_odd(axis)
    return jnp.where(odd, first, second), jnp.where(odd, second, first)


def cols_kernel(src, cpl, inv, row_first, row_second, col_first, col_second):
    nv, rows, cols = src.shape
    nc = cpl.shape[0]
    lane = lax.broadcasted_iota(jnp.int32, (rows, LANE), 1) // EDGE
    lane_h = lane[:EDGE]
    slabs = []
    for window, extra in ((slice(0, LANE), 0), (slice(cols - LANE, cols), EDGE)):
        mid = jnp.zeros((rows, LANE), F32)
        up = jnp.zeros((EDGE, LANE), F32)
        down = jnp.zeros((EDGE, LANE), F32)
        for f in range(nv + nc + 1):
            if f < nv:
                x = src[f, :, window].astype(F32)
            elif f < nv + nc:
                x = cpl[f - nv, :, window].astype(F32)
            else:
                x = inv[:, window]
            shift = (EDGE * f + extra) % LANE
            mid = jnp.where(lane == f, pltpu.roll(x, shift, 1), mid)
            north, south = ordered("gx", row_first[f, :, window], row_second[f, :, window])
            up = jnp.where(lane_h == f, pltpu.roll(north, shift, 1), up)
            down = jnp.where(lane_h == f, pltpu.roll(south, shift, 1), down)
        slabs.append(jnp.concatenate([up, mid, down], axis=0))
    odd = is_odd("gy")
    col_first[...] = jnp.where(odd, slabs[0], slabs[1])
    col_second[...] = jnp.where(odd, slabs[1], slabs[0])


def col_slabs(source, coupling, inv, row_halos):
    slab = ((source.shape[1] + 2 * EDGE, LANE), F32)
    return on_chip(cols_kernel, [source, coupling, inv, *row_halos], [slab, slab], name="col_slabs")


def column_of(row):
    hidden = row.shape[1]
    wide = jnp.concatenate([row, jnp.zeros((1, LANE - hidden), F32)], axis=1)
    return jnp.transpose(jnp.broadcast_to(wide, (LANE, LANE)))[:hidden]


def across(block, width):
    return jnp.concatenate([block] * (width // LANE), axis=1)


def weights_kernel(win, wmid, wtop, wout, bias, w1, w2, w3, cst):
    nf, hidden = win.shape
    step_rows, blk = hidden + 16, 16
    depth = w1.shape[1]
    feat_of = lax.broadcasted_iota(jnp.int32, (nf, depth), 1) // blk
    pick = (feat_of == lax.broadcasted_iota(jnp.int32, (nf, depth), 0)).astype(F32).astype(BF16)
    spread = lax.dot_general(win[...], pick, TN, preferred_element_type=F32)
    col = lax.broadcasted_iota(jnp.int32, (hidden, depth), 1)
    col_f = lax.broadcasted_iota(jnp.int32, (16, depth), 1)
    row_f = lax.broadcasted_iota(jnp.int32, (16, depth), 0)
    for r in range(blk):
        base = r * step_rows
        w1[base : base + hidden] = jnp.where(col % blk == r, spread, 0.0).astype(BF16)
        same = jnp.logical_and(col_f == row_f * blk + r, row_f < nf)
        w1[base + hidden : base + step_rows] = jnp.where(same, 1.0, 0.0).astype(BF16)
    w2[...] = jnp.transpose(wmid[...].astype(F32)).astype(BF16)
    w3[...] = jnp.transpose(wtop[...].astype(F32)).astype(BF16)
    for k in range(3):
        cst[k] = column_of(bias[k : k + 1, :])
    cst[3] = column_of(wout[...])


def prepare(weight_in, weight_mid, weight_top, weight_out, biases):
    nf, hidden = weight_in.shape
    depth = -(-nf * 16 // LANE) * LANE
    return on_chip(
        weights_kernel,
        [weight_in, weight_mid, weight_top, weight_out, biases],
        [
            ((16 * (hidden + 16), depth), BF16),
            ((hidden, hidden), BF16),
            ((hidden, hidden), BF16),
            ((4, hidden, LANE), F32),
        ],
        name="weights",
    )


def forward_kernel(first_row, feat, w1, w2, w3, cst, acts, beta, x1):
    nf, _, cols = feat.shape
    hidden = w2.shape[0]
    step_rows, blk, per = hidden + 16, 16, 4
    x1[...] = jnp.zeros(x1.shape, BF16)

    @pl.loop(0, acts.shape[0] // blk)
    def _(block):
        start = pl.multiple_of(block * blk, blk)
        x1[0 : nf * blk] = feat[:, pl.ds(first_row + start, blk), :].reshape(nf * blk, cols)
        b1, b2, b3, wo = (across(cst[k], cols) for k in range(4))
        lines = []
        for g in range(blk // per):
            lo = g * per * step_rows
            first = jnp.dot(w1[lo : lo + per * step_rows], x1[...], preferred_element_type=F32)
            ones = []
            for q in range(per):
                part = first[q * step_rows : (q + 1) * step_rows]
                one = jnp.tanh(part[:hidden] + b1).astype(BF16)
                acts[start + (g * per + q), 0:hidden] = one
                acts[start + (g * per + q), 3 * hidden :] = part[hidden:].astype(BF16)
                ones.append(one)
            second = jnp.dot(w2[...], jnp.concatenate(ones, axis=1), preferred_element_type=F32)
            twos = []
            for q in range(per):
                two = jnp.tanh(second[:, q * cols : (q + 1) * cols] + b2).astype(BF16)
                acts[start + (g * per + q), hidden : 2 * hidden] = two
                twos.append(two)
            third = jnp.dot(w3[...], jnp.concatenate(twos, axis=1), preferred_element_type=F32)
            for q in range(per):
                three = jnp.tanh(third[:, q * cols : (q + 1) * cols] + b3).astype(BF16)
                acts[start + (g * per + q), 2 * hidden : 3 * hidden] = three
                lines.append(1.0 + jnp.sum(three.astype(F32) * wo, axis=0, keepdims=True))
        beta[pl.ds(start, blk), :] = jnp.concatenate(lines, axis=0)


def forward(features, prepared, first_row, count):
    nf, _, cols = features.shape
    w1, w2 = prepared[:2]
    hidden = w2.shape[0]
    high = 3 * hidden + 16
    return on_chip(
        functools.partial(forward_kernel, first_row),
        [features, *prepared],
        [((count, high, cols), BF16), ((count, cols), F32)],
        [pltpu.VMEM((w1.shape[1], cols), BF16)],
        cost_estimate=pl.CostEstimate(
            flops=2 * count * cols * (nf + 2 * hidden) * hidden,
            bytes_accessed=2 * count * cols * (high + nf),
            transcendentals=3 * count * cols * hidden,
        ),
        name="network_forward",
    )


def tile_at(ref, lead, t, k):
    return ref[lead + (slice(t * SUB, (t + 1) * SUB), slice(k * LANE, (k + 1) * LANE))]


class Shifts:
    def __init__(self, tiles, lanes):
        self.tiles, self.lanes = tiles, lanes
        sub = lax.broadcasted_iota(jnp.int32, (SUB, LANE), 0)
        lane = lax.broadcasted_iota(jnp.int32, (SUB, LANE), 1)
        self.first_sub, self.last_sub = sub == 0, sub == SUB - 1
        self.first_lane, self.last_lane = lane == 0, lane == LANE - 1

    def above(self, ref, lead, t, k):
        here, other = tile_at(ref, lead, t, k), tile_at(ref, lead, max(t - 1, 0), k)
        return pltpu.roll(jnp.where(self.last_sub, other, here), 1, 0)

    def below(self, ref, lead, t, k):
        here, other = tile_at(ref, lead, t, k), tile_at(ref, lead, min(t + 1, self.tiles - 1), k)
        return pltpu.roll(jnp.where(self.first_sub, other, here), SUB - 1, 0)

    def left(self, ref, lead, t, k):
        here, other = tile_at(ref, lead, t, k), tile_at(ref, lead, t, (k - 1) % self.lanes)
        return pltpu.roll(jnp.where(self.last_lane, other, here), 1, 1)

    def right(self, ref, lead, t, k):
        here, other = tile_at(ref, lead, t, k), tile_at(ref, lead, t, (k + 1) % self.lanes)
        return pltpu.roll(jnp.where(self.first_lane, other, here), LANE - 1, 1)


def sweep_kernel(
    src, cpl, inverse, prod, beta_a, beta_b, row_first, row_second, col_first, col_second, mix,
    adj_out, sens, beta,
    raw, src_x, cpl_x, adj_a, adj_b,
):
    nv, rows, cols = src.shape
    nc = cpl.shape[0]
    tall = rows + 2 * EDGE
    tiles, lanes = tall // SUB, cols // LANE + 1
    shifts = Shifts(tiles, lanes)
    inner = slice(EDGE, EDGE + rows)
    lane = lax.broadcasted_iota(jnp.int32, (tall, LANE), 1)
    from_east, from_west = lane < EDGE, lane >= LANE - EDGE
    west, east = ordered("gy", col_first[...], col_second[...])
    for f in range(nv + nc + 1):
        if f < nv:
            raw[f, inner, 0:cols] = src[f].astype(F32)
        elif f < nv + nc:
            raw[f, inner, 0:cols] = cpl[f - nv].astype(F32)
        else:
            raw[f, inner, 0:cols] = inverse[...]
        north, south = ordered("gx", row_first[f], row_second[f])
        raw[f, 0:EDGE, 0:cols] = north
        raw[f, EDGE + rows :, 0:cols] = south
        e = pltpu.roll(east, (LANE - EDGE * f) % LANE, 1)
        w = pltpu.roll(west, (LANE - EDGE - EDGE * f) % LANE, 1)
        raw[f, :, cols:] = jnp.where(from_east, e, jnp.where(from_west, w, 0.0))

    moves = (shifts.above, shifts.below, shifts.left, shifts.right)
    for t in range(tiles):
        for k in range(lanes):
            at = (slice(t * SUB, (t + 1) * SUB), slice(k * LANE, (k + 1) * LANE))
            inv = tile_at(raw, (nv + nc,), t, k)
            for v in range(nv):
                src_x[(v,) + at] = inv * tile_at(raw, (v,), t, k)
            for d in range(nc):
                cpl_x[(d,) + at] = inv * moves[d](raw, (nv + d,), t, k)

    def sweep(old, new, last):
        for t in range(1, tiles - 1) if last else range(tiles):
            for k in range(lanes - 1) if last else range(lanes):
                at = (slice(t * SUB, (t + 1) * SUB), slice(k * LANE, (k + 1) * LANE))
                couple = [cpl_x[(d,) + at] for d in range(nc)]
                total = [src_x[(a,) + at] for a in range(nv)]
                for b in range(nv):
                    inc = couple[0] * moves[0](old, (b,), t, k)
                    for d in range(1, nc):
                        inc = inc + couple[d] * moves[d](old, (b,), t, k)
                    total = [total[a] + mix[b, a] * inc for a in range(nv)]
                if last:
                    at = (slice((t - 1) * SUB, t * SUB), at[1])
                for a in range(nv):
                    new[(a,) + at] = total[a]

    sweep(src_x, adj_a, False)

    @pl.loop(0, (SWEEPS - 2) // 2)
    def _(i):
        sweep(adj_a, adj_b, False)
        sweep(adj_b, adj_a, False)

    sweep(adj_a, adj_out, True)
    half = beta_a.shape[0]
    beta[0:half] = beta_a[...]
    beta[half:] = beta_b[...]
    sens[...] = adj_out[nv - 1] * prod[...] + REG_WEIGHT * (beta[...] - 1.0)


def sweeps(source, coupling, inverse, production, betas, halos, mixing):
    nv, rows, cols = source.shape
    nc = coupling.shape[0]
    tall, wide = rows + 2 * EDGE, cols + LANE
    near = pl.BlockSpec(memory_space=pltpu.VMEM)
    operands = [source, coupling, inverse, production, *betas, *halos]
    flat = ((rows, cols), F32)
    return pl.pallas_call(
        sweep_kernel,
        in_specs=[near] * len(operands) + [pl.BlockSpec(memory_space=pltpu.SMEM)],
        out_specs=[near] * 3,
        out_shape=[pltpu.VMEM((nv, rows, cols), F32), pltpu.VMEM(*flat), pltpu.VMEM(*flat)],
        scratch_shapes=[
            pltpu.VMEM((nv + nc + 1, tall, wide), F32),
            pltpu.VMEM((nv, tall, wide), F32),
            pltpu.VMEM((nc, tall, wide), F32),
            pltpu.VMEM((nv, tall, wide), F32),
            pltpu.VMEM((nv, tall, wide), F32),
        ],
        compiler_params=params(),
        name="sweeps",
    )(*operands, mixing)


def backward_kernel(
    adj, beta, sens, wmid, wtop, cst, acts_a, acts_b,
    packed, adj_out, beta_out,
    sums, g_mid, g_top, g_in, sems,
):
    out_copies = [
        pltpu.make_async_copy(adj, adj_out, sems.at[0]),
        pltpu.make_async_copy(beta, beta_out, sems.at[1]),
    ]
    for copy in out_copies:
        copy.start()
    blk, cols = 8, sens.shape[1]
    hidden = wmid.shape[0]
    sums[...] = jnp.zeros(sums.shape, F32)
    g_mid[...] = jnp.zeros(g_mid.shape, F32)
    g_top[...] = jnp.zeros(g_top.shape, F32)
    g_in[...] = jnp.zeros(g_in.shape, F32)

    def fold(x):
        parts = [x[:, k * LANE : (k + 1) * LANE] for k in range(cols // LANE)]
        return functools.reduce(jnp.add, parts)

    def outer(xs, ds):
        return lax.dot_general(
            jnp.concatenate(xs, axis=1), jnp.concatenate(ds, axis=1), NT, preferred_element_type=F32
        )

    def block(acts, start, first_row):
        rows_sens = sens[pl.ds(pl.multiple_of(first_row + start, blk), blk), :]
        wo = across(cst[3], cols)
        ones, twos, feats, d1s, d2s, d3s = [], [], [], [], [], []
        acc = [jnp.zeros((hidden, LANE), F32) for _ in range(4)]
        for q in range(blk):
            one, two = acts[start + q, 0:hidden], acts[start + q, hidden : 2 * hidden]
            three_f = acts[start + q, 2 * hidden : 3 * hidden].astype(F32)
            sen = jnp.broadcast_to(rows_sens[q : q + 1], (hidden, cols))
            acc[0] = acc[0] + fold(three_f * sen)
            d3 = sen * wo * (1.0 - three_f * three_f)
            acc[3] = acc[3] + fold(d3)
            d3 = d3.astype(BF16)
            two_f = two.astype(F32)
            d2 = jnp.dot(wtop[...], d3, preferred_element_type=F32) * (1.0 - two_f * two_f)
            acc[2] = acc[2] + fold(d2)
            d2 = d2.astype(BF16)
            one_f = one.astype(F32)
            d1 = jnp.dot(wmid[...], d2, preferred_element_type=F32) * (1.0 - one_f * one_f)
            acc[1] = acc[1] + fold(d1)
            d1 = d1.astype(BF16)
            ones.append(one)
            twos.append(two)
            feats.append(acts[start + q, 3 * hidden :])
            d1s.append(d1)
            d2s.append(d2)
            d3s.append(d3)
        g_mid[...] += outer(ones, d2s)
        g_top[...] += outer(twos, d3s)
        g_in[...] += outer(feats, d1s)
        for k in range(4):
            sums[k] += acc[k]

    half = acts_a.shape[0]
    for acts, first_row in ((acts_a, 0), (acts_b, half)):

        @pl.loop(0, acts.shape[0] // blk)
        def _(i, acts=acts, first_row=first_row):
            block(acts, pl.multiple_of(i * blk, blk), first_row)

    packed[0:hidden, :] = jnp.concatenate([g_mid[...], g_top[...]], axis=1)
    tail = g_in[SUB : 2 * SUB]
    row = lax.broadcasted_iota(jnp.int32, (SUB, hidden), 0)
    for k in range(4):
        line = jnp.sum(jnp.transpose(sums[k]), axis=0, keepdims=True)
        tail = tail + jnp.where(row == k + 2, jnp.broadcast_to(line, (SUB, hidden)), 0.0)
    packed[hidden : hidden + SUB, :] = jnp.concatenate([g_in[0:SUB], tail], axis=1)
    for copy in out_copies:
        copy.wait()


def backward(adj, beta, sens, weight_mid, weight_top, cst, acts):
    hidden = weight_mid.shape[0]
    return on_chip(
        backward_kernel,
        [adj, beta, sens, weight_mid, weight_top, cst, *acts],
        [((hidden + SUB, LANE), F32)],
        [
            pltpu.VMEM((4, hidden, LANE), F32),
            pltpu.VMEM((hidden, hidden), F32),
            pltpu.VMEM((hidden, hidden), F32),
            pltpu.VMEM((16, hidden), F32),
            pltpu.SemaphoreType.DMA((2,)),
        ],
        far_outs=[like(adj), like(beta)],
        name="backward",
    )


def clip_kernel(summed, gin, gmid, gtop, gout, gbias):
    hidden = gmid.shape[0]
    total = summed[0 : hidden + SUB]
    squares = jnp.sum(jnp.sum(total * total, axis=0, keepdims=True), axis=1, keepdims=True)
    total = total * (CLIP_NORM / jnp.maximum(jnp.sqrt(squares), CLIP_NORM))
    gmid[...] = total[:hidden, :hidden]
    gtop[...] = total[:hidden, hidden:]
    low, high = total[hidden:, :hidden], total[hidden:, hidden:]
    gin[0:SUB] = low
    gin[SUB:] = high[: gin.shape[0] - SUB]
    gout[...] = high[2:3]
    gbias[...] = high[3:6]


def clip_all(summed, num_feat, hidden):
    shapes = [(num_feat, hidden), (hidden, hidden), (hidden, hidden), (1, hidden), (3, hidden)]
    return pl.pallas_call(
        clip_kernel,
        grid=(1,),
        in_specs=[whole(summed.shape)],
        out_specs=[whole(s) for s in shapes],
        out_shape=[jax.ShapeDtypeStruct(s, F32) for s in shapes],
        compiler_params=params(),
        name="clip",
    )(summed)


def sum_over_case(packed):
    axes = ("gx", "gy")
    count = lax.axis_size(axes)
    piece = -(-packed.shape[0] // (count * SUB)) * SUB
    padded = jnp.pad(packed, ((0, count * piece - packed.shape[0]), (0, 0))).reshape(count, piece, LANE)
    mine = jnp.sum(lax.all_to_all(padded, axes, 0, 0), axis=0, keepdims=True)
    pieces = lax.all_to_all(jnp.broadcast_to(mine, padded.shape), axes, 0, 0)
    return pieces.reshape(count * piece, LANE)


def swaps(first, second, axis):
    count = lax.axis_size(axis)

    def pairs(start):
        low = range(start, count - 1, 2)
        return [(i, i + 1) for i in low] + [(i + 1, i) for i in low]

    return lax.ppermute(first, axis, pairs(0)), lax.ppermute(second, axis, pairs(1))


def shards(
    features, source, coupling, diagonal, production, bc_code, mixing,
    weight_in, weight_mid, weight_top, weight_out, biases,
):
    num_feat, rows, _ = features.shape
    hidden = weight_mid.shape[0]
    loaded = load([
        source, coupling, diagonal, bc_code, production, features,
        weight_in, weight_mid, weight_top, weight_out.reshape(1, hidden), biases,
    ])
    source, coupling, _, _, production, features, weight_in, weight_mid, weight_top, wout, biases = loaded[:11]
    inverse, *row_slabs = loaded[11:]
    row_halos = swaps(*row_slabs, "gx")
    prepared = prepare(weight_in, weight_mid, weight_top, wout, biases)
    half = rows // 32 * 16
    acts_a, beta_a = forward(features, prepared, 0, half)
    *row_halos, beta_a = lax.optimization_barrier((*row_halos, beta_a))
    col_halos = swaps(*col_slabs(source, coupling, inverse, row_halos), "gy")
    acts_b, beta_b = forward(features, prepared, half, rows - half)
    adj, sens, beta = sweeps(
        source, coupling, inverse, production, (beta_a, beta_b), (*row_halos, *col_halos), mixing
    )
    packed, adjoint, beta = backward(adj, beta, sens, weight_mid, weight_top, prepared[3], (acts_a, acts_b))
    grad_in, grad_mid, grad_top, grad_out, grad_bias = clip_all(sum_over_case(packed), num_feat, hidden)
    return (adjoint, beta, grad_in, grad_mid, grad_top, grad_out.reshape(hidden), grad_bias)


def solution(mesh):
    cells3 = P(None, ("case", "gx"), "gy")
    cells2 = P(("case", "gx"), "gy")
    return jax.shard_map(
        shards,
        mesh=mesh,
        in_specs=(cells3,) * 3 + (cells2,) * 3 + (P(),) * 6,
        out_specs=(cells3, cells2, P("case"), P("case"), P("case"), P("case"), P("case")),
        check_vma=False,
    )
```

```python
import functools

import jax
import jax.numpy as jnp
from jax import lax
from jax.experimental import pallas as pl
from jax.experimental.pallas import tpu as pltpu
from jax.sharding import PartitionSpec as P

SWEEPS = 6
WALL_EXTRA = 0.2
FAR_EXTRA = 0.6
REG_WEIGHT = 0.5
CLIP_NORM = 64.0
EDGE = 8
SUB, LANE = 8, 128
F32, BF16 = jnp.float32, jnp.bfloat16
NT = (((1,), (1,)), ((), ()))
TN = (((0,), (0,)), ((), ()))
VMEM_BYTES = 16 * 1024 * 1024


def whole(shape):
    return pl.BlockSpec(shape, lambda *_: (0,) * len(shape))


def in_hbm(x):
    return pltpu.with_memory_space_constraint(x, pltpu.HBM)


def on_chip(kernel, operands, outs, scratch=(), far=(), far_outs=(), **kwargs):
    here, there = pl.BlockSpec(memory_space=pltpu.VMEM), pl.BlockSpec(memory_space=pltpu.HBM)
    return pl.pallas_call(
        kernel,
        in_specs=[here] * len(operands) + [there] * len(far),
        out_specs=[here] * len(outs) + [there] * len(far_outs),
        out_shape=[pltpu.VMEM(*o) for o in outs] + [pltpu.HBM(*o) for o in far_outs],
        scratch_shapes=list(scratch),
        compiler_params=params(),
        **kwargs,
    )(*operands, *[in_hbm(x) for x in far])


def like(x):
    return (x.shape, x.dtype)


def params():
    return pltpu.CompilerParams(vmem_limit_bytes=VMEM_BYTES)


def inverse_diag(diag, code):
    total = diag + jnp.where(code == 1, WALL_EXTRA, 0.0) + jnp.where(code == 2, FAR_EXTRA, 0.0)
    return 1.0 / total


def is_odd(axis):
    return lax.axis_index(axis) % 2 == 1


def load_kernel(count, *refs):
    far, near = refs[:count], refs[count : 2 * count]
    inv, first, second, sems = refs[2 * count :]
    copies = [pltpu.make_async_copy(far[k], near[k], sems.at[k]) for k in range(count)]
    for copy in copies:
        copy.start()
    src, cpl, dia, bc = near[:4]
    for copy in copies[:4]:
        copy.wait()
    nv, rows, _ = src.shape
    nc = cpl.shape[0]
    inv[...] = inverse_diag(dia[...], bc[...])
    odd = is_odd("gx")
    for f in range(nv + nc + 1):
        if f < nv + nc:
            ref, k = (src, f) if f < nv else (cpl, f - nv)
            top, bottom = ref[k, 0:16].astype(F32)[:EDGE], ref[k, rows - 16 :].astype(F32)[16 - EDGE :]
        else:
            top, bottom = inv[0:EDGE], inv[rows - EDGE :]
        first[f] = jnp.where(odd, top, bottom)
        second[f] = jnp.where(odd, bottom, top)
    for copy in copies[4:]:
        copy.wait()


def load(arrays):
    source, coupling = arrays[:2]
    nv, rows, cols = source.shape
    slab = ((nv + coupling.shape[0] + 1, EDGE, cols), F32)
    return on_chip(
        functools.partial(load_kernel, len(arrays)),
        [],
        [like(x) for x in arrays] + [((rows, cols), F32), slab, slab],
        [pltpu.SemaphoreType.DMA((len(arrays),))],
        far=arrays,
        name="load",
    )


def ordered(axis, first, second):
    odd = is_odd(axis)
    return jnp.where(odd, first, second), jnp.where(odd, second, first)


def cols_kernel(src, cpl, inv, row_first, row_second, col_first, col_second):
    nv, rows, cols = src.shape
    nc = cpl.shape[0]
    lane = lax.broadcasted_iota(jnp.int32, (rows, LANE), 1) // EDGE
    lane_h = lane[:EDGE]
    slabs = []
    for window, extra in ((slice(0, LANE), 0), (slice(cols - LANE, cols), EDGE)):
        mid = jnp.zeros((rows, LANE), F32)
        up = jnp.zeros((EDGE, LANE), F32)
        down = jnp.zeros((EDGE, LANE), F32)
        for f in range(nv + nc + 1):
            if f < nv:
                x = src[f, :, window].astype(F32)
            elif f < nv + nc:
                x = cpl[f - nv, :, window].astype(F32)
            else:
                x = inv[:, window]
            shift = (EDGE * f + extra) % LANE
            mid = jnp.where(lane == f, pltpu.roll(x, shift, 1), mid)
            north, south = ordered("gx", row_first[f, :, window], row_second[f, :, window])
            up = jnp.where(lane_h == f, pltpu.roll(north, shift, 1), up)
            down = jnp.where(lane_h == f, pltpu.roll(south, shift, 1), down)
        slabs.append(jnp.concatenate([up, mid, down], axis=0))
    odd = is_odd("gy")
    col_first[...] = jnp.where(odd, slabs[0], slabs[1])
    col_second[...] = jnp.where(odd, slabs[1], slabs[0])


def col_slabs(source, coupling, inv, row_halos):
    slab = ((source.shape[1] + 2 * EDGE, LANE), F32)
    return on_chip(cols_kernel, [source, coupling, inv, *row_halos], [slab, slab], name="col_slabs")


def column_of(row):
    hidden = row.shape[1]
    wide = jnp.concatenate([row, jnp.zeros((1, LANE - hidden), F32)], axis=1)
    return jnp.transpose(jnp.broadcast_to(wide, (LANE, LANE)))[:hidden]


def across(block, width):
    return jnp.concatenate([block] * (width // LANE), axis=1)


def weights_kernel(win, wmid, wtop, wout, bias, w1, w2, w3, cst):
    nf, hidden = win.shape
    step_rows, blk = hidden + 16, 16
    depth = w1.shape[1]
    feat_of = lax.broadcasted_iota(jnp.int32, (nf, depth), 1) // blk
    pick = (feat_of == lax.broadcasted_iota(jnp.int32, (nf, depth), 0)).astype(F32).astype(BF16)
    spread = lax.dot_general(win[...], pick, TN, preferred_element_type=F32)
    col = lax.broadcasted_iota(jnp.int32, (hidden, depth), 1)
    col_f = lax.broadcasted_iota(jnp.int32, (16, depth), 1)
    row_f = lax.broadcasted_iota(jnp.int32, (16, depth), 0)
    for r in range(blk):
        base = r * step_rows
        w1[base : base + hidden] = jnp.where(col % blk == r, spread, 0.0).astype(BF16)
        same = jnp.logical_and(col_f == row_f * blk + r, row_f < nf)
        w1[base + hidden : base + step_rows] = jnp.where(same, 1.0, 0.0).astype(BF16)
    w2[...] = jnp.transpose(wmid[...].astype(F32)).astype(BF16)
    w3[...] = jnp.transpose(wtop[...].astype(F32)).astype(BF16)
    for k in range(3):
        cst[k] = column_of(bias[k : k + 1, :])
    cst[3] = column_of(wout[...])


def prepare(weight_in, weight_mid, weight_top, weight_out, biases):
    nf, hidden = weight_in.shape
    depth = -(-nf * 16 // LANE) * LANE
    return on_chip(
        weights_kernel,
        [weight_in, weight_mid, weight_top, weight_out, biases],
        [
            ((16 * (hidden + 16), depth), BF16),
            ((hidden, hidden), BF16),
            ((hidden, hidden), BF16),
            ((4, hidden, LANE), F32),
        ],
        name="weights",
    )


def forward_kernel(first_row, feat, w1, w2, w3, cst, acts, beta, x1):
    nf, _, cols = feat.shape
    hidden = w2.shape[0]
    step_rows, blk, per = hidden + 16, 16, 4
    x1[...] = jnp.zeros(x1.shape, BF16)

    @pl.loop(0, acts.shape[0] // blk)
    def _(block):
        start = pl.multiple_of(block * blk, blk)
        x1[0 : nf * blk] = feat[:, pl.ds(first_row + start, blk), :].reshape(nf * blk, cols)
        b1, b2, b3, wo = (across(cst[k], cols) for k in range(4))
        lines = []
        first = jnp.dot(w1[...], x1[...], preferred_element_type=F32)
        for g in range(blk // per):
            ones = []
            for q in range(g * per, (g + 1) * per):
                part = first[q * step_rows : (q + 1) * step_rows]
                one = jnp.tanh(part[:hidden] + b1).astype(BF16)
                acts[start + q, 0:hidden] = one
                acts[start + q, 2 * hidden : 2 * hidden + 16] = part[hidden:].astype(BF16)
                ones.append(one)
            second = jnp.dot(w2[...], jnp.concatenate(ones, axis=1), preferred_element_type=F32)
            twos = []
            for q in range(per):
                two = jnp.tanh(second[:, q * cols : (q + 1) * cols] + b2).astype(BF16)
                acts[start + (g * per + q), hidden : 2 * hidden] = two
                twos.append(two)
            third = jnp.dot(w3[...], jnp.concatenate(twos, axis=1), preferred_element_type=F32)
            for q in range(per):
                three = jnp.tanh(third[:, q * cols : (q + 1) * cols] + b3).astype(BF16)
                acts[start + (g * per + q), 2 * hidden + 16 :] = three
                lines.append(1.0 + jnp.sum(three.astype(F32) * wo, axis=0, keepdims=True))
        beta[pl.ds(start, blk), :] = jnp.concatenate(lines, axis=0)


def forward(features, prepared, first_row, count):
    nf, _, cols = features.shape
    w1, w2 = prepared[:2]
    hidden = w2.shape[0]
    high = 3 * hidden + 16
    return on_chip(
        functools.partial(forward_kernel, first_row),
        [features, *prepared],
        [((count, high, cols), BF16), ((count, cols), F32)],
        [pltpu.VMEM((w1.shape[1], cols), BF16)],
        cost_estimate=pl.CostEstimate(
            flops=2 * count * cols * (nf + 2 * hidden) * hidden,
            bytes_accessed=2 * count * cols * (high + nf),
            transcendentals=3 * count * cols * hidden,
        ),
        name="network_forward",
    )


def tile_at(ref, lead, t, k):
    return ref[lead + (slice(t * SUB, (t + 1) * SUB), slice(k * LANE, (k + 1) * LANE))]


class Shifts:
    def __init__(self, tiles, lanes):
        self.tiles, self.lanes = tiles, lanes
        sub = lax.broadcasted_iota(jnp.int32, (SUB, LANE), 0)
        lane = lax.broadcasted_iota(jnp.int32, (SUB, LANE), 1)
        self.first_sub, self.last_sub = sub == 0, sub == SUB - 1
        self.first_lane, self.last_lane = lane == 0, lane == LANE - 1

    def above(self, ref, lead, t, k):
        here, other = tile_at(ref, lead, t, k), tile_at(ref, lead, max(t - 1, 0), k)
        return pltpu.roll(jnp.where(self.last_sub, other, here), 1, 0)

    def below(self, ref, lead, t, k):
        here, other = tile_at(ref, lead, t, k), tile_at(ref, lead, min(t + 1, self.tiles - 1), k)
        return pltpu.roll(jnp.where(self.first_sub, other, here), SUB - 1, 0)

    def left(self, ref, lead, t, k):
        here, other = tile_at(ref, lead, t, k), tile_at(ref, lead, t, (k - 1) % self.lanes)
        return pltpu.roll(jnp.where(self.last_lane, other, here), 1, 1)

    def right(self, ref, lead, t, k):
        here, other = tile_at(ref, lead, t, k), tile_at(ref, lead, t, (k + 1) % self.lanes)
        return pltpu.roll(jnp.where(self.first_lane, other, here), LANE - 1, 1)


def sweep_kernel(
    src, cpl, inverse, prod, beta_a, beta_b, row_first, row_second, col_first, col_second, mix,
    adj_out, sens, beta,
    raw, src_x, cpl_x, adj_a, adj_b,
):
    nv, rows, cols = src.shape
    nc = cpl.shape[0]
    tall = rows + 2 * EDGE
    tiles, lanes = tall // SUB, cols // LANE + 1
    shifts = Shifts(tiles, lanes)
    inner = slice(EDGE, EDGE + rows)
    lane = lax.broadcasted_iota(jnp.int32, (tall, LANE), 1)
    from_east, from_west = lane < EDGE, lane >= LANE - EDGE
    west, east = ordered("gy", col_first[...], col_second[...])
    for f in range(nv + nc + 1):
        if f < nv:
            raw[f, inner, 0:cols] = src[f].astype(F32)
        elif f < nv + nc:
            raw[f, inner, 0:cols] = cpl[f - nv].astype(F32)
        else:
            raw[f, inner, 0:cols] = inverse[...]
        north, south = ordered("gx", row_first[f], row_second[f])
        raw[f, 0:EDGE, 0:cols] = north
        raw[f, EDGE + rows :, 0:cols] = south
        e = pltpu.roll(east, (LANE - EDGE * f) % LANE, 1)
        w = pltpu.roll(west, (LANE - EDGE - EDGE * f) % LANE, 1)
        raw[f, :, cols:] = jnp.where(from_east, e, jnp.where(from_west, w, 0.0))

    moves = (shifts.above, shifts.below, shifts.left, shifts.right)
    for t in range(tiles):
        for k in range(lanes):
            at = (slice(t * SUB, (t + 1) * SUB), slice(k * LANE, (k + 1) * LANE))
            inv = tile_at(raw, (nv + nc,), t, k)
            for v in range(nv):
                src_x[(v,) + at] = inv * tile_at(raw, (v,), t, k)
            for d in range(nc):
                cpl_x[(d,) + at] = inv * moves[d](raw, (nv + d,), t, k)

    def sweep(old, new, last):
        for t in range(1, tiles - 1) if last else range(tiles):
            for k in range(lanes - 1) if last else range(lanes):
                at = (slice(t * SUB, (t + 1) * SUB), slice(k * LANE, (k + 1) * LANE))
                couple = [cpl_x[(d,) + at] for d in range(nc)]
                total = [src_x[(a,) + at] for a in range(nv)]
                for b in range(nv):
                    inc = couple[0] * moves[0](old, (b,), t, k)
                    for d in range(1, nc):
                        inc = inc + couple[d] * moves[d](old, (b,), t, k)
                    total = [total[a] + mix[b, a] * inc for a in range(nv)]
                if last:
                    at = (slice((t - 1) * SUB, t * SUB), at[1])
                for a in range(nv):
                    new[(a,) + at] = total[a]

    sweep(src_x, adj_a, False)

    @pl.loop(0, (SWEEPS - 2) // 2)
    def _(i):
        sweep(adj_a, adj_b, False)
        sweep(adj_b, adj_a, False)

    sweep(adj_a, adj_out, True)
    half = beta_a.shape[0]
    beta[0:half] = beta_a[...]
    beta[half:] = beta_b[...]
    sens[...] = adj_out[nv - 1] * prod[...] + REG_WEIGHT * (beta[...] - 1.0)


def sweeps(source, coupling, inverse, production, betas, halos, mixing):
    nv, rows, cols = source.shape
    nc = coupling.shape[0]
    tall, wide = rows + 2 * EDGE, cols + LANE
    near = pl.BlockSpec(memory_space=pltpu.VMEM)
    operands = [source, coupling, inverse, production, *betas, *halos]
    flat = ((rows, cols), F32)
    return pl.pallas_call(
        sweep_kernel,
        in_specs=[near] * len(operands) + [pl.BlockSpec(memory_space=pltpu.SMEM)],
        out_specs=[near] * 3,
        out_shape=[pltpu.VMEM((nv, rows, cols), F32), pltpu.VMEM(*flat), pltpu.VMEM(*flat)],
        scratch_shapes=[
            pltpu.VMEM((nv + nc + 1, tall, wide), F32),
            pltpu.VMEM((nv, tall, wide), F32),
            pltpu.VMEM((nc, tall, wide), F32),
            pltpu.VMEM((nv, tall, wide), F32),
            pltpu.VMEM((nv, tall, wide), F32),
        ],
        compiler_params=params(),
        name="sweeps",
    )(*operands, mixing)


def backward_kernel(
    num_feat, adj, beta, sens, wmid, wtop, cst, acts_a, acts_b,
    packed, adj_out, beta_out,
    sums, grads, sems,
):
    out_copies = [
        pltpu.make_async_copy(adj, adj_out, sems.at[0]),
        pltpu.make_async_copy(beta, beta_out, sems.at[1]),
    ]
    for copy in out_copies:
        copy.start()
    blk, cols = 8, sens.shape[1]
    hidden = wmid.shape[0]
    sums[...] = jnp.zeros(sums.shape, F32)
    grads[...] = jnp.zeros(grads.shape, F32)
    feat_row = lax.broadcasted_iota(jnp.int32, (16, cols), 0)

    def fold(x):
        parts = [x[:, k * LANE : (k + 1) * LANE] for k in range(cols // LANE)]
        return functools.reduce(jnp.add, parts)

    def with_sens(feats, line):
        out, rest = feats.astype(F32), line
        for k in range(3):
            part = rest.astype(BF16).astype(F32)
            out = jnp.where(feat_row == num_feat + k, jnp.broadcast_to(part, out.shape), out)
            rest = rest - part
        return out.astype(BF16)

    def block(acts, start, first_row):
        rows_sens = sens[pl.ds(pl.multiple_of(first_row + start, blk), blk), :]
        wo = across(cst[3], cols)
        lefts, rights = [], []
        acc = [jnp.zeros((hidden, LANE), F32) for _ in range(3)]
        for q in range(blk):
            one, two = acts[start + q, 0:hidden], acts[start + q, hidden : 2 * hidden]
            three = acts[start + q, 2 * hidden + 16 :]
            three_f = three.astype(F32)
            line = rows_sens[q : q + 1]
            d3 = jnp.broadcast_to(line, (hidden, cols)) * wo * (1.0 - three_f * three_f)
            acc[2] = acc[2] + fold(d3)
            d3 = d3.astype(BF16)
            two_f = two.astype(F32)
            d2 = jnp.dot(wtop[...], d3, preferred_element_type=F32) * (1.0 - two_f * two_f)
            acc[1] = acc[1] + fold(d2)
            d2 = d2.astype(BF16)
            one_f = one.astype(F32)
            d1 = jnp.dot(wmid[...], d2, preferred_element_type=F32) * (1.0 - one_f * one_f)
            acc[0] = acc[0] + fold(d1)
            d1 = d1.astype(BF16)
            feats = with_sens(acts[start + q, 2 * hidden : 2 * hidden + 16], line)
            lefts.append(jnp.concatenate([one, two, feats], axis=0))
            rights.append(jnp.concatenate([d2, d3, d1, three], axis=0))
        grads[...] += lax.dot_general(
            jnp.concatenate(lefts, axis=1), jnp.concatenate(rights, axis=1), NT, preferred_element_type=F32
        )
        for k in range(3):
            sums[k] += acc[k]

    half = acts_a.shape[0]
    for acts, first_row in ((acts_a, 0), (acts_b, half)):

        @pl.loop(0, acts.shape[0] // blk)
        def _(i, acts=acts, first_row=first_row):
            block(acts, pl.multiple_of(i * blk, blk), first_row)

    lane = lax.broadcasted_iota(jnp.int32, (hidden, LANE), 1)
    packed[0:hidden, :] = jnp.where(
        lane < hidden, grads[0:hidden, 0:LANE], grads[hidden : 2 * hidden, 0:LANE]
    )
    low = grads[2 * hidden : 2 * hidden + SUB, 2 * hidden : 3 * hidden]
    high = grads[2 * hidden + SUB :, 2 * hidden : 3 * hidden]
    outs = grads[2 * hidden + SUB :, 3 * hidden :]
    row = lax.broadcasted_iota(jnp.int32, (SUB, hidden), 0)
    at = num_feat - SUB
    tail = jnp.where(row < at, high, 0.0)
    lines = [jnp.sum(jnp.where((row >= at) & (row < at + 3), outs, 0.0), axis=0, keepdims=True)]
    lines += [jnp.sum(jnp.transpose(sums[k]), axis=0, keepdims=True) for k in range(3)]
    for k, line in enumerate(lines):
        tail = tail + jnp.where(row == k + at, jnp.broadcast_to(line, (SUB, hidden)), 0.0)
    packed[hidden : hidden + SUB, :] = jnp.concatenate([low, tail], axis=1)
    for copy in out_copies:
        copy.wait()


def backward(num_feat, adj, beta, sens, weight_mid, weight_top, cst, acts):
    hidden = weight_mid.shape[0]
    return on_chip(
        functools.partial(backward_kernel, num_feat),
        [adj, beta, sens, weight_mid, weight_top, cst, *acts],
        [((hidden + SUB, LANE), F32)],
        [
            pltpu.VMEM((3, hidden, LANE), F32),
            pltpu.VMEM((2 * hidden + 16, 4 * hidden), F32),
            pltpu.SemaphoreType.DMA((2,)),
        ],
        far_outs=[like(adj), like(beta)],
        name="backward",
    )


def clip_kernel(own, other, gin, gmid, gtop, gout, gbias):
    hidden = gmid.shape[0]
    total = jnp.where(is_odd("gy"), own[...], other[...])
    squares = jnp.sum(jnp.sum(total * total, axis=0, keepdims=True), axis=1, keepdims=True)
    total = total * (CLIP_NORM / jnp.maximum(jnp.sqrt(squares), CLIP_NORM))
    gmid[...] = total[:hidden, :hidden]
    gtop[...] = total[:hidden, hidden:]
    low, high = total[hidden:, :hidden], total[hidden:, hidden:]
    gin[0:SUB] = low
    gin[SUB:] = high[: gin.shape[0] - SUB]
    at = gin.shape[0] - SUB
    gout[...] = high[at : at + 1]
    gbias[...] = high[at + 1 : at + 4]


def clip_all(own, other, num_feat, hidden):
    shapes = [(num_feat, hidden), (hidden, hidden), (hidden, hidden), (1, hidden), (3, hidden)]
    return pl.pallas_call(
        clip_kernel,
        grid=(1,),
        in_specs=[whole(own.shape)] * 2,
        out_specs=[whole(s) for s in shapes],
        out_shape=[jax.ShapeDtypeStruct(s, F32) for s in shapes],
        compiler_params=params(),
        name="clip",
    )(own, other)


def sum_over_case(packed):
    num_x, num_y = lax.axis_size("gx"), lax.axis_size("gy")
    to_odd = [(i, i + 1) for i in range(0, num_y, 2)]
    total = packed + lax.ppermute(packed, "gy", to_odd)
    step = 2
    while step < num_y:
        pairs = [(i, i ^ step) for i in range(1, num_y, 2)]
        total = total + lax.ppermute(total, "gy", pairs)
        step *= 2
    step = 1
    while step < num_x:
        pairs = [(i * num_y + j, (i ^ step) * num_y + j) for i in range(num_x) for j in range(1, num_y, 2)]
        total = total + lax.ppermute(total, ("gx", "gy"), pairs)
        step *= 2
    return total, lax.ppermute(total, "gy", [(b, a) for a, b in to_odd])


def swaps(first, second, axis):
    count = lax.axis_size(axis)

    def pairs(start):
        low = range(start, count - 1, 2)
        return [(i, i + 1) for i in low] + [(i + 1, i) for i in low]

    return lax.ppermute(first, axis, pairs(0)), lax.ppermute(second, axis, pairs(1))


def shards(
    features, source, coupling, diagonal, production, bc_code, mixing,
    weight_in, weight_mid, weight_top, weight_out, biases,
):
    num_feat, rows, _ = features.shape
    hidden = weight_mid.shape[0]
    loaded = load([
        source, coupling, diagonal, bc_code, production, features,
        weight_in, weight_mid, weight_top, weight_out.reshape(1, hidden), biases,
    ])
    source, coupling, _, _, production, features, weight_in, weight_mid, weight_top, wout, biases = loaded[:11]
    inverse, *row_slabs = loaded[11:]
    row_halos = swaps(*row_slabs, "gx")
    prepared = prepare(weight_in, weight_mid, weight_top, wout, biases)
    half = rows // 32 * 16
    acts_a, beta_a = forward(features, prepared, 0, half)
    *row_halos, beta_a = lax.optimization_barrier((*row_halos, beta_a))
    col_halos = swaps(*col_slabs(source, coupling, inverse, row_halos), "gy")
    acts_b, beta_b = forward(features, prepared, half, rows - half)
    adj, sens, beta = sweeps(
        source, coupling, inverse, production, (beta_a, beta_b), (*row_halos, *col_halos), mixing
    )
    packed, adjoint, beta = backward(num_feat, adj, beta, sens, weight_mid, weight_top, prepared[3], (acts_a, acts_b))
    grad_in, grad_mid, grad_top, grad_out, grad_bias = clip_all(*sum_over_case(packed), num_feat, hidden)
    return (adjoint, beta, grad_in, grad_mid, grad_top, grad_out.reshape(hidden), grad_bias)


def solution(mesh):
    cells3 = P(None, ("case", "gx"), "gy")
    cells2 = P(("case", "gx"), "gy")
    return jax.shard_map(
        shards,
        mesh=mesh,
        in_specs=(cells3,) * 3 + (cells2,) * 3 + (P(),) * 6,
        out_specs=(cells3, cells2, P("case"), P("case"), P("case"), P("case"), P("case")),
        check_vma=False,
    )
```

```python
import functools

import jax
import jax.numpy as jnp
from jax import lax
from jax.experimental import pallas as pl
from jax.experimental.pallas import tpu as pltpu
from jax.sharding import PartitionSpec as P

SWEEPS = 6
WALL_EXTRA = 0.2
FAR_EXTRA = 0.6
REG_WEIGHT = 0.5
CLIP_NORM = 64.0
EDGE = 8
SUB, LANE = 8, 128
F32, BF16 = jnp.float32, jnp.bfloat16
NT = (((1,), (1,)), ((), ()))
TN = (((0,), (0,)), ((), ()))
VMEM_BYTES = 16 * 1024 * 1024


def whole(shape):
    return pl.BlockSpec(shape, lambda *_: (0,) * len(shape))


def in_hbm(x):
    return pltpu.with_memory_space_constraint(x, pltpu.HBM)


def on_chip(kernel, operands, outs, scratch=(), far=(), far_outs=(), **kwargs):
    here, there = pl.BlockSpec(memory_space=pltpu.VMEM), pl.BlockSpec(memory_space=pltpu.HBM)
    return pl.pallas_call(
        kernel,
        in_specs=[here] * len(operands) + [there] * len(far),
        out_specs=[here] * len(outs) + [there] * len(far_outs),
        out_shape=[pltpu.VMEM(*o) for o in outs] + [pltpu.HBM(*o) for o in far_outs],
        scratch_shapes=list(scratch),
        compiler_params=params(),
        **kwargs,
    )(*operands, *[in_hbm(x) for x in far])


def like(x):
    return (x.shape, x.dtype)


def params():
    return pltpu.CompilerParams(vmem_limit_bytes=VMEM_BYTES)


def inverse_diag(diag, code):
    total = diag + jnp.where(code == 1, WALL_EXTRA, 0.0) + jnp.where(code == 2, FAR_EXTRA, 0.0)
    return 1.0 / total


def is_odd(axis):
    return lax.axis_index(axis) % 2 == 1


def load_kernel(count, *refs):
    far, near = refs[:count], refs[count : 2 * count]
    inv, first, second, sems = refs[2 * count :]
    copies = [pltpu.make_async_copy(far[k], near[k], sems.at[k]) for k in range(count)]
    for copy in copies:
        copy.start()
    src, cpl, dia, bc = near[:4]
    for copy in copies[:4]:
        copy.wait()
    nv, rows, _ = src.shape
    nc = cpl.shape[0]
    inv[...] = inverse_diag(dia[...], bc[...])
    odd = is_odd("gx")
    for f in range(nv + nc + 1):
        if f < nv + nc:
            ref, k = (src, f) if f < nv else (cpl, f - nv)
            top, bottom = ref[k, 0:16].astype(F32)[:EDGE], ref[k, rows - 16 :].astype(F32)[16 - EDGE :]
        else:
            top, bottom = inv[0:EDGE], inv[rows - EDGE :]
        first[f] = jnp.where(odd, top, bottom)
        second[f] = jnp.where(odd, bottom, top)
    for copy in copies[4:]:
        copy.wait()


def load(arrays):
    source, coupling = arrays[:2]
    nv, rows, cols = source.shape
    slab = ((nv + coupling.shape[0] + 1, EDGE, cols), F32)
    return on_chip(
        functools.partial(load_kernel, len(arrays)),
        [],
        [like(x) for x in arrays] + [((rows, cols), F32), slab, slab],
        [pltpu.SemaphoreType.DMA((len(arrays),))],
        far=arrays,
        name="load",
    )


def ordered(axis, first, second):
    odd, at = is_odd(axis), lax.axis_index(axis)
    before, after = jnp.where(odd, first, second), jnp.where(odd, second, first)
    return jnp.where(at == 0, 0.0, before), jnp.where(at == lax.axis_size(axis) - 1, 0.0, after)


def cols_kernel(src, cpl, inv, row_first, row_second, col_first, col_second):
    nv, rows, cols = src.shape
    nc = cpl.shape[0]
    lane = lax.broadcasted_iota(jnp.int32, (rows, LANE), 1) // EDGE
    lane_h = lane[:EDGE]
    slabs = []
    for window, extra in ((slice(0, LANE), 0), (slice(cols - LANE, cols), EDGE)):
        mid = jnp.zeros((rows, LANE), F32)
        up = jnp.zeros((EDGE, LANE), F32)
        down = jnp.zeros((EDGE, LANE), F32)
        for f in range(nv + nc + 1):
            if f < nv:
                x = src[f, :, window].astype(F32)
            elif f < nv + nc:
                x = cpl[f - nv, :, window].astype(F32)
            else:
                x = inv[:, window]
            shift = (EDGE * f + extra) % LANE
            mid = jnp.where(lane == f, pltpu.roll(x, shift, 1), mid)
            north, south = ordered("gx", row_first[f, :, window], row_second[f, :, window])
            up = jnp.where(lane_h == f, pltpu.roll(north, shift, 1), up)
            down = jnp.where(lane_h == f, pltpu.roll(south, shift, 1), down)
        slabs.append(jnp.concatenate([up, mid, down], axis=0))
    odd = is_odd("gy")
    col_first[...] = jnp.where(odd, slabs[0], slabs[1])
    col_second[...] = jnp.where(odd, slabs[1], slabs[0])


def col_slabs(source, coupling, inv, row_halos):
    slab = ((source.shape[1] + 2 * EDGE, LANE), F32)
    return on_chip(cols_kernel, [source, coupling, inv, *row_halos], [slab, slab], name="col_slabs")


def column_of(row):
    hidden = row.shape[1]
    wide = jnp.concatenate([row, jnp.zeros((1, LANE - hidden), F32)], axis=1)
    return jnp.transpose(jnp.broadcast_to(wide, (LANE, LANE)))[:hidden]


def across(block, width):
    return jnp.concatenate([block] * (width // LANE), axis=1)


def weights_kernel(win, wmid, wtop, wout, bias, w1, w2, w3, cst):
    nf, hidden = win.shape
    step_rows, blk = hidden + 16, 16
    depth = w1.shape[1]
    feat_of = lax.broadcasted_iota(jnp.int32, (nf, depth), 1) // blk
    pick = (feat_of == lax.broadcasted_iota(jnp.int32, (nf, depth), 0)).astype(F32).astype(BF16)
    spread = lax.dot_general(win[...], pick, TN, preferred_element_type=F32)
    col = lax.broadcasted_iota(jnp.int32, (hidden, depth), 1)
    col_f = lax.broadcasted_iota(jnp.int32, (16, depth), 1)
    row_f = lax.broadcasted_iota(jnp.int32, (16, depth), 0)
    for r in range(blk):
        base = r * step_rows
        w1[base : base + hidden] = jnp.where(col % blk == r, spread, 0.0).astype(BF16)
        same = jnp.logical_and(col_f == row_f * blk + r, row_f < nf)
        w1[base + hidden : base + step_rows] = jnp.where(same, 1.0, 0.0).astype(BF16)
    w2[...] = jnp.transpose(wmid[...].astype(F32)).astype(BF16)
    w3[...] = jnp.transpose(wtop[...].astype(F32)).astype(BF16)
    for k in range(3):
        cst[k] = column_of(bias[k : k + 1, :])
    cst[3] = column_of(wout[...])


def prepare(weight_in, weight_mid, weight_top, weight_out, biases):
    nf, hidden = weight_in.shape
    depth = -(-nf * 16 // LANE) * LANE
    return on_chip(
        weights_kernel,
        [weight_in, weight_mid, weight_top, weight_out, biases],
        [
            ((16 * (hidden + 16), depth), BF16),
            ((hidden, hidden), BF16),
            ((hidden, hidden), BF16),
            ((4, hidden, LANE), F32),
        ],
        name="weights",
    )


def forward_kernel(first_row, feat, w1, w2, w3, cst, acts, beta, x1):
    nf, _, cols = feat.shape
    hidden = w2.shape[0]
    step_rows, blk, per = hidden + 16, 16, 4
    x1[...] = jnp.zeros(x1.shape, BF16)

    @pl.loop(0, acts.shape[0] // blk)
    def _(block):
        start = pl.multiple_of(block * blk, blk)
        x1[0 : nf * blk] = feat[:, pl.ds(first_row + start, blk), :].reshape(nf * blk, cols)
        b1, b2, b3, wo = (across(cst[k], cols) for k in range(4))
        lines = []
        first = jnp.dot(w1[...], x1[...], preferred_element_type=F32)
        for g in range(blk // per):
            ones = []
            for q in range(g * per, (g + 1) * per):
                part = first[q * step_rows : (q + 1) * step_rows]
                one = jnp.tanh(part[:hidden] + b1).astype(BF16)
                acts[start + q, 0:hidden] = one
                acts[start + q, 2 * hidden : 2 * hidden + 16] = part[hidden:].astype(BF16)
                ones.append(one)
            second = jnp.dot(w2[...], jnp.concatenate(ones, axis=1), preferred_element_type=F32)
            twos = []
            for q in range(per):
                two = jnp.tanh(second[:, q * cols : (q + 1) * cols] + b2).astype(BF16)
                acts[start + (g * per + q), hidden : 2 * hidden] = two
                twos.append(two)
            third = jnp.dot(w3[...], jnp.concatenate(twos, axis=1), preferred_element_type=F32)
            for q in range(per):
                three = jnp.tanh(third[:, q * cols : (q + 1) * cols] + b3).astype(BF16)
                acts[start + (g * per + q), 2 * hidden + 16 :] = three
                lines.append(1.0 + jnp.sum(three.astype(F32) * wo, axis=0, keepdims=True))
        beta[pl.ds(start, blk), :] = jnp.concatenate(lines, axis=0)


def forward(features, prepared, first_row, count):
    nf, _, cols = features.shape
    w1, w2 = prepared[:2]
    hidden = w2.shape[0]
    high = 3 * hidden + 16
    return on_chip(
        functools.partial(forward_kernel, first_row),
        [features, *prepared],
        [((count, high, cols), BF16), ((count, cols), F32)],
        [pltpu.VMEM((w1.shape[1], cols), BF16)],
        cost_estimate=pl.CostEstimate(
            flops=2 * count * cols * (nf + 2 * hidden) * hidden,
            bytes_accessed=2 * count * cols * (high + nf),
            transcendentals=3 * count * cols * hidden,
        ),
        name="network_forward",
    )


def tile_at(ref, lead, t, k):
    return ref[lead + (slice(t * SUB, (t + 1) * SUB), slice(k * LANE, (k + 1) * LANE))]


class Shifts:
    def __init__(self, tiles, lanes):
        self.tiles, self.lanes = tiles, lanes
        sub = lax.broadcasted_iota(jnp.int32, (SUB, LANE), 0)
        lane = lax.broadcasted_iota(jnp.int32, (SUB, LANE), 1)
        self.first_sub, self.last_sub = sub == 0, sub == SUB - 1
        self.first_lane, self.last_lane = lane == 0, lane == LANE - 1

    def above(self, ref, lead, t, k):
        here, other = tile_at(ref, lead, t, k), tile_at(ref, lead, max(t - 1, 0), k)
        return pltpu.roll(jnp.where(self.last_sub, other, here), 1, 0)

    def below(self, ref, lead, t, k):
        here, other = tile_at(ref, lead, t, k), tile_at(ref, lead, min(t + 1, self.tiles - 1), k)
        return pltpu.roll(jnp.where(self.first_sub, other, here), SUB - 1, 0)

    def left(self, ref, lead, t, k):
        here, other = tile_at(ref, lead, t, k), tile_at(ref, lead, t, (k - 1) % self.lanes)
        return pltpu.roll(jnp.where(self.last_lane, other, here), 1, 1)

    def right(self, ref, lead, t, k):
        here, other = tile_at(ref, lead, t, k), tile_at(ref, lead, t, (k + 1) % self.lanes)
        return pltpu.roll(jnp.where(self.first_lane, other, here), LANE - 1, 1)


def sweep_kernel(
    src, cpl, inverse, prod, beta_a, beta_b, row_first, row_second, col_first, col_second, mix,
    adj_out, sens, beta,
    raw, src_x, cpl_x, adj_a, adj_b,
):
    nv, rows, cols = src.shape
    nc = cpl.shape[0]
    tall = rows + 2 * EDGE
    tiles, lanes = tall // SUB, cols // LANE + 1
    shifts = Shifts(tiles, lanes)
    inner = slice(EDGE, EDGE + rows)
    lane = lax.broadcasted_iota(jnp.int32, (tall, LANE), 1)
    from_east, from_west = lane < EDGE, lane >= LANE - EDGE
    west, east = ordered("gy", col_first[...], col_second[...])
    for f in range(nv + nc + 1):
        if f < nv:
            raw[f, inner, 0:cols] = src[f].astype(F32)
        elif f < nv + nc:
            raw[f, inner, 0:cols] = cpl[f - nv].astype(F32)
        else:
            raw[f, inner, 0:cols] = inverse[...]
        north, south = ordered("gx", row_first[f], row_second[f])
        raw[f, 0:EDGE, 0:cols] = north
        raw[f, EDGE + rows :, 0:cols] = south
        e = pltpu.roll(east, (LANE - EDGE * f) % LANE, 1)
        w = pltpu.roll(west, (LANE - EDGE - EDGE * f) % LANE, 1)
        raw[f, :, cols:] = jnp.where(from_east, e, jnp.where(from_west, w, 0.0))

    moves = (shifts.above, shifts.below, shifts.left, shifts.right)
    for t in range(tiles):
        for k in range(lanes):
            at = (slice(t * SUB, (t + 1) * SUB), slice(k * LANE, (k + 1) * LANE))
            inv = tile_at(raw, (nv + nc,), t, k)
            for v in range(nv):
                src_x[(v,) + at] = inv * tile_at(raw, (v,), t, k)
            for d in range(nc):
                cpl_x[(d,) + at] = inv * moves[d](raw, (nv + d,), t, k)

    def sweep(old, new, last):
        for t in range(1, tiles - 1) if last else range(tiles):
            for k in range(lanes - 1) if last else range(lanes):
                at = (slice(t * SUB, (t + 1) * SUB), slice(k * LANE, (k + 1) * LANE))
                couple = [cpl_x[(d,) + at] for d in range(nc)]
                total = [src_x[(a,) + at] for a in range(nv)]
                for b in range(nv):
                    inc = couple[0] * moves[0](old, (b,), t, k)
                    for d in range(1, nc):
                        inc = inc + couple[d] * moves[d](old, (b,), t, k)
                    total = [total[a] + mix[b, a] * inc for a in range(nv)]
                if last:
                    at = (slice((t - 1) * SUB, t * SUB), at[1])
                for a in range(nv):
                    new[(a,) + at] = total[a]

    sweep(src_x, adj_a, False)

    @pl.loop(0, (SWEEPS - 2) // 2)
    def _(i):
        sweep(adj_a, adj_b, False)
        sweep(adj_b, adj_a, False)

    sweep(adj_a, adj_out, True)
    half = beta_a.shape[0]
    beta[0:half] = beta_a[...]
    beta[half:] = beta_b[...]
    sens[...] = adj_out[nv - 1] * prod[...] + REG_WEIGHT * (beta[...] - 1.0)


def sweeps(source, coupling, inverse, production, betas, halos, mixing):
    nv, rows, cols = source.shape
    nc = coupling.shape[0]
    tall, wide = rows + 2 * EDGE, cols + LANE
    near = pl.BlockSpec(memory_space=pltpu.VMEM)
    operands = [source, coupling, inverse, production, *betas, *halos]
    flat = ((rows, cols), F32)
    return pl.pallas_call(
        sweep_kernel,
        in_specs=[near] * len(operands) + [pl.BlockSpec(memory_space=pltpu.SMEM)],
        out_specs=[near] * 3,
        out_shape=[pltpu.VMEM((nv, rows, cols), F32), pltpu.VMEM(*flat), pltpu.VMEM(*flat)],
        scratch_shapes=[
            pltpu.VMEM((nv + nc + 1, tall, wide), F32),
            pltpu.VMEM((nv, tall, wide), F32),
            pltpu.VMEM((nc, tall, wide), F32),
            pltpu.VMEM((nv, tall, wide), F32),
            pltpu.VMEM((nv, tall, wide), F32),
        ],
        compiler_params=params(),
        name="sweeps",
    )(*operands, mixing)


def backward_kernel(
    num_feat, adj, beta, sens, wmid, wtop, cst, acts_a, acts_b,
    packed, adj_out, beta_out,
    sums, g_mid, g_top, g_in, sems,
):
    out_copies = [
        pltpu.make_async_copy(adj, adj_out, sems.at[0]),
        pltpu.make_async_copy(beta, beta_out, sems.at[1]),
    ]
    for copy in out_copies:
        copy.start()
    blk, cols = 8, sens.shape[1]
    hidden = wmid.shape[0]
    sums[...] = jnp.zeros(sums.shape, F32)
    g_mid[...] = jnp.zeros(g_mid.shape, F32)
    g_top[...] = jnp.zeros(g_top.shape, F32)
    g_in[...] = jnp.zeros(g_in.shape, F32)

    def fold(x):
        parts = [x[:, k * LANE : (k + 1) * LANE] for k in range(cols // LANE)]
        return functools.reduce(jnp.add, parts)

    def joined(xs):
        return jnp.concatenate(xs, axis=1)

    def outer(x, d):
        return lax.dot_general(x, d, NT, preferred_element_type=F32)

    def block(acts, start, first_row):
        rows_sens = sens[pl.ds(pl.multiple_of(first_row + start, blk), blk), :]
        wo = across(cst[3], cols)

        def layer(lo, high):
            return joined([acts[start + q, lo:high] for q in range(blk)])

        def behind(weight, delta, lo):
            raw = jnp.dot(weight, delta, preferred_element_type=F32)
            total, out = jnp.zeros((hidden, LANE), F32), []
            for q in range(blk):
                act = acts[start + q, lo : lo + hidden].astype(F32)
                d = raw[:, q * cols : (q + 1) * cols] * (1.0 - act * act)
                total = total + fold(d)
                out.append(d.astype(BF16))
            return joined(out), total

        out_sum, top_sum, d3 = jnp.zeros((hidden, LANE), F32), jnp.zeros((hidden, LANE), F32), []
        for q in range(blk):
            act = acts[start + q, 2 * hidden + 16 :].astype(F32)
            sen = jnp.broadcast_to(rows_sens[q : q + 1], (hidden, cols))
            out_sum = out_sum + fold(act * sen)
            d = sen * wo * (1.0 - act * act)
            top_sum = top_sum + fold(d)
            d3.append(d.astype(BF16))
        d3 = joined(d3)
        d2, mid_sum = behind(wtop[...], d3, hidden)
        g_top[...] += outer(layer(hidden, 2 * hidden), d3)
        d1, in_sum = behind(wmid[...], d2, 0)
        g_mid[...] += outer(layer(0, hidden), d2)
        g_in[...] += outer(d1, layer(2 * hidden, 2 * hidden + 16))
        for k, part in enumerate((out_sum, in_sum, mid_sum, top_sum)):
            sums[k] += part

    half = acts_a.shape[0]
    for acts, first_row in ((acts_a, 0), (acts_b, half)):

        @pl.loop(0, acts.shape[0] // blk)
        def _(i, acts=acts, first_row=first_row):
            block(acts, pl.multiple_of(i * blk, blk), first_row)

    packed[0:hidden, :] = joined([g_mid[...], g_top[...]])
    turned = jnp.transpose(joined([g_in[...], jnp.zeros((hidden, LANE - 16), F32)]))
    tail = turned[SUB : 2 * SUB]
    row = lax.broadcasted_iota(jnp.int32, (SUB, hidden), 0)
    for k in range(4):
        line = jnp.sum(jnp.transpose(sums[k]), axis=0, keepdims=True)
        tail = tail + jnp.where(row == k + num_feat - SUB, jnp.broadcast_to(line, (SUB, hidden)), 0.0)
    packed[hidden : hidden + SUB, :] = joined([turned[0:SUB], tail])
    for copy in out_copies:
        copy.wait()


def backward(num_feat, adj, beta, sens, weight_mid, weight_top, cst, acts):
    hidden = weight_mid.shape[0]
    return on_chip(
        functools.partial(backward_kernel, num_feat),
        [adj, beta, sens, weight_mid, weight_top, cst, *acts],
        [((hidden + SUB, LANE), F32)],
        [
            pltpu.VMEM((4, hidden, LANE), F32),
            pltpu.VMEM((hidden, hidden), F32),
            pltpu.VMEM((hidden, hidden), F32),
            pltpu.VMEM((hidden, 16), F32),
            pltpu.SemaphoreType.DMA((2,)),
        ],
        far_outs=[like(adj), like(beta)],
        name="backward",
    )


def clip_kernel(parts, gin, gmid, gtop, gout, gbias):
    hidden = gmid.shape[0]
    total = parts[0]
    for k in range(1, parts.shape[0]):
        total = total + parts[k]
    squares = jnp.sum(jnp.sum(total * total, axis=0, keepdims=True), axis=1, keepdims=True)
    total = total * (CLIP_NORM / jnp.maximum(jnp.sqrt(squares), CLIP_NORM))
    gmid[...] = total[:hidden, :hidden]
    gtop[...] = total[:hidden, hidden:]
    low, high = total[hidden:, :hidden], total[hidden:, hidden:]
    gin[0:SUB] = low
    gin[SUB:] = high[: gin.shape[0] - SUB]
    at = gin.shape[0] - SUB
    gout[...] = high[at : at + 1]
    gbias[...] = high[at + 1 : at + 4]


def clip_all(parts, num_feat, hidden):
    shapes = [(num_feat, hidden), (hidden, hidden), (hidden, hidden), (1, hidden), (3, hidden)]
    return pl.pallas_call(
        clip_kernel,
        grid=(1,),
        in_specs=[whole(parts.shape)],
        out_specs=[whole(s) for s in shapes],
        out_shape=[jax.ShapeDtypeStruct(s, F32) for s in shapes],
        compiler_params=params(),
        name="clip",
    )(parts)


def parts_of_sum(packed):
    count = lax.axis_size("gy")
    step = 1
    while step < count:
        packed = packed + lax.ppermute(packed, "gy", [(i, i ^ step) for i in range(count)])
        step *= 2
    return lax.all_gather(packed, "gx")


def swaps(first, second, axis):
    count = lax.axis_size(axis)

    def pairs(start):
        low = range(start, count - 1, 2)
        paired = [(i, i + 1) for i in low] + [(i + 1, i) for i in low]
        alone = set(range(count)) - {i for i, _ in paired}
        return paired + [(i, i) for i in sorted(alone)]

    return lax.ppermute(first, axis, pairs(0)), lax.ppermute(second, axis, pairs(1))


def shards(
    features, source, coupling, diagonal, production, bc_code, mixing,
    weight_in, weight_mid, weight_top, weight_out, biases,
):
    num_feat, rows, _ = features.shape
    hidden = weight_mid.shape[0]
    loaded = load([
        source, coupling, diagonal, bc_code, production, features,
        weight_in, weight_mid, weight_top, weight_out.reshape(1, hidden), biases,
    ])
    source, coupling, _, _, production, features, weight_in, weight_mid, weight_top, wout, biases = loaded[:11]
    inverse, *row_slabs = loaded[11:]
    row_halos = swaps(*row_slabs, "gx")
    prepared = prepare(weight_in, weight_mid, weight_top, wout, biases)
    half = rows // 32 * 16
    acts_a, beta_a = forward(features, prepared, 0, half)
    *row_halos, beta_a = lax.optimization_barrier((*row_halos, beta_a))
    col_halos = swaps(*col_slabs(source, coupling, inverse, row_halos), "gy")
    acts_b, beta_b = forward(features, prepared, half, rows - half)
    adj, sens, beta = sweeps(
        source, coupling, inverse, production, (beta_a, beta_b), (*row_halos, *col_halos), mixing
    )
    packed, adjoint, beta = backward(num_feat, adj, beta, sens, weight_mid, weight_top, prepared[3], (acts_a, acts_b))
    grad_in, grad_mid, grad_top, grad_out, grad_bias = clip_all(parts_of_sum(packed), num_feat, hidden)
    return (adjoint, beta, grad_in, grad_mid, grad_top, grad_out.reshape(hidden), grad_bias)


def solution(mesh):
    cells3 = P(None, ("case", "gx"), "gy")
    cells2 = P(("case", "gx"), "gy")
    return jax.shard_map(
        shards,
        mesh=mesh,
        in_specs=(cells3,) * 3 + (cells2,) * 3 + (P(),) * 6,
        out_specs=(cells3, cells2, P("case"), P("case"), P("case"), P("case"), P("case")),
        check_vma=False,
    )
```

```python
import functools

import jax
import jax.numpy as jnp
from jax import lax
from jax.experimental import pallas as pl
from jax.experimental.pallas import tpu as pltpu
from jax.sharding import PartitionSpec as P

SWEEPS = 6
WALL_EXTRA = 0.2
FAR_EXTRA = 0.6
REG_WEIGHT = 0.5
CLIP_NORM = 64.0
EDGE = 8
SUB, LANE = 8, 128
F32, BF16 = jnp.float32, jnp.bfloat16
NT = (((1,), (1,)), ((), ()))
TN = (((0,), (0,)), ((), ()))
VMEM_BYTES = 16 * 1024 * 1024


def whole(shape):
    return pl.BlockSpec(shape, lambda *_: (0,) * len(shape))


def in_hbm(x):
    return pltpu.with_memory_space_constraint(x, pltpu.HBM)


def on_chip(kernel, operands, outs, scratch=(), far=(), far_outs=(), **kwargs):
    here, there = pl.BlockSpec(memory_space=pltpu.VMEM), pl.BlockSpec(memory_space=pltpu.HBM)
    return pl.pallas_call(
        kernel,
        in_specs=[here] * len(operands) + [there] * len(far),
        out_specs=[here] * len(outs) + [there] * len(far_outs),
        out_shape=[pltpu.VMEM(*o) for o in outs] + [pltpu.HBM(*o) for o in far_outs],
        scratch_shapes=list(scratch),
        compiler_params=params(),
        **kwargs,
    )(*operands, *[in_hbm(x) for x in far])


def like(x):
    return (x.shape, x.dtype)


def params():
    return pltpu.CompilerParams(vmem_limit_bytes=VMEM_BYTES)


def inverse_diag(diag, code):
    total = diag + jnp.where(code == 1, WALL_EXTRA, 0.0) + jnp.where(code == 2, FAR_EXTRA, 0.0)
    return 1.0 / total


def is_odd(axis):
    return lax.axis_index(axis) % 2 == 1


def load_kernel(count, *refs):
    far, near = refs[:count], refs[count : 2 * count]
    inv, first, second, sems = refs[2 * count :]
    copies = [pltpu.make_async_copy(far[k], near[k], sems.at[k]) for k in range(count)]
    for copy in copies:
        copy.start()
    src, cpl, dia, bc = near[:4]
    for copy in copies[:4]:
        copy.wait()
    nv, rows, _ = src.shape
    nc = cpl.shape[0]
    inv[...] = inverse_diag(dia[...], bc[...])
    odd = is_odd("gx")
    for f in range(nv + nc + 1):
        if f < nv + nc:
            ref, k = (src, f) if f < nv else (cpl, f - nv)
            top, bottom = ref[k, 0:16].astype(F32)[:EDGE], ref[k, rows - 16 :].astype(F32)[16 - EDGE :]
        else:
            top, bottom = inv[0:EDGE], inv[rows - EDGE :]
        first[f] = jnp.where(odd, top, bottom)
        second[f] = jnp.where(odd, bottom, top)
    for copy in copies[4:]:
        copy.wait()


def load(arrays):
    source, coupling = arrays[:2]
    nv, rows, cols = source.shape
    slab = ((nv + coupling.shape[0] + 1, EDGE, cols), F32)
    return on_chip(
        functools.partial(load_kernel, len(arrays)),
        [],
        [like(x) for x in arrays] + [((rows, cols), F32), slab, slab],
        [pltpu.SemaphoreType.DMA((len(arrays),))],
        far=arrays,
        name="load",
    )


def ordered(axis, first, second):
    odd, at = is_odd(axis), lax.axis_index(axis)
    before, after = jnp.where(odd, first, second), jnp.where(odd, second, first)
    return jnp.where(at == 0, 0.0, before), jnp.where(at == lax.axis_size(axis) - 1, 0.0, after)


def cols_kernel(src, cpl, inv, row_first, row_second, col_first, col_second):
    nv, rows, cols = src.shape
    nc = cpl.shape[0]
    lane = lax.broadcasted_iota(jnp.int32, (rows, LANE), 1) // EDGE
    lane_h = lane[:EDGE]
    slabs = []
    for window, extra in ((slice(0, LANE), 0), (slice(cols - LANE, cols), EDGE)):
        mid = jnp.zeros((rows, LANE), F32)
        up = jnp.zeros((EDGE, LANE), F32)
        down = jnp.zeros((EDGE, LANE), F32)
        for f in range(nv + nc + 1):
            if f < nv:
                x = src[f, :, window].astype(F32)
            elif f < nv + nc:
                x = cpl[f - nv, :, window].astype(F32)
            else:
                x = inv[:, window]
            shift = (EDGE * f + extra) % LANE
            mid = jnp.where(lane == f, pltpu.roll(x, shift, 1), mid)
            north, south = ordered("gx", row_first[f, :, window], row_second[f, :, window])
            up = jnp.where(lane_h == f, pltpu.roll(north, shift, 1), up)
            down = jnp.where(lane_h == f, pltpu.roll(south, shift, 1), down)
        slabs.append(jnp.concatenate([up, mid, down], axis=0))
    odd = is_odd("gy")
    col_first[...] = jnp.where(odd, slabs[0], slabs[1])
    col_second[...] = jnp.where(odd, slabs[1], slabs[0])


def col_slabs(source, coupling, inv, row_halos):
    slab = ((source.shape[1] + 2 * EDGE, LANE), F32)
    return on_chip(cols_kernel, [source, coupling, inv, *row_halos], [slab, slab], name="col_slabs")


def column_of(row):
    hidden = row.shape[1]
    wide = jnp.concatenate([row, jnp.zeros((1, LANE - hidden), F32)], axis=1)
    return jnp.transpose(jnp.broadcast_to(wide, (LANE, LANE)))[:hidden]


def across(block, width):
    return jnp.concatenate([block] * (width // LANE), axis=1)


def weights_kernel(win, wmid, wtop, wout, bias, w1, w2, w3, cst):
    nf, hidden = win.shape
    step_rows, blk = hidden + 16, 16
    depth = w1.shape[1]
    feat_of = lax.broadcasted_iota(jnp.int32, (nf, depth), 1) // blk
    pick = (feat_of == lax.broadcasted_iota(jnp.int32, (nf, depth), 0)).astype(F32).astype(BF16)
    spread = lax.dot_general(win[...], pick, TN, preferred_element_type=F32)
    col = lax.broadcasted_iota(jnp.int32, (hidden, depth), 1)
    col_f = lax.broadcasted_iota(jnp.int32, (16, depth), 1)
    row_f = lax.broadcasted_iota(jnp.int32, (16, depth), 0)
    for r in range(blk):
        base = r * step_rows
        w1[base : base + hidden] = jnp.where(col % blk == r, spread, 0.0).astype(BF16)
        same = jnp.logical_and(col_f == row_f * blk + r, row_f < nf)
        w1[base + hidden : base + step_rows] = jnp.where(same, 1.0, 0.0).astype(BF16)
    w2[...] = jnp.transpose(wmid[...].astype(F32)).astype(BF16)
    w3[...] = jnp.transpose(wtop[...].astype(F32)).astype(BF16)
    for k in range(3):
        cst[k] = column_of(bias[k : k + 1, :])
    cst[3] = column_of(wout[...])


def prepare(weight_in, weight_mid, weight_top, weight_out, biases):
    nf, hidden = weight_in.shape
    depth = -(-nf * 16 // LANE) * LANE
    return on_chip(
        weights_kernel,
        [weight_in, weight_mid, weight_top, weight_out, biases],
        [
            ((16 * (hidden + 16), depth), BF16),
            ((hidden, hidden), BF16),
            ((hidden, hidden), BF16),
            ((4, hidden, LANE), F32),
        ],
        name="weights",
    )


def slope(act):
    return 1.0 - act * act


def forward_kernel(first_row, feat, w1, w2, w3, cst, acts, slopes, beta, x1):
    nf, _, cols = feat.shape
    hidden = w2.shape[0]
    step_rows, blk, per = hidden + 16, 16, 4
    x1[...] = jnp.zeros(x1.shape, BF16)

    @pl.loop(0, acts.shape[0] // blk)
    def _(block):
        start = pl.multiple_of(block * blk, blk)
        x1[0 : nf * blk] = feat[:, pl.ds(first_row + start, blk), :].reshape(nf * blk, cols)
        b1, b2, b3, wo = (across(cst[k], cols) for k in range(4))
        lines = []
        first = jnp.dot(w1[...], x1[...], preferred_element_type=F32)
        for g in range(blk // per):
            ones = []
            for q in range(g * per, (g + 1) * per):
                part = first[q * step_rows : (q + 1) * step_rows]
                one = jnp.tanh(part[:hidden] + b1).astype(BF16)
                slopes[start + q, 0:hidden] = slope(one.astype(F32))
                acts[start + q, 0:hidden] = one
                acts[start + q, 2 * hidden : 2 * hidden + 16] = part[hidden:].astype(BF16)
                ones.append(one)
            second = jnp.dot(w2[...], jnp.concatenate(ones, axis=1), preferred_element_type=F32)
            twos = []
            for q in range(per):
                two = jnp.tanh(second[:, q * cols : (q + 1) * cols] + b2).astype(BF16)
                slopes[start + (g * per + q), hidden : 2 * hidden] = slope(two.astype(F32))
                acts[start + (g * per + q), hidden : 2 * hidden] = two
                twos.append(two)
            third = jnp.dot(w3[...], jnp.concatenate(twos, axis=1), preferred_element_type=F32)
            for q in range(per):
                three = jnp.tanh(third[:, q * cols : (q + 1) * cols] + b3).astype(BF16)
                acts[start + (g * per + q), 2 * hidden + 16 :] = three
                three = three.astype(F32)
                slopes[start + (g * per + q), 2 * hidden :] = wo * slope(three)
                lines.append(1.0 + jnp.sum(three * wo, axis=0, keepdims=True))
        beta[pl.ds(start, blk), :] = jnp.concatenate(lines, axis=0)


def forward(features, prepared, first_row, count):
    nf, _, cols = features.shape
    w1, w2 = prepared[:2]
    hidden = w2.shape[0]
    high = 3 * hidden + 16
    return on_chip(
        functools.partial(forward_kernel, first_row),
        [features, *prepared],
        [((count, high, cols), BF16), ((count, 3 * hidden, cols), F32), ((count, cols), F32)],
        [pltpu.VMEM((w1.shape[1], cols), BF16)],
        cost_estimate=pl.CostEstimate(
            flops=2 * count * cols * (nf + 2 * hidden) * hidden,
            bytes_accessed=2 * count * cols * (high + nf),
            transcendentals=3 * count * cols * hidden,
        ),
        name="network_forward",
    )


def tile_at(ref, lead, t, k):
    return ref[lead + (slice(t * SUB, (t + 1) * SUB), slice(k * LANE, (k + 1) * LANE))]


class Shifts:
    def __init__(self, tiles, lanes):
        self.tiles, self.lanes = tiles, lanes
        sub = lax.broadcasted_iota(jnp.int32, (SUB, LANE), 0)
        lane = lax.broadcasted_iota(jnp.int32, (SUB, LANE), 1)
        self.first_sub, self.last_sub = sub == 0, sub == SUB - 1
        self.first_lane, self.last_lane = lane == 0, lane == LANE - 1

    def above(self, ref, lead, t, k):
        here, other = tile_at(ref, lead, t, k), tile_at(ref, lead, max(t - 1, 0), k)
        return pltpu.roll(jnp.where(self.last_sub, other, here), 1, 0)

    def below(self, ref, lead, t, k):
        here, other = tile_at(ref, lead, t, k), tile_at(ref, lead, min(t + 1, self.tiles - 1), k)
        return pltpu.roll(jnp.where(self.first_sub, other, here), SUB - 1, 0)

    def left(self, ref, lead, t, k):
        here, other = tile_at(ref, lead, t, k), tile_at(ref, lead, t, (k - 1) % self.lanes)
        return pltpu.roll(jnp.where(self.last_lane, other, here), 1, 1)

    def right(self, ref, lead, t, k):
        here, other = tile_at(ref, lead, t, k), tile_at(ref, lead, t, (k + 1) % self.lanes)
        return pltpu.roll(jnp.where(self.first_lane, other, here), LANE - 1, 1)


def sweep_kernel(
    src, cpl, inverse, prod, beta_a, beta_b, row_first, row_second, col_first, col_second, mix,
    adj_out, sens, beta,
    raw, src_x, cpl_x, adj_a, adj_b,
):
    nv, rows, cols = src.shape
    nc = cpl.shape[0]
    tall = rows + 2 * EDGE
    tiles, lanes = tall // SUB, cols // LANE + 1
    shifts = Shifts(tiles, lanes)
    inner = slice(EDGE, EDGE + rows)
    lane = lax.broadcasted_iota(jnp.int32, (tall, LANE), 1)
    from_east, from_west = lane < EDGE, lane >= LANE - EDGE
    west, east = ordered("gy", col_first[...], col_second[...])
    for f in range(nv + nc + 1):
        if f < nv:
            raw[f, inner, 0:cols] = src[f].astype(F32)
        elif f < nv + nc:
            raw[f, inner, 0:cols] = cpl[f - nv].astype(F32)
        else:
            raw[f, inner, 0:cols] = inverse[...]
        north, south = ordered("gx", row_first[f], row_second[f])
        raw[f, 0:EDGE, 0:cols] = north
        raw[f, EDGE + rows :, 0:cols] = south
        e = pltpu.roll(east, (LANE - EDGE * f) % LANE, 1)
        w = pltpu.roll(west, (LANE - EDGE - EDGE * f) % LANE, 1)
        raw[f, :, cols:] = jnp.where(from_east, e, jnp.where(from_west, w, 0.0))

    moves = (shifts.above, shifts.below, shifts.left, shifts.right)
    for t in range(tiles):
        for k in range(lanes):
            at = (slice(t * SUB, (t + 1) * SUB), slice(k * LANE, (k + 1) * LANE))
            inv = tile_at(raw, (nv + nc,), t, k)
            for v in range(nv):
                src_x[(v,) + at] = inv * tile_at(raw, (v,), t, k)
            for d in range(nc):
                cpl_x[(d,) + at] = inv * moves[d](raw, (nv + d,), t, k)

    def sweep(old, new, last):
        for t in range(1, tiles - 1) if last else range(tiles):
            for k in range(lanes - 1) if last else range(lanes):
                at = (slice(t * SUB, (t + 1) * SUB), slice(k * LANE, (k + 1) * LANE))
                couple = [cpl_x[(d,) + at] for d in range(nc)]
                total = [src_x[(a,) + at] for a in range(nv)]
                for b in range(nv):
                    inc = couple[0] * moves[0](old, (b,), t, k)
                    for d in range(1, nc):
                        inc = inc + couple[d] * moves[d](old, (b,), t, k)
                    total = [total[a] + mix[b, a] * inc for a in range(nv)]
                if last:
                    at = (slice((t - 1) * SUB, t * SUB), at[1])
                for a in range(nv):
                    new[(a,) + at] = total[a]

    sweep(src_x, adj_a, False)

    @pl.loop(0, (SWEEPS - 2) // 2)
    def _(i):
        sweep(adj_a, adj_b, False)
        sweep(adj_b, adj_a, False)

    sweep(adj_a, adj_out, True)
    half = beta_a.shape[0]
    beta[0:half] = beta_a[...]
    beta[half:] = beta_b[...]
    sens[...] = adj_out[nv - 1] * prod[...] + REG_WEIGHT * (beta[...] - 1.0)


def sweeps(source, coupling, inverse, production, betas, halos, mixing):
    nv, rows, cols = source.shape
    nc = coupling.shape[0]
    tall, wide = rows + 2 * EDGE, cols + LANE
    near = pl.BlockSpec(memory_space=pltpu.VMEM)
    operands = [source, coupling, inverse, production, *betas, *halos]
    flat = ((rows, cols), F32)
    return pl.pallas_call(
        sweep_kernel,
        in_specs=[near] * len(operands) + [pl.BlockSpec(memory_space=pltpu.SMEM)],
        out_specs=[near] * 3,
        out_shape=[pltpu.VMEM((nv, rows, cols), F32), pltpu.VMEM(*flat), pltpu.VMEM(*flat)],
        scratch_shapes=[
            pltpu.VMEM((nv + nc + 1, tall, wide), F32),
            pltpu.VMEM((nv, tall, wide), F32),
            pltpu.VMEM((nc, tall, wide), F32),
            pltpu.VMEM((nv, tall, wide), F32),
            pltpu.VMEM((nv, tall, wide), F32),
        ],
        compiler_params=params(),
        name="sweeps",
    )(*operands, mixing)


def backward_kernel(
    num_feat, adj, beta, sens, wmid, wtop, acts_a, slopes_a, acts_b, slopes_b,
    packed, adj_out, beta_out,
    sums, g_mid, g_top, g_in, sems,
):
    out_copies = [
        pltpu.make_async_copy(adj, adj_out, sems.at[0]),
        pltpu.make_async_copy(beta, beta_out, sems.at[1]),
    ]
    for copy in out_copies:
        copy.start()
    blk, cols = 8, sens.shape[1]
    hidden = wmid.shape[0]
    sums[...] = jnp.zeros(sums.shape, F32)
    g_mid[...] = jnp.zeros(g_mid.shape, F32)
    g_top[...] = jnp.zeros(g_top.shape, F32)
    g_in[...] = jnp.zeros(g_in.shape, F32)

    def fold(x):
        parts = [x[:, k * LANE : (k + 1) * LANE] for k in range(cols // LANE)]
        return functools.reduce(jnp.add, parts)

    def joined(xs):
        return jnp.concatenate(xs, axis=1)

    def outer(x, d):
        return lax.dot_general(x, d, NT, preferred_element_type=F32)

    def block(acts, slopes, start, first_row):
        rows_sens = sens[pl.ds(pl.multiple_of(first_row + start, blk), blk), :]

        def layer(lo, high):
            return joined([acts[start + q, lo:high] for q in range(blk)])

        def behind(weight, delta, lo):
            raw = jnp.dot(weight, delta, preferred_element_type=F32)
            total, out = jnp.zeros((hidden, LANE), F32), []
            for q in range(blk):
                d = raw[:, q * cols : (q + 1) * cols] * slopes[start + q, lo : lo + hidden]
                total = total + fold(d)
                out.append(d.astype(BF16))
            return joined(out), total

        out_sum, top_sum, d3 = jnp.zeros((hidden, LANE), F32), jnp.zeros((hidden, LANE), F32), []
        for q in range(blk):
            act = acts[start + q, 2 * hidden + 16 :].astype(F32)
            sen = jnp.broadcast_to(rows_sens[q : q + 1], (hidden, cols))
            out_sum = out_sum + fold(act * sen)
            d = sen * slopes[start + q, 2 * hidden :]
            top_sum = top_sum + fold(d)
            d3.append(d.astype(BF16))
        d3 = joined(d3)
        d2, mid_sum = behind(wtop[...], d3, hidden)
        g_top[...] += outer(layer(hidden, 2 * hidden), d3)
        d1, in_sum = behind(wmid[...], d2, 0)
        g_mid[...] += outer(layer(0, hidden), d2)
        g_in[...] += outer(d1, layer(2 * hidden, 2 * hidden + 16))
        for k, part in enumerate((out_sum, in_sum, mid_sum, top_sum)):
            sums[k] += part

    half = acts_a.shape[0]
    for acts, slopes, first_row in ((acts_a, slopes_a, 0), (acts_b, slopes_b, half)):

        @pl.loop(0, acts.shape[0] // blk)
        def _(i, acts=acts, slopes=slopes, first_row=first_row):
            block(acts, slopes, pl.multiple_of(i * blk, blk), first_row)

    packed[0:hidden, :] = joined([g_mid[...], g_top[...]])
    turned = jnp.transpose(joined([g_in[...], jnp.zeros((hidden, LANE - 16), F32)]))
    tail = turned[SUB : 2 * SUB]
    row = lax.broadcasted_iota(jnp.int32, (SUB, hidden), 0)
    for k in range(4):
        line = jnp.sum(jnp.transpose(sums[k]), axis=0, keepdims=True)
        tail = tail + jnp.where(row == k + num_feat - SUB, jnp.broadcast_to(line, (SUB, hidden)), 0.0)
    packed[hidden : hidden + SUB, :] = joined([turned[0:SUB], tail])
    for copy in out_copies:
        copy.wait()


def backward(num_feat, adj, beta, sens, weight_mid, weight_top, nets):
    hidden = weight_mid.shape[0]
    return on_chip(
        functools.partial(backward_kernel, num_feat),
        [adj, beta, sens, weight_mid, weight_top, *nets],
        [((hidden + SUB, LANE), F32)],
        [
            pltpu.VMEM((4, hidden, LANE), F32),
            pltpu.VMEM((hidden, hidden), F32),
            pltpu.VMEM((hidden, hidden), F32),
            pltpu.VMEM((hidden, 16), F32),
            pltpu.SemaphoreType.DMA((2,)),
        ],
        far_outs=[like(adj), like(beta)],
        name="backward",
    )


def clip_kernel(summed, gin, gmid, gtop, gout, gbias):
    hidden = gmid.shape[0]
    total = summed[...]
    squares = jnp.sum(jnp.sum(total * total, axis=0, keepdims=True), axis=1, keepdims=True)
    total = total * (CLIP_NORM / jnp.maximum(jnp.sqrt(squares), CLIP_NORM))
    gmid[...] = total[:hidden, :hidden]
    gtop[...] = total[:hidden, hidden:]
    low, high = total[hidden:, :hidden], total[hidden:, hidden:]
    gin[0:SUB] = low
    gin[SUB:] = high[: gin.shape[0] - SUB]
    at = gin.shape[0] - SUB
    gout[...] = high[at : at + 1]
    gbias[...] = high[at + 1 : at + 4]


def clip_all(summed, num_feat, hidden):
    shapes = [(num_feat, hidden), (hidden, hidden), (hidden, hidden), (1, hidden), (3, hidden)]
    return pl.pallas_call(
        clip_kernel,
        grid=(1,),
        in_specs=[whole(summed.shape)],
        out_specs=[whole(s) for s in shapes],
        out_shape=[jax.ShapeDtypeStruct(s, F32) for s in shapes],
        compiler_params=params(),
        name="clip",
    )(summed)


def sum_over_case(packed):
    for axis, radix in (("gy", 2), ("gx", 4)):
        count = lax.axis_size(axis)
        step = 1
        while step < count:
            parts = [packed]
            for k in range(1, min(radix, count // step)):
                parts.append(lax.ppermute(packed, axis, [(i, i ^ (k * step)) for i in range(count)]))
            while len(parts) > 1:
                parts = [a + b for a, b in zip(parts[::2], parts[1::2])]
            packed = parts[0]
            step *= radix
    return packed


def swaps(first, second, axis):
    count = lax.axis_size(axis)

    def pairs(start):
        low = [(i, i + 1) for i in range(start, count - 1, 2)]
        if count % 2 == 0 and start == 1:
            low.append((0, count - 1))
        return low + [(b, a) for a, b in low]

    return lax.ppermute(first, axis, pairs(0)), lax.ppermute(second, axis, pairs(1))


def shards(
    features, source, coupling, diagonal, production, bc_code, mixing,
    weight_in, weight_mid, weight_top, weight_out, biases,
):
    num_feat, rows, _ = features.shape
    hidden = weight_mid.shape[0]
    loaded = load([
        source, coupling, diagonal, bc_code, production, features,
        weight_in, weight_mid, weight_top, weight_out.reshape(1, hidden), biases,
    ])
    source, coupling, _, _, production, features, weight_in, weight_mid, weight_top, wout, biases = loaded[:11]
    inverse, *row_slabs = loaded[11:]
    row_halos = swaps(*row_slabs, "gx")
    prepared = prepare(weight_in, weight_mid, weight_top, wout, biases)
    half = rows // 32 * 16
    *net_a, beta_a = forward(features, prepared, 0, half)
    *row_halos, beta_a = lax.optimization_barrier((*row_halos, beta_a))
    col_halos = swaps(*col_slabs(source, coupling, inverse, row_halos), "gy")
    *net_b, beta_b = forward(features, prepared, half, rows - half)
    adj, sens, beta = sweeps(
        source, coupling, inverse, production, (beta_a, beta_b), (*row_halos, *col_halos), mixing
    )
    packed, adjoint, beta = backward(num_feat, adj, beta, sens, weight_mid, weight_top, (*net_a, *net_b))
    grad_in, grad_mid, grad_top, grad_out, grad_bias = clip_all(sum_over_case(packed), num_feat, hidden)
    return (adjoint, beta, grad_in, grad_mid, grad_top, grad_out.reshape(hidden), grad_bias)


def solution(mesh):
    cells3 = P(None, ("case", "gx"), "gy")
    cells2 = P(("case", "gx"), "gy")
    return jax.shard_map(
        shards,
        mesh=mesh,
        in_specs=(cells3,) * 3 + (cells2,) * 3 + (P(),) * 6,
        out_specs=(cells3, cells2, P("case"), P("case"), P("case"), P("case"), P("case")),
        check_vma=False,
    )
```

```python
import functools

import jax
import jax.numpy as jnp
from jax import lax
from jax.experimental import pallas as pl
from jax.experimental.pallas import tpu as pltpu
from jax.sharding import PartitionSpec as P

SWEEPS = 6
WALL_EXTRA = 0.2
FAR_EXTRA = 0.6
REG_WEIGHT = 0.5
CLIP_NORM = 64.0
EDGE = 8
SUB, LANE = 8, 128
F32, BF16 = jnp.float32, jnp.bfloat16
NT = (((1,), (1,)), ((), ()))
TN = (((0,), (0,)), ((), ()))
VMEM_BYTES = 16 * 1024 * 1024


def whole(shape):
    return pl.BlockSpec(shape, lambda *_: (0,) * len(shape))


def in_hbm(x):
    return pltpu.with_memory_space_constraint(x, pltpu.HBM)


def on_chip(kernel, operands, outs, scratch=(), far=(), far_outs=(), **kwargs):
    here, there = pl.BlockSpec(memory_space=pltpu.VMEM), pl.BlockSpec(memory_space=pltpu.HBM)
    return pl.pallas_call(
        kernel,
        in_specs=[here] * len(operands) + [there] * len(far),
        out_specs=[here] * len(outs) + [there] * len(far_outs),
        out_shape=[pltpu.VMEM(*o) for o in outs] + [pltpu.HBM(*o) for o in far_outs],
        scratch_shapes=list(scratch),
        compiler_params=params(),
        **kwargs,
    )(*operands, *[in_hbm(x) for x in far])


def like(x):
    return (x.shape, x.dtype)


def params():
    return pltpu.CompilerParams(vmem_limit_bytes=VMEM_BYTES)


def inverse_diag(diag, code):
    total = diag + jnp.where(code == 1, WALL_EXTRA, 0.0) + jnp.where(code == 2, FAR_EXTRA, 0.0)
    return 1.0 / total


def is_odd(axis):
    return lax.axis_index(axis) % 2 == 1


def load_kernel(count, *refs):
    far, near = refs[:count], refs[count : 2 * count]
    inv, first, second, sems = refs[2 * count :]
    copies = [pltpu.make_async_copy(far[k], near[k], sems.at[k]) for k in range(count)]
    for copy in copies:
        copy.start()
    src, cpl, dia, bc = near[:4]
    for copy in copies[:4]:
        copy.wait()
    nv, rows, _ = src.shape
    nc = cpl.shape[0]
    inv[...] = inverse_diag(dia[...], bc[...])
    odd = is_odd("gx")
    for f in range(nv + nc + 1):
        if f < nv + nc:
            ref, k = (src, f) if f < nv else (cpl, f - nv)
            top, bottom = ref[k, 0:16].astype(F32)[:EDGE], ref[k, rows - 16 :].astype(F32)[16 - EDGE :]
        else:
            top, bottom = inv[0:EDGE], inv[rows - EDGE :]
        first[f] = jnp.where(odd, top, bottom)
        second[f] = jnp.where(odd, bottom, top)
    for copy in copies[4:]:
        copy.wait()


def load(arrays):
    source, coupling = arrays[:2]
    nv, rows, cols = source.shape
    slab = ((nv + coupling.shape[0] + 1, EDGE, cols), F32)
    return on_chip(
        functools.partial(load_kernel, len(arrays)),
        [],
        [like(x) for x in arrays] + [((rows, cols), F32), slab, slab],
        [pltpu.SemaphoreType.DMA((len(arrays),))],
        far=arrays,
        name="load",
    )


def ordered(axis, first, second):
    odd, at = is_odd(axis), lax.axis_index(axis)
    before, after = jnp.where(odd, first, second), jnp.where(odd, second, first)
    return jnp.where(at == 0, 0.0, before), jnp.where(at == lax.axis_size(axis) - 1, 0.0, after)


def cols_kernel(src, cpl, inv, row_first, row_second, col_first, col_second):
    nv, rows, cols = src.shape
    nc = cpl.shape[0]
    lane = lax.broadcasted_iota(jnp.int32, (rows, LANE), 1) // EDGE
    lane_h = lane[:EDGE]
    slabs = []
    for window, extra in ((slice(0, LANE), 0), (slice(cols - LANE, cols), EDGE)):
        mid = jnp.zeros((rows, LANE), F32)
        up = jnp.zeros((EDGE, LANE), F32)
        down = jnp.zeros((EDGE, LANE), F32)
        for f in range(nv + nc + 1):
            if f < nv:
                x = src[f, :, window].astype(F32)
            elif f < nv + nc:
                x = cpl[f - nv, :, window].astype(F32)
            else:
                x = inv[:, window]
            shift = (EDGE * f + extra) % LANE
            mid = jnp.where(lane == f, pltpu.roll(x, shift, 1), mid)
            north, south = ordered("gx", row_first[f, :, window], row_second[f, :, window])
            up = jnp.where(lane_h == f, pltpu.roll(north, shift, 1), up)
            down = jnp.where(lane_h == f, pltpu.roll(south, shift, 1), down)
        slabs.append(jnp.concatenate([up, mid, down], axis=0))
    odd = is_odd("gy")
    col_first[...] = jnp.where(odd, slabs[0], slabs[1])
    col_second[...] = jnp.where(odd, slabs[1], slabs[0])


def col_slabs(source, coupling, inv, row_halos):
    slab = ((source.shape[1] + 2 * EDGE, LANE), F32)
    return on_chip(cols_kernel, [source, coupling, inv, *row_halos], [slab, slab], name="col_slabs")


def column_of(row):
    hidden = row.shape[1]
    wide = jnp.concatenate([row, jnp.zeros((1, LANE - hidden), F32)], axis=1)
    return jnp.transpose(jnp.broadcast_to(wide, (LANE, LANE)))[:hidden]


def across(block, width):
    return jnp.concatenate([block] * (width // LANE), axis=1)


def weights_kernel(win, wmid, wtop, wout, bias, w1, w2, w3, cst):
    nf, hidden = win.shape
    step_rows, blk = hidden + 16, 16
    depth = w1.shape[1]
    feat_of = lax.broadcasted_iota(jnp.int32, (nf, depth), 1) // blk
    pick = (feat_of == lax.broadcasted_iota(jnp.int32, (nf, depth), 0)).astype(F32).astype(BF16)
    spread = lax.dot_general(win[...], pick, TN, preferred_element_type=F32)
    col = lax.broadcasted_iota(jnp.int32, (hidden, depth), 1)
    col_f = lax.broadcasted_iota(jnp.int32, (16, depth), 1)
    row_f = lax.broadcasted_iota(jnp.int32, (16, depth), 0)
    for r in range(blk):
        base = r * step_rows
        w1[base : base + hidden] = jnp.where(col % blk == r, spread, 0.0).astype(BF16)
        same = jnp.logical_and(col_f == row_f * blk + r, row_f < nf)
        w1[base + hidden : base + step_rows] = jnp.where(same, 1.0, 0.0).astype(BF16)
    w2[...] = jnp.transpose(wmid[...].astype(F32)).astype(BF16)
    w3[...] = jnp.transpose(wtop[...].astype(F32)).astype(BF16)
    for k in range(3):
        cst[k] = column_of(bias[k : k + 1, :])
    cst[3] = column_of(wout[...])


def prepare(weight_in, weight_mid, weight_top, weight_out, biases):
    nf, hidden = weight_in.shape
    depth = -(-nf * 16 // LANE) * LANE
    return on_chip(
        weights_kernel,
        [weight_in, weight_mid, weight_top, weight_out, biases],
        [
            ((16 * (hidden + 16), depth), BF16),
            ((hidden, hidden), BF16),
            ((hidden, hidden), BF16),
            ((4, hidden, LANE), F32),
        ],
        name="weights",
    )


def slope(act):
    return 1.0 - act * act


def forward_kernel(first_row, feat, w1, w2, w3, cst, acts, slopes, beta, x1):
    nf, _, cols = feat.shape
    hidden = w2.shape[0]
    step_rows, blk, per = hidden + 16, 16, 4
    x1[...] = jnp.zeros(x1.shape, BF16)

    @pl.loop(0, acts.shape[0] // blk)
    def _(block):
        start = pl.multiple_of(block * blk, blk)
        x1[0 : nf * blk] = feat[:, pl.ds(first_row + start, blk), :].reshape(nf * blk, cols)
        b1, b2, b3, wo = (across(cst[k], cols) for k in range(4))
        lines = []
        first = jnp.dot(w1[...], x1[...], preferred_element_type=F32)
        for g in range(blk // per):
            ones = []
            for q in range(g * per, (g + 1) * per):
                part = first[q * step_rows : (q + 1) * step_rows]
                one = jnp.tanh(part[:hidden] + b1).astype(BF16)
                slopes[start + q, 0:hidden] = slope(one.astype(F32))
                acts[start + q, 0:hidden] = one
                acts[start + q, 2 * hidden : 2 * hidden + 16] = part[hidden:].astype(BF16)
                ones.append(one)
            second = jnp.dot(w2[...], jnp.concatenate(ones, axis=1), preferred_element_type=F32)
            twos = []
            for q in range(per):
                two = jnp.tanh(second[:, q * cols : (q + 1) * cols] + b2).astype(BF16)
                slopes[start + (g * per + q), hidden : 2 * hidden] = slope(two.astype(F32))
                acts[start + (g * per + q), hidden : 2 * hidden] = two
                twos.append(two)
            third = jnp.dot(w3[...], jnp.concatenate(twos, axis=1), preferred_element_type=F32)
            for q in range(per):
                three = jnp.tanh(third[:, q * cols : (q + 1) * cols] + b3).astype(BF16)
                acts[start + (g * per + q), 2 * hidden + 16 :] = three
                three = three.astype(F32)
                slopes[start + (g * per + q), 2 * hidden :] = wo * slope(three)
                lines.append(1.0 + jnp.sum(three * wo, axis=0, keepdims=True))
        beta[pl.ds(start, blk), :] = jnp.concatenate(lines, axis=0)


def forward(features, prepared, first_row, count):
    nf, _, cols = features.shape
    w1, w2 = prepared[:2]
    hidden = w2.shape[0]
    high = 3 * hidden + 16
    return on_chip(
        functools.partial(forward_kernel, first_row),
        [features, *prepared],
        [((count, high, cols), BF16), ((count, 3 * hidden, cols), F32), ((count, cols), F32)],
        [pltpu.VMEM((w1.shape[1], cols), BF16)],
        cost_estimate=pl.CostEstimate(
            flops=2 * count * cols * (nf + 2 * hidden) * hidden,
            bytes_accessed=2 * count * cols * (high + nf),
            transcendentals=3 * count * cols * hidden,
        ),
        name="network_forward",
    )


def span(t, k):
    return (slice(t * SUB, (t + 1) * SUB), slice(k * LANE, (k + 1) * LANE))


class Shifts:
    def __init__(self, tiles, lanes):
        self.tiles, self.lanes = tiles, lanes
        sub = lax.broadcasted_iota(jnp.int32, (SUB, LANE), 0)
        lane = lax.broadcasted_iota(jnp.int32, (SUB, LANE), 1)
        self.first_sub, self.last_sub = sub == 0, sub == SUB - 1
        self.first_lane, self.last_lane = lane == 0, lane == LANE - 1
        self.all = (self.above, self.below, self.left, self.right)

    def above(self, ref, lead, t, k):
        here, other = ref[lead + span(t, k)], ref[lead + span(max(t - 1, 0), k)]
        return pltpu.roll(jnp.where(self.last_sub, other, here), 1, 0)

    def below(self, ref, lead, t, k):
        here, other = ref[lead + span(t, k)], ref[lead + span(min(t + 1, self.tiles - 1), k)]
        return pltpu.roll(jnp.where(self.first_sub, other, here), SUB - 1, 0)

    def left(self, ref, lead, t, k):
        here, other = ref[lead + span(t, k)], ref[lead + span(t, (k - 1) % self.lanes)]
        return pltpu.roll(jnp.where(self.last_lane, other, here), 1, 1)

    def right(self, ref, lead, t, k):
        here, other = ref[lead + span(t, k)], ref[lead + span(t, (k + 1) % self.lanes)]
        return pltpu.roll(jnp.where(self.first_lane, other, here), LANE - 1, 1)


def extend(src, cpl, inverse, row_halos, col_halos, shifts, raw, src_x, cpl_x):
    nv, rows, cols = src.shape
    nc = cpl.shape[0]
    tall = rows + 2 * EDGE
    inner = slice(EDGE, EDGE + rows)
    lane = lax.broadcasted_iota(jnp.int32, (tall, LANE), 1)
    from_east, from_west = lane < EDGE, lane >= LANE - EDGE
    west, east = ordered("gy", *(x[...] for x in col_halos))
    for f in range(nv + nc + 1):
        if f < nv:
            raw[f, inner, 0:cols] = src[f].astype(F32)
        elif f < nv + nc:
            raw[f, inner, 0:cols] = cpl[f - nv].astype(F32)
        else:
            raw[f, inner, 0:cols] = inverse[...]
        north, south = ordered("gx", *(x[f] for x in row_halos))
        raw[f, 0:EDGE, 0:cols] = north
        raw[f, EDGE + rows :, 0:cols] = south
        e = pltpu.roll(east, (LANE - EDGE * f) % LANE, 1)
        w = pltpu.roll(west, (LANE - EDGE - EDGE * f) % LANE, 1)
        raw[f, :, cols:] = jnp.where(from_east, e, jnp.where(from_west, w, 0.0))
    for t in range(shifts.tiles):
        for k in range(shifts.lanes):
            inv = raw[(nv + nc,) + span(t, k)]
            for v in range(nv):
                src_x[(v,) + span(t, k)] = inv * raw[(v,) + span(t, k)]
            for d in range(nc):
                cpl_x[(d,) + span(t, k)] = inv * shifts.all[d](raw, (nv + d,), t, k)


def adjoint_kernel(
    num_feat, src, cpl, inverse, prod, beta_a, beta_b, row_first, row_second, col_first, col_second,
    wmid, wtop, acts_a, slopes_a, acts_b, slopes_b, mix,
    packed, adj_out, beta_out,
    raw, src_x, cpl_x, adj, done, sums, g_mid, g_top, g_in, sems,
):
    nv, rows, cols = src.shape
    nc = cpl.shape[0]
    hidden, blk = wmid.shape[0], SUB
    half = beta_a.shape[0]
    tiles, lanes = (rows + 2 * EDGE) // SUB, cols // LANE + 1
    copies = [
        pltpu.make_async_copy(beta_a, beta_out.at[0:half], sems.at[0]),
        pltpu.make_async_copy(beta_b, beta_out.at[half:rows], sems.at[1]),
        pltpu.make_async_copy(done, adj_out, sems.at[2]),
    ]
    copies[0].start()
    copies[1].start()
    shifts = Shifts(tiles, lanes)
    extend(
        src, cpl, inverse, (row_first, row_second), (col_first, col_second), shifts, raw, src_x, cpl_x
    )

    def sweep(number, t):
        last = number == SWEEPS
        for k in range(lanes - 1 if last else lanes):
            couple = [cpl_x[(d,) + span(t, k)] for d in range(nc)]
            total = [src_x[(a,) + span(t, k)] for a in range(nv)]
            for b in range(nv):
                old, lead = (src_x, (b,)) if number == 1 else (adj, (number - 2, b))
                inc = couple[0] * shifts.all[0](old, lead, t, k)
                for d in range(1, nc):
                    inc = inc + couple[d] * shifts.all[d](old, lead, t, k)
                total = [total[a] + mix[b, a] * inc for a in range(nv)]
            for a in range(nv):
                if last:
                    done[(a,) + span(t - EDGE // SUB, k)] = total[a]
                else:
                    adj[(number - 1, a) + span(t, k)] = total[a]

    def fold(x):
        parts = [x[:, k * LANE : (k + 1) * LANE] for k in range(cols // LANE)]
        return functools.reduce(jnp.add, parts)

    def joined(xs):
        return jnp.concatenate(xs, axis=1)

    def outer(x, d):
        return lax.dot_general(x, d, NT, preferred_element_type=F32)

    def backward(first):
        if first < half:
            acts, slopes, beta, start = acts_a, slopes_a, beta_a, first
        else:
            acts, slopes, beta, start = acts_b, slopes_b, beta_b, first - half
        here = slice(first, first + blk)
        sens = done[nv - 1, here] * prod[here] + REG_WEIGHT * (beta[start : start + blk] - 1.0)

        def layer(lo, high):
            return joined([acts[start + q, lo:high] for q in range(blk)])

        def behind(weight, delta, lo):
            product = jnp.dot(weight, delta, preferred_element_type=F32)
            total, out = jnp.zeros((hidden, LANE), F32), []
            for q in range(blk):
                d = product[:, q * cols : (q + 1) * cols] * slopes[start + q, lo : lo + hidden]
                total = total + fold(d)
                out.append(d.astype(BF16))
            return joined(out), total

        out_sum, top_sum, d3 = jnp.zeros((hidden, LANE), F32), jnp.zeros((hidden, LANE), F32), []
        for q in range(blk):
            act = acts[start + q, 2 * hidden + 16 :].astype(F32)
            sen = jnp.broadcast_to(sens[q : q + 1], (hidden, cols))
            out_sum = out_sum + fold(act * sen)
            d = sen * slopes[start + q, 2 * hidden :]
            top_sum = top_sum + fold(d)
            d3.append(d.astype(BF16))
        d3 = joined(d3)
        d2, mid_sum = behind(wtop[...], d3, hidden)
        d1, in_sum = behind(wmid[...], d2, 0)
        new = (
            (g_top, outer(layer(hidden, 2 * hidden), d3)),
            (g_mid, outer(layer(0, hidden), d2)),
            (g_in, outer(d1, layer(2 * hidden, 2 * hidden + 16))),
            *((sums.at[k], part) for k, part in enumerate((out_sum, in_sum, mid_sum, top_sum))),
        )
        for ref, part in new:
            ref[...] = part if first == 0 else ref[...] + part

    for number in range(1, SWEEPS):
        for t in range(SWEEPS + 1 - number):
            sweep(number, t)
    for t in range(1, tiles - 1):
        for number in range(1, SWEEPS + 1):
            if t + SWEEPS - number < tiles:
                sweep(number, t + SWEEPS - number)
        if t > 1:
            backward((t - 2) * blk)
    copies[2].start()
    backward(rows - blk)

    packed[0:hidden, :] = joined([g_mid[...], g_top[...]])
    turned = jnp.transpose(joined([g_in[...], jnp.zeros((hidden, LANE - 16), F32)]))
    tail = turned[SUB : 2 * SUB]
    row = lax.broadcasted_iota(jnp.int32, (SUB, hidden), 0)
    for k in range(4):
        line = jnp.sum(jnp.transpose(sums[k]), axis=0, keepdims=True)
        tail = tail + jnp.where(row == k + num_feat - SUB, jnp.broadcast_to(line, (SUB, hidden)), 0.0)
    packed[hidden : hidden + SUB, :] = joined([turned[0:SUB], tail])
    for copy in copies:
        copy.wait()


def sweeps_and_backward(num_feat, source, coupling, inverse, production, betas, halos, weights, nets, mixing):
    nv, rows, cols = source.shape
    nc = coupling.shape[0]
    hidden = weights[0].shape[0]
    tall, wide = rows + 2 * EDGE, cols + LANE
    near, far = pl.BlockSpec(memory_space=pltpu.VMEM), pl.BlockSpec(memory_space=pltpu.HBM)
    operands = [source, coupling, inverse, production, *betas, *halos, *weights, *nets]
    return pl.pallas_call(
        functools.partial(adjoint_kernel, num_feat),
        in_specs=[near] * len(operands) + [pl.BlockSpec(memory_space=pltpu.SMEM)],
        out_specs=[near, far, far],
        out_shape=[
            pltpu.VMEM((hidden + SUB, LANE), F32),
            pltpu.HBM((nv, rows, cols), F32),
            pltpu.HBM((rows, cols), F32),
        ],
        scratch_shapes=[
            pltpu.VMEM((nv + nc + 1, tall, wide), F32),
            pltpu.VMEM((nv, tall, wide), F32),
            pltpu.VMEM((nc, tall, wide), F32),
            pltpu.VMEM((SWEEPS - 1, nv, tall, wide), F32),
            pltpu.VMEM((nv, rows, cols), F32),
            pltpu.VMEM((4, hidden, LANE), F32),
            pltpu.VMEM((hidden, hidden), F32),
            pltpu.VMEM((hidden, hidden), F32),
            pltpu.VMEM((hidden, 16), F32),
            pltpu.SemaphoreType.DMA((3,)),
        ],
        compiler_params=params(),
        name="sweeps_backward",
    )(*operands, mixing)


def clip_kernel(summed, gin, gmid, gtop, gout, gbias):
    hidden = gmid.shape[0]
    total = summed[...]
    squares = jnp.sum(jnp.sum(total * total, axis=0, keepdims=True), axis=1, keepdims=True)
    total = total * (CLIP_NORM / jnp.maximum(jnp.sqrt(squares), CLIP_NORM))
    gmid[...] = total[:hidden, :hidden]
    gtop[...] = total[:hidden, hidden:]
    low, high = total[hidden:, :hidden], total[hidden:, hidden:]
    gin[0:SUB] = low
    gin[SUB:] = high[: gin.shape[0] - SUB]
    at = gin.shape[0] - SUB
    gout[...] = high[at : at + 1]
    gbias[...] = high[at + 1 : at + 4]


def clip_all(summed, num_feat, hidden):
    shapes = [(num_feat, hidden), (hidden, hidden), (hidden, hidden), (1, hidden), (3, hidden)]
    return pl.pallas_call(
        clip_kernel,
        grid=(1,),
        in_specs=[whole(summed.shape)],
        out_specs=[whole(s) for s in shapes],
        out_shape=[jax.ShapeDtypeStruct(s, F32) for s in shapes],
        compiler_params=params(),
        name="clip",
    )(summed)


def sum_over_case(packed):
    for axis, radix in (("gy", 2), ("gx", 4)):
        count = lax.axis_size(axis)
        step = 1
        while step < count:
            parts = [packed]
            for k in range(1, min(radix, count // step)):
                parts.append(lax.ppermute(packed, axis, [(i, i ^ (k * step)) for i in range(count)]))
            while len(parts) > 1:
                parts = [a + b for a, b in zip(parts[::2], parts[1::2])]
            packed = parts[0]
            step *= radix
    return packed


def row_swaps(first, second):
    num_x, num_y = lax.axis_size("gx"), lax.axis_size("gy")
    out = []
    for start, slab in ((0, first), (1, second)):
        partner = {}
        for i in range(num_x):
            j = i + 1 if i % 2 == start else i - 1
            for y in range(num_y):
                if 0 <= j < num_x:
                    partner[i * num_y + y] = j * num_y + y
                elif num_y % 2 == 0:
                    partner[i * num_y + y] = i * num_y + (y ^ 1)
        out.append(lax.ppermute(slab, ("gx", "gy"), sorted(partner.items())))
    return out


def col_swaps(first, second):
    count = lax.axis_size("gy")
    out = []
    for start, slab in ((0, first), (1, second)):
        low = [(i, i + 1) for i in range(start, count - 1, 2)]
        if count % 2 == 0 and start == 1:
            low.append((0, count - 1))
        out.append(lax.ppermute(slab, "gy", low + [(b, a) for a, b in low]))
    return out


def shards(
    features, source, coupling, diagonal, production, bc_code, mixing,
    weight_in, weight_mid, weight_top, weight_out, biases,
):
    num_feat, rows, _ = features.shape
    hidden = weight_mid.shape[0]
    loaded = load([
        source, coupling, diagonal, bc_code, production, features,
        weight_in, weight_mid, weight_top, weight_out.reshape(1, hidden), biases,
    ])
    source, coupling, _, _, production, features, weight_in, weight_mid, weight_top, wout, biases = loaded[:11]
    inverse, *row_slabs = loaded[11:]
    row_halos = row_swaps(*row_slabs)
    prepared = prepare(weight_in, weight_mid, weight_top, wout, biases)
    half = rows - 32
    *net_a, beta_a = forward(features, prepared, 0, half)
    *row_halos, beta_a = lax.optimization_barrier((*row_halos, beta_a))
    col_halos = col_swaps(*col_slabs(source, coupling, inverse, row_halos))
    *net_b, beta_b = forward(features, prepared, half, rows - half)
    packed, adjoint, beta = sweeps_and_backward(
        num_feat, source, coupling, inverse, production, (beta_a, beta_b), (*row_halos, *col_halos),
        (weight_mid, weight_top), (*net_a, *net_b), mixing,
    )
    grad_in, grad_mid, grad_top, grad_out, grad_bias = clip_all(sum_over_case(packed), num_feat, hidden)
    return (adjoint, beta, grad_in, grad_mid, grad_top, grad_out.reshape(hidden), grad_bias)


def solution(mesh):
    cells3 = P(None, ("case", "gx"), "gy")
    cells2 = P(("case", "gx"), "gy")
    return jax.shard_map(
        shards,
        mesh=mesh,
        in_specs=(cells3,) * 3 + (cells2,) * 3 + (P(),) * 6,
        out_specs=(cells3, cells2, P("case"), P("case"), P("case"), P("case"), P("case")),
        check_vma=False,
    )
```

```python
import functools

import jax
import jax.numpy as jnp
from jax import lax
from jax.experimental import pallas as pl
from jax.experimental.pallas import tpu as pltpu
from jax.sharding import PartitionSpec as P

SWEEPS = 6
WALL_EXTRA = 0.2
FAR_EXTRA = 0.6
REG_WEIGHT = 0.5
CLIP_NORM = 64.0
DEPTH = SWEEPS
EDGE = 8
SUB, LANE = 8, 128
F32, BF16 = jnp.float32, jnp.bfloat16
NT = (((1,), (1,)), ((), ()))
TN = (((0,), (0,)), ((), ()))
VMEM_BYTES = 16 * 1024 * 1024


def whole(shape):
    return pl.BlockSpec(shape, lambda *_: (0,) * len(shape))


def in_hbm(x):
    return pltpu.with_memory_space_constraint(x, pltpu.HBM)


def on_chip(kernel, operands, outs, scratch=(), far=(), far_outs=(), **kwargs):
    here, there = pl.BlockSpec(memory_space=pltpu.VMEM), pl.BlockSpec(memory_space=pltpu.HBM)
    return pl.pallas_call(
        kernel,
        in_specs=[here] * len(operands) + [there] * len(far),
        out_specs=[here] * len(outs) + [there] * len(far_outs),
        out_shape=[pltpu.VMEM(*o) for o in outs] + [pltpu.HBM(*o) for o in far_outs],
        scratch_shapes=list(scratch),
        compiler_params=params(),
        **kwargs,
    )(*operands, *[in_hbm(x) for x in far])


def like(x):
    return (x.shape, x.dtype)


def params():
    return pltpu.CompilerParams(vmem_limit_bytes=VMEM_BYTES)


def inverse_diag(diag, code):
    total = diag + jnp.where(code == 1, WALL_EXTRA, 0.0) + jnp.where(code == 2, FAR_EXTRA, 0.0)
    return 1.0 / total


def is_odd(axis):
    return lax.axis_index(axis) % 2 == 1


def load_kernel(count, *refs):
    far, near = refs[:count], refs[count : 2 * count]
    inv, first, second, sems = refs[2 * count :]
    copies = [pltpu.make_async_copy(far[k], near[k], sems.at[k]) for k in range(count)]
    for copy in copies:
        copy.start()
    src, cpl, dia, bc = near[:4]
    for copy in copies[:4]:
        copy.wait()
    nv, rows, _ = src.shape
    nc = cpl.shape[0]
    inv[...] = inverse_diag(dia[...], bc[...])
    odd = is_odd("gx")
    for f in range(nv + nc + 1):
        if f < nv + nc:
            ref, k = (src, f) if f < nv else (cpl, f - nv)
            top, bottom = ref[k, 0:16].astype(F32)[:DEPTH], ref[k, rows - 16 :].astype(F32)[16 - DEPTH :]
        else:
            top, bottom = inv[0:DEPTH], inv[rows - DEPTH :]
        first[f * DEPTH : (f + 1) * DEPTH] = jnp.where(odd, top, bottom)
        second[f * DEPTH : (f + 1) * DEPTH] = jnp.where(odd, bottom, top)
    for copy in copies[4:]:
        copy.wait()


def load(arrays):
    source, coupling = arrays[:2]
    nv, rows, cols = source.shape
    slab = (((nv + coupling.shape[0] + 1) * DEPTH, cols), F32)
    return on_chip(
        functools.partial(load_kernel, len(arrays)),
        [],
        [like(x) for x in arrays] + [((rows, cols), F32), slab, slab],
        [pltpu.SemaphoreType.DMA((len(arrays),))],
        far=arrays,
        name="load",
    )


def ordered(axis, first, second):
    odd, at = is_odd(axis), lax.axis_index(axis)
    before, after = jnp.where(odd, first, second), jnp.where(odd, second, first)
    return jnp.where(at == 0, 0.0, before), jnp.where(at == lax.axis_size(axis) - 1, 0.0, after)


def cols_kernel(src, cpl, inv, row_first, row_second, col_first, col_second, north, south):
    nv, rows, cols = src.shape
    nc = cpl.shape[0]
    half = col_first.shape[0]
    north[...] = jnp.zeros(north.shape, F32)
    south[...] = jnp.zeros(south.shape, F32)
    for f in range(nv + nc + 1):
        here = slice(f * DEPTH, (f + 1) * DEPTH)
        before, after = ordered("gx", row_first[here], row_second[here])
        north[f, EDGE - DEPTH :] = before
        south[f, 0:DEPTH] = after
    lane = lax.broadcasted_iota(jnp.int32, (half, LANE), 1)
    slabs = []
    for window, extra in ((slice(0, LANE), 0), (slice(cols - LANE, cols), DEPTH)):
        slab = jnp.zeros((half, LANE), F32)
        for f in range(nv + nc + 1):
            if f < nv:
                x = src[f, :, window].astype(F32)
            elif f < nv + nc:
                x = cpl[f - nv, :, window].astype(F32)
            else:
                x = inv[:, window]
            x = jnp.concatenate([north[f, :, window], x, south[f, :, window]], axis=0)
            for part, at in ((x[:half], DEPTH * f), (x[half:], DEPTH * f + LANE // 2)):
                own = jnp.logical_and(lane >= at, lane < at + DEPTH)
                slab = jnp.where(own, pltpu.roll(part, (at + extra) % LANE, 1), slab)
        slabs.append(slab)
    odd = is_odd("gy")
    col_first[...] = jnp.where(odd, slabs[0], slabs[1])
    col_second[...] = jnp.where(odd, slabs[1], slabs[0])


def col_slabs(source, coupling, inv, row_halos):
    nv, rows, cols = source.shape
    slab = (((rows + 2 * EDGE) // 2, LANE), F32)
    halo = ((nv + coupling.shape[0] + 1, EDGE, cols), F32)
    return on_chip(
        cols_kernel, [source, coupling, inv, *row_halos], [slab, slab, halo, halo], name="col_slabs"
    )


def column_of(row):
    hidden = row.shape[1]
    wide = jnp.concatenate([row, jnp.zeros((1, LANE - hidden), F32)], axis=1)
    return jnp.transpose(jnp.broadcast_to(wide, (LANE, LANE)))[:hidden]


def across(block, width):
    return jnp.concatenate([block] * (width // LANE), axis=1)


def weights_kernel(win, wmid, wtop, wout, bias, w1, w2, w3, cst):
    nf, hidden = win.shape
    step_rows, blk = hidden + 16, 16
    depth = w1.shape[1]
    feat_of = lax.broadcasted_iota(jnp.int32, (nf, depth), 1) // blk
    pick = (feat_of == lax.broadcasted_iota(jnp.int32, (nf, depth), 0)).astype(F32).astype(BF16)
    spread = lax.dot_general(win[...], pick, TN, preferred_element_type=F32)
    col = lax.broadcasted_iota(jnp.int32, (hidden, depth), 1)
    col_f = lax.broadcasted_iota(jnp.int32, (16, depth), 1)
    row_f = lax.broadcasted_iota(jnp.int32, (16, depth), 0)
    for r in range(blk):
        base = r * step_rows
        w1[base : base + hidden] = jnp.where(col % blk == r, spread, 0.0).astype(BF16)
        same = jnp.logical_and(col_f == row_f * blk + r, row_f < nf)
        w1[base + hidden : base + step_rows] = jnp.where(same, 1.0, 0.0).astype(BF16)
    w2[...] = jnp.transpose(wmid[...].astype(F32)).astype(BF16)
    w3[...] = jnp.transpose(wtop[...].astype(F32)).astype(BF16)
    for k in range(3):
        cst[k] = column_of(bias[k : k + 1, :])
    cst[3] = column_of(wout[...])


def prepare(weight_in, weight_mid, weight_top, weight_out, biases):
    nf, hidden = weight_in.shape
    depth = -(-nf * 16 // LANE) * LANE
    return on_chip(
        weights_kernel,
        [weight_in, weight_mid, weight_top, weight_out, biases],
        [
            ((16 * (hidden + 16), depth), BF16),
            ((hidden, hidden), BF16),
            ((hidden, hidden), BF16),
            ((4, hidden, LANE), F32),
        ],
        name="weights",
    )


def slope(act):
    return 1.0 - act * act


def forward_kernel(first_row, feat, w1, w2, w3, cst, acts, slopes, beta, x1):
    nf, _, cols = feat.shape
    hidden = w2.shape[0]
    step_rows, blk, per = hidden + 16, 16, 4
    x1[...] = jnp.zeros(x1.shape, BF16)

    @pl.loop(0, acts.shape[0] // blk)
    def _(block):
        start = pl.multiple_of(block * blk, blk)
        x1[0 : nf * blk] = feat[:, pl.ds(first_row + start, blk), :].reshape(nf * blk, cols)
        b1, b2, b3, wo = (across(cst[k], cols) for k in range(4))
        lines = []
        first = jnp.dot(w1[...], x1[...], preferred_element_type=F32)
        for g in range(blk // per):
            ones = []
            for q in range(g * per, (g + 1) * per):
                part = first[q * step_rows : (q + 1) * step_rows]
                one = jnp.tanh(part[:hidden] + b1).astype(BF16)
                slopes[start + q, 0:hidden] = slope(one.astype(F32))
                acts[start + q, 0:hidden] = one
                acts[start + q, 2 * hidden : 2 * hidden + 16] = part[hidden:].astype(BF16)
                ones.append(one)
            second = jnp.dot(w2[...], jnp.concatenate(ones, axis=1), preferred_element_type=F32)
            twos = []
            for q in range(per):
                two = jnp.tanh(second[:, q * cols : (q + 1) * cols] + b2).astype(BF16)
                slopes[start + (g * per + q), hidden : 2 * hidden] = slope(two.astype(F32))
                acts[start + (g * per + q), hidden : 2 * hidden] = two
                twos.append(two)
            third = jnp.dot(w3[...], jnp.concatenate(twos, axis=1), preferred_element_type=F32)
            for q in range(per):
                three = jnp.tanh(third[:, q * cols : (q + 1) * cols] + b3).astype(BF16)
                acts[start + (g * per + q), 2 * hidden + 16 :] = three
                three = three.astype(F32)
                slopes[start + (g * per + q), 2 * hidden :] = wo * slope(three)
                lines.append(1.0 + jnp.sum(three * wo, axis=0, keepdims=True))
        beta[pl.ds(start, blk), :] = jnp.concatenate(lines, axis=0)


def forward(features, prepared, first_row, count):
    nf, _, cols = features.shape
    w1, w2 = prepared[:2]
    hidden = w2.shape[0]
    high = 3 * hidden + 16
    return on_chip(
        functools.partial(forward_kernel, first_row),
        [features, *prepared],
        [((count, high, cols), BF16), ((count, 3 * hidden, cols), F32), ((count, cols), F32)],
        [pltpu.VMEM((w1.shape[1], cols), BF16)],
        cost_estimate=pl.CostEstimate(
            flops=2 * count * cols * (nf + 2 * hidden) * hidden,
            bytes_accessed=2 * count * cols * (high + nf),
            transcendentals=3 * count * cols * hidden,
        ),
        name="network_forward",
    )


def span(t, k):
    return (slice(t * SUB, (t + 1) * SUB), slice(k * LANE, (k + 1) * LANE))


class Shifts:
    def __init__(self, tiles, lanes):
        self.tiles, self.lanes = tiles, lanes
        sub = lax.broadcasted_iota(jnp.int32, (SUB, LANE), 0)
        lane = lax.broadcasted_iota(jnp.int32, (SUB, LANE), 1)
        self.first_sub, self.last_sub = sub == 0, sub == SUB - 1
        self.first_lane, self.last_lane = lane == 0, lane == LANE - 1

    def row(self, ref, lead, t):
        t = min(max(t, 0), self.tiles - 1)
        return [ref[lead + span(t, k)] for k in range(self.lanes)]

    def above(self, rows, k):
        return pltpu.roll(jnp.where(self.last_sub, rows[0][k], rows[1][k]), 1, 0)

    def below(self, rows, k):
        return pltpu.roll(jnp.where(self.first_sub, rows[2][k], rows[1][k]), SUB - 1, 0)

    def left(self, rows, k):
        return pltpu.roll(jnp.where(self.last_lane, rows[1][(k - 1) % self.lanes], rows[1][k]), 1, 1)

    def right(self, rows, k):
        other = rows[1][(k + 1) % self.lanes]
        return pltpu.roll(jnp.where(self.first_lane, other, rows[1][k]), LANE - 1, 1)

    def around(self, ref, lead, t, k_count):
        rows = [self.row(ref, lead, t + o) for o in (-1, 0, 1)]
        moves = (self.above, self.below, self.left, self.right)
        return [[move(rows, k) for move in moves] for k in range(k_count)]


def extend(src, cpl, inverse, north, south, col_halos, shifts, raw, src_x, cpl_x):
    nv, rows, cols = src.shape
    nc = cpl.shape[0]
    tall = rows + 2 * EDGE
    inner = slice(EDGE, EDGE + rows)
    lane = lax.broadcasted_iota(jnp.int32, (tall, LANE), 1)
    from_east, from_west = lane < DEPTH, lane >= LANE - DEPTH
    west, east = ordered("gy", *(x[...] for x in col_halos))
    for f in range(nv + nc + 1):
        if f < nv:
            raw[f, inner, 0:cols] = src[f].astype(F32)
        elif f < nv + nc:
            raw[f, inner, 0:cols] = cpl[f - nv].astype(F32)
        else:
            raw[f, inner, 0:cols] = inverse[...]
        raw[f, 0:EDGE, 0:cols] = north[f]
        raw[f, EDGE + rows :, 0:cols] = south[f]
        low, high = (-DEPTH * f) % LANE, (LANE // 2 - DEPTH * f) % LANE
        e = jnp.concatenate([pltpu.roll(east, at, 1) for at in (low, high)], axis=0)
        w = jnp.concatenate([pltpu.roll(west, (at - DEPTH) % LANE, 1) for at in (low, high)], axis=0)
        raw[f, :, cols:] = jnp.where(from_east, e, jnp.where(from_west, w, 0.0))
    for t in range(shifts.tiles):
        inv = shifts.row(raw, (nv + nc,), t)
        for k in range(shifts.lanes):
            for v in range(nv):
                src_x[(v,) + span(t, k)] = inv[k] * raw[(v,) + span(t, k)]
        for d, move in enumerate((shifts.above, shifts.below, shifts.left, shifts.right)):
            rows_d = [shifts.row(raw, (nv + d,), t + o) for o in (-1, 0, 1)]
            for k in range(shifts.lanes):
                cpl_x[(d,) + span(t, k)] = inv[k] * move(rows_d, k)


def adjoint_kernel(
    num_feat, src, cpl, inverse, prod, beta_a, beta_b, north, south, col_first, col_second,
    wmid, wtop, acts_a, slopes_a, acts_b, slopes_b, mix,
    keep, give, adj_out, beta_out,
    raw, src_x, cpl_x, adj, done, sums, g_mid, g_top, g_in, sems,
):
    nv, rows, cols = src.shape
    nc = cpl.shape[0]
    hidden, blk = wmid.shape[0], SUB
    half = beta_a.shape[0]
    tiles, lanes = (rows + 2 * EDGE) // SUB, cols // LANE + 1
    copies = [
        pltpu.make_async_copy(beta_a, beta_out.at[0:half], sems.at[0]),
        pltpu.make_async_copy(beta_b, beta_out.at[half:rows], sems.at[1]),
        pltpu.make_async_copy(done, adj_out, sems.at[2]),
    ]
    copies[0].start()
    copies[1].start()
    shifts = Shifts(tiles, lanes)
    extend(src, cpl, inverse, north, south, (col_first, col_second), shifts, raw, src_x, cpl_x)
    weights = [[mix[b, a] for a in range(nv)] for b in range(nv)]

    def sweep(number, t):
        last = number == SWEEPS
        count = lanes - 1 if last else lanes
        couple = [[cpl_x[(d,) + span(t, k)] for d in range(nc)] for k in range(count)]
        total = [[src_x[(a,) + span(t, k)] for a in range(nv)] for k in range(count)]
        for b in range(nv):
            old, lead = (src_x, (b,)) if number == 1 else (adj, (number - 2, b))
            around = shifts.around(old, lead, t, count)
            for k in range(count):
                terms = [couple[k][d] * around[k][d] for d in range(nc)]
                inc = (terms[0] + terms[1]) + (terms[2] + terms[3])
                total[k] = [total[k][a] + weights[b][a] * inc for a in range(nv)]
        for k in range(count):
            for a in range(nv):
                if last:
                    done[(a,) + span(t - EDGE // SUB, k)] = total[k][a]
                else:
                    adj[(number - 1, a) + span(t, k)] = total[k][a]

    def fold(x):
        parts = [x[:, k * LANE : (k + 1) * LANE] for k in range(cols // LANE)]
        return functools.reduce(jnp.add, parts)

    def joined(xs):
        return jnp.concatenate(xs, axis=1)

    def outer(x, d):
        return lax.dot_general(x, d, NT, preferred_element_type=F32)

    def backward(first):
        if first < half:
            acts, slopes, beta, start = acts_a, slopes_a, beta_a, first
        else:
            acts, slopes, beta, start = acts_b, slopes_b, beta_b, first - half
        here = slice(first, first + blk)
        sens = done[nv - 1, here] * prod[here] + REG_WEIGHT * (beta[start : start + blk] - 1.0)

        def layer(lo, high):
            return joined([acts[start + q, lo:high] for q in range(blk)])

        def behind(weight, delta, lo):
            product = jnp.dot(weight, delta, preferred_element_type=F32)
            total, out = jnp.zeros((hidden, LANE), F32), []
            for q in range(blk):
                d = product[:, q * cols : (q + 1) * cols] * slopes[start + q, lo : lo + hidden]
                total = total + fold(d)
                out.append(d.astype(BF16))
            return joined(out), total

        out_sum, top_sum, d3 = jnp.zeros((hidden, LANE), F32), jnp.zeros((hidden, LANE), F32), []
        for q in range(blk):
            act = acts[start + q, 2 * hidden + 16 :].astype(F32)
            sen = jnp.broadcast_to(sens[q : q + 1], (hidden, cols))
            out_sum = out_sum + fold(act * sen)
            d = sen * slopes[start + q, 2 * hidden :]
            top_sum = top_sum + fold(d)
            d3.append(d.astype(BF16))
        d3 = joined(d3)
        d2, mid_sum = behind(wtop[...], d3, hidden)
        d1, in_sum = behind(wmid[...], d2, 0)
        new = (
            (g_top, outer(layer(hidden, 2 * hidden), d3)),
            (g_mid, outer(layer(0, hidden), d2)),
            (g_in, outer(d1, layer(2 * hidden, 2 * hidden + 16))),
            *((sums.at[k], part) for k, part in enumerate((out_sum, in_sum, mid_sum, top_sum))),
        )
        for ref, part in new:
            ref[...] = part if first == 0 else ref[...] + part

    for number in range(1, SWEEPS):
        for t in range(SWEEPS + 1 - number):
            sweep(number, t)
    for t in range(1, tiles - 1):
        for number in range(1, SWEEPS + 1):
            if t + SWEEPS - number < tiles:
                sweep(number, t + SWEEPS - number)
        if t > 1:
            backward((t - 2) * blk)
    copies[2].start()
    backward(rows - blk)

    turned = jnp.transpose(joined([g_in[...], jnp.zeros((hidden, LANE - 16), F32)]))
    tail = turned[SUB : 2 * SUB]
    row = lax.broadcasted_iota(jnp.int32, (SUB, hidden), 0)
    for k in range(4):
        line = jnp.sum(jnp.transpose(sums[k]), axis=0, keepdims=True)
        tail = tail + jnp.where(row == k + num_feat - SUB, jnp.broadcast_to(line, (SUB, hidden)), 0.0)
    whole_sum = jnp.concatenate([joined([g_mid[...], g_top[...]]), joined([turned[0:SUB], tail])], axis=0)
    size = keep.shape[0]
    missing = jnp.zeros((2 * size - hidden - SUB, LANE), F32)
    upper, lower = whole_sum[:size], jnp.concatenate([whole_sum[size:], missing], axis=0)
    odd = is_odd("gy")
    keep[...] = jnp.where(odd, lower, upper)
    give[...] = jnp.where(odd, upper, lower)
    for copy in copies:
        copy.wait()


def sweeps_and_backward(num_feat, source, coupling, inverse, production, betas, halos, weights, nets, mixing):
    nv, rows, cols = source.shape
    nc = coupling.shape[0]
    hidden = weights[0].shape[0]
    size = -(-(hidden + SUB) // (2 * SUB)) * SUB
    tall, wide = rows + 2 * EDGE, cols + LANE
    near, far = pl.BlockSpec(memory_space=pltpu.VMEM), pl.BlockSpec(memory_space=pltpu.HBM)
    operands = [source, coupling, inverse, production, *betas, *halos, *weights, *nets]
    return pl.pallas_call(
        functools.partial(adjoint_kernel, num_feat),
        in_specs=[near] * len(operands) + [pl.BlockSpec(memory_space=pltpu.SMEM)],
        out_specs=[near, near, far, far],
        out_shape=[
            pltpu.VMEM((size, LANE), F32),
            pltpu.VMEM((size, LANE), F32),
            pltpu.HBM((nv, rows, cols), F32),
            pltpu.HBM((rows, cols), F32),
        ],
        scratch_shapes=[
            pltpu.VMEM((nv + nc + 1, tall, wide), F32),
            pltpu.VMEM((nv, tall, wide), F32),
            pltpu.VMEM((nc, tall, wide), F32),
            pltpu.VMEM((SWEEPS - 1, nv, tall, wide), F32),
            pltpu.VMEM((nv, rows, cols), F32),
            pltpu.VMEM((4, hidden, LANE), F32),
            pltpu.VMEM((hidden, hidden), F32),
            pltpu.VMEM((hidden, hidden), F32),
            pltpu.VMEM((hidden, 16), F32),
            pltpu.SemaphoreType.DMA((3,)),
        ],
        compiler_params=params(),
        name="sweeps_backward",
    )(*operands, mixing)


def clip_kernel(mine, other, gin, gmid, gtop, gout, gbias):
    hidden = gmid.shape[0]
    odd = is_odd("gy")
    own, sent = mine[...], other[...]
    total = jnp.concatenate([jnp.where(odd, sent, own), jnp.where(odd, own, sent)], axis=0)[: hidden + SUB]
    squares = jnp.sum(jnp.sum(total * total, axis=0, keepdims=True), axis=1, keepdims=True)
    total = total * (CLIP_NORM / jnp.maximum(jnp.sqrt(squares), CLIP_NORM))
    gmid[...] = total[:hidden, :hidden]
    gtop[...] = total[:hidden, hidden:]
    low, high = total[hidden:, :hidden], total[hidden:, hidden:]
    gin[0:SUB] = low
    gin[SUB:] = high[: gin.shape[0] - SUB]
    at = gin.shape[0] - SUB
    gout[...] = high[at : at + 1]
    gbias[...] = high[at + 1 : at + 4]


def clip_all(mine, other, num_feat, hidden):
    shapes = [(num_feat, hidden), (hidden, hidden), (hidden, hidden), (1, hidden), (3, hidden)]
    return pl.pallas_call(
        clip_kernel,
        grid=(1,),
        in_specs=[whole(mine.shape)] * 2,
        out_specs=[whole(s) for s in shapes],
        out_shape=[jax.ShapeDtypeStruct(s, F32) for s in shapes],
        compiler_params=params(),
        name="clip",
    )(mine, other)


def sum_over_case(keep, give):
    def swapped(x, axis, k):
        return lax.ppermute(x, axis, [(i, i ^ k) for i in range(lax.axis_size(axis))])

    mine = keep + swapped(give, "gy", 1)
    for axis, step, radix in (("gy", 2, 2), ("gx", 1, 4)):
        count = lax.axis_size(axis)
        while step < count:
            parts = [mine] + [swapped(mine, axis, k * step) for k in range(1, min(radix, count // step))]
            while len(parts) > 1:
                parts = [a + b for a, b in zip(parts[::2], parts[1::2])]
            mine = parts[0]
            step *= radix
    return mine, swapped(mine, "gy", 1)


def row_swaps(first, second):
    num_x, num_y = lax.axis_size("gx"), lax.axis_size("gy")
    out = []
    for start, slab in ((0, first), (1, second)):
        partner = {}
        for i in range(num_x):
            j = i + 1 if i % 2 == start else i - 1
            for y in range(num_y):
                if 0 <= j < num_x:
                    partner[i * num_y + y] = j * num_y + y
                elif num_y % 2 == 0:
                    partner[i * num_y + y] = i * num_y + (y ^ 1)
        out.append(lax.ppermute(slab, ("gx", "gy"), sorted(partner.items())))
    return out


def col_swaps(first, second):
    count = lax.axis_size("gy")
    out = []
    for start, slab in ((0, first), (1, second)):
        low = [(i, i + 1) for i in range(start, count - 1, 2)]
        if count % 2 == 0 and start == 1:
            low.append((0, count - 1))
        out.append(lax.ppermute(slab, "gy", low + [(b, a) for a, b in low]))
    return out


def shards(
    features, source, coupling, diagonal, production, bc_code, mixing,
    weight_in, weight_mid, weight_top, weight_out, biases,
):
    num_feat, rows, _ = features.shape
    hidden = weight_mid.shape[0]
    loaded = load([
        source, coupling, diagonal, bc_code, production, features,
        weight_in, weight_mid, weight_top, weight_out.reshape(1, hidden), biases,
    ])
    source, coupling, _, _, production, features, weight_in, weight_mid, weight_top, wout, biases = loaded[:11]
    inverse, *row_slabs = loaded[11:]
    row_halos = row_swaps(*row_slabs)
    prepared = prepare(weight_in, weight_mid, weight_top, wout, biases)
    half = rows - 32
    *net_a, beta_a = forward(features, prepared, 0, half)
    *row_halos, beta_a = lax.optimization_barrier((*row_halos, beta_a))
    first, second, *row_halos = col_slabs(source, coupling, inverse, row_halos)
    col_halos = col_swaps(first, second)
    *net_b, beta_b = forward(features, prepared, half, rows - half)
    keep, give, adjoint, beta = sweeps_and_backward(
        num_feat, source, coupling, inverse, production, (beta_a, beta_b), (*row_halos, *col_halos),
        (weight_mid, weight_top), (*net_a, *net_b), mixing,
    )
    grad_in, grad_mid, grad_top, grad_out, grad_bias = clip_all(*sum_over_case(keep, give), num_feat, hidden)
    return (adjoint, beta, grad_in, grad_mid, grad_top, grad_out.reshape(hidden), grad_bias)


def solution(mesh):
    cells3 = P(None, ("case", "gx"), "gy")
    cells2 = P(("case", "gx"), "gy")
    return jax.shard_map(
        shards,
        mesh=mesh,
        in_specs=(cells3,) * 3 + (cells2,) * 3 + (P(),) * 6,
        out_specs=(cells3, cells2, P("case"), P("case"), P("case"), P("case"), P("case")),
        check_vma=False,
    )
```

```python
import functools

import jax
import jax.numpy as jnp
from jax import lax
from jax.experimental import pallas as pl
from jax.experimental.pallas import tpu as pltpu
from jax.sharding import PartitionSpec as P

SWEEPS = 6
WALL_EXTRA = 0.2
FAR_EXTRA = 0.6
REG_WEIGHT = 0.5
CLIP_NORM = 64.0
DEPTH = SWEEPS
EDGE = 8
SUB, LANE = 8, 128
F32, BF16 = jnp.float32, jnp.bfloat16
NT = (((1,), (1,)), ((), ()))
TN = (((0,), (0,)), ((), ()))
VMEM_BYTES = 16 * 1024 * 1024


def whole(shape):
    return pl.BlockSpec(shape, lambda *_: (0,) * len(shape))


def in_hbm(x):
    return pltpu.with_memory_space_constraint(x, pltpu.HBM)


def on_chip(kernel, operands, outs, scratch=(), far=(), far_outs=(), **kwargs):
    here, there = pl.BlockSpec(memory_space=pltpu.VMEM), pl.BlockSpec(memory_space=pltpu.HBM)
    return pl.pallas_call(
        kernel,
        in_specs=[here] * len(operands) + [there] * len(far),
        out_specs=[here] * len(outs) + [there] * len(far_outs),
        out_shape=[pltpu.VMEM(*o) for o in outs] + [pltpu.HBM(*o) for o in far_outs],
        scratch_shapes=list(scratch),
        compiler_params=params(),
        **kwargs,
    )(*operands, *[in_hbm(x) for x in far])


def like(x):
    return (x.shape, x.dtype)


def params():
    return pltpu.CompilerParams(vmem_limit_bytes=VMEM_BYTES)


def inverse_diag(diag, code):
    total = diag + jnp.where(code == 1, WALL_EXTRA, 0.0) + jnp.where(code == 2, FAR_EXTRA, 0.0)
    return 1.0 / total


def is_odd(axis):
    return lax.axis_index(axis) % 2 == 1


def load_kernel(count, *refs):
    far, near = refs[:count], refs[count : 2 * count]
    inv, first, second, sems = refs[2 * count :]
    copies = [pltpu.make_async_copy(far[k], near[k], sems.at[k]) for k in range(count)]
    for copy in copies:
        copy.start()
    src, cpl, dia, bc = near[:4]
    for copy in copies[:4]:
        copy.wait()
    nv, rows, _ = src.shape
    nc = cpl.shape[0]
    inv[...] = inverse_diag(dia[...], bc[...])
    odd = is_odd("gx")
    for f in range(nv + nc + 1):
        if f < nv + nc:
            ref, k = (src, f) if f < nv else (cpl, f - nv)
            top, bottom = ref[k, 0:16].astype(F32)[:DEPTH], ref[k, rows - 16 :].astype(F32)[16 - DEPTH :]
        else:
            top, bottom = inv[0:DEPTH], inv[rows - DEPTH :]
        first[f * DEPTH : (f + 1) * DEPTH] = jnp.where(odd, top, bottom)
        second[f * DEPTH : (f + 1) * DEPTH] = jnp.where(odd, bottom, top)
    for copy in copies[4:]:
        copy.wait()


def load(arrays):
    source, coupling = arrays[:2]
    nv, rows, cols = source.shape
    slab = (((nv + coupling.shape[0] + 1) * DEPTH, cols), F32)
    return on_chip(
        functools.partial(load_kernel, len(arrays)),
        [],
        [like(x) for x in arrays] + [((rows, cols), F32), slab, slab],
        [pltpu.SemaphoreType.DMA((len(arrays),))],
        far=arrays,
        name="load",
    )


def ordered(axis, first, second):
    odd, at = is_odd(axis), lax.axis_index(axis)
    before, after = jnp.where(odd, first, second), jnp.where(odd, second, first)
    return jnp.where(at == 0, 0.0, before), jnp.where(at == lax.axis_size(axis) - 1, 0.0, after)


def cols_kernel(src, cpl, inv, row_first, row_second, col_first, col_second, north, south):
    nv, rows, cols = src.shape
    nc = cpl.shape[0]
    half = col_first.shape[0]
    north[...] = jnp.zeros(north.shape, F32)
    south[...] = jnp.zeros(south.shape, F32)
    for f in range(nv + nc + 1):
        here = slice(f * DEPTH, (f + 1) * DEPTH)
        before, after = ordered("gx", row_first[here], row_second[here])
        north[f, EDGE - DEPTH :] = before
        south[f, 0:DEPTH] = after
    lane = lax.broadcasted_iota(jnp.int32, (half, LANE), 1)
    slabs = []
    for window, extra in ((slice(0, LANE), 0), (slice(cols - LANE, cols), DEPTH)):
        slab = jnp.zeros((half, LANE), F32)
        for f in range(nv + nc + 1):
            if f < nv:
                x = src[f, :, window].astype(F32)
            elif f < nv + nc:
                x = cpl[f - nv, :, window].astype(F32)
            else:
                x = inv[:, window]
            x = jnp.concatenate([north[f, :, window], x, south[f, :, window]], axis=0)
            for part, at in ((x[:half], DEPTH * f), (x[half:], DEPTH * f + LANE // 2)):
                own = jnp.logical_and(lane >= at, lane < at + DEPTH)
                slab = jnp.where(own, pltpu.roll(part, (at + extra) % LANE, 1), slab)
        slabs.append(slab)
    odd = is_odd("gy")
    col_first[...] = jnp.where(odd, slabs[0], slabs[1])
    col_second[...] = jnp.where(odd, slabs[1], slabs[0])


def col_slabs(source, coupling, inv, row_halos):
    nv, rows, cols = source.shape
    slab = (((rows + 2 * EDGE) // 2, LANE), F32)
    halo = ((nv + coupling.shape[0] + 1, EDGE, cols), F32)
    return on_chip(
        cols_kernel, [source, coupling, inv, *row_halos], [slab, slab, halo, halo], name="col_slabs"
    )


def column_of(row):
    hidden = row.shape[1]
    wide = jnp.concatenate([row, jnp.zeros((1, LANE - hidden), F32)], axis=1)
    return jnp.transpose(jnp.broadcast_to(wide, (LANE, LANE)))[:hidden]


def across(block, width):
    return jnp.concatenate([block] * (width // LANE), axis=1)


def weights_kernel(win, wmid, wtop, wout, bias, w1, w2, w3, cst):
    nf, hidden = win.shape
    step_rows, blk = hidden + 16, 16
    depth = w1.shape[1]
    feat_of = lax.broadcasted_iota(jnp.int32, (nf, depth), 1) // blk
    pick = (feat_of == lax.broadcasted_iota(jnp.int32, (nf, depth), 0)).astype(F32).astype(BF16)
    spread = lax.dot_general(win[...], pick, TN, preferred_element_type=F32)
    col = lax.broadcasted_iota(jnp.int32, (hidden, depth), 1)
    col_f = lax.broadcasted_iota(jnp.int32, (16, depth), 1)
    row_f = lax.broadcasted_iota(jnp.int32, (16, depth), 0)
    for r in range(blk):
        base = r * step_rows
        w1[base : base + hidden] = jnp.where(col % blk == r, spread, 0.0).astype(BF16)
        same = jnp.logical_and(col_f == row_f * blk + r, row_f < nf)
        w1[base + hidden : base + step_rows] = jnp.where(same, 1.0, 0.0).astype(BF16)
    w2[...] = jnp.transpose(wmid[...].astype(F32)).astype(BF16)
    w3[...] = jnp.transpose(wtop[...].astype(F32)).astype(BF16)
    for k in range(3):
        cst[k] = column_of(bias[k : k + 1, :])
    cst[3] = column_of(wout[...])


def prepare(weight_in, weight_mid, weight_top, weight_out, biases):
    nf, hidden = weight_in.shape
    depth = -(-nf * 16 // LANE) * LANE
    return on_chip(
        weights_kernel,
        [weight_in, weight_mid, weight_top, weight_out, biases],
        [
            ((16 * (hidden + 16), depth), BF16),
            ((hidden, hidden), BF16),
            ((hidden, hidden), BF16),
            ((4, hidden, LANE), F32),
        ],
        name="weights",
    )


def slope(act):
    return 1.0 - act * act


def forward_kernel(first_row, feat, w1, w2, w3, cst, acts, slopes, beta, x1):
    nf, _, cols = feat.shape
    hidden = w2.shape[0]
    step_rows, blk, per = hidden + 16, 16, 4
    x1[...] = jnp.zeros(x1.shape, BF16)

    @pl.loop(0, acts.shape[0] // blk)
    def _(block):
        start = pl.multiple_of(block * blk, blk)
        x1[0 : nf * blk] = feat[:, pl.ds(first_row + start, blk), :].reshape(nf * blk, cols)
        b1, b2, b3, wo = (across(cst[k], cols) for k in range(4))
        lines = []
        first = jnp.dot(w1[...], x1[...], preferred_element_type=F32)
        for g in range(blk // per):
            ones = []
            for q in range(g * per, (g + 1) * per):
                part = first[q * step_rows : (q + 1) * step_rows]
                one = jnp.tanh(part[:hidden] + b1).astype(BF16)
                slopes[start + q, 0:hidden] = slope(one.astype(F32))
                acts[start + q, 0:hidden] = one
                acts[start + q, 2 * hidden : 2 * hidden + 16] = part[hidden:].astype(BF16)
                ones.append(one)
            second = jnp.dot(w2[...], jnp.concatenate(ones, axis=1), preferred_element_type=F32)
            twos = []
            for q in range(per):
                two = jnp.tanh(second[:, q * cols : (q + 1) * cols] + b2).astype(BF16)
                slopes[start + (g * per + q), hidden : 2 * hidden] = slope(two.astype(F32))
                acts[start + (g * per + q), hidden : 2 * hidden] = two
                twos.append(two)
            third = jnp.dot(w3[...], jnp.concatenate(twos, axis=1), preferred_element_type=F32)
            for q in range(per):
                three = jnp.tanh(third[:, q * cols : (q + 1) * cols] + b3).astype(BF16)
                acts[start + (g * per + q), 2 * hidden + 16 :] = three
                three = three.astype(F32)
                slopes[start + (g * per + q), 2 * hidden :] = wo * slope(three)
                lines.append(1.0 + jnp.sum(three * wo, axis=0, keepdims=True))
        beta[pl.ds(start, blk), :] = jnp.concatenate(lines, axis=0)


def forward(features, prepared, first_row, count):
    nf, _, cols = features.shape
    w1, w2 = prepared[:2]
    hidden = w2.shape[0]
    high = 3 * hidden + 16
    return on_chip(
        functools.partial(forward_kernel, first_row),
        [features, *prepared],
        [((count, high, cols), BF16), ((count, 3 * hidden, cols), F32), ((count, cols), F32)],
        [pltpu.VMEM((w1.shape[1], cols), BF16)],
        cost_estimate=pl.CostEstimate(
            flops=2 * count * cols * (nf + 2 * hidden) * hidden,
            bytes_accessed=2 * count * cols * (high + nf),
            transcendentals=3 * count * cols * hidden,
        ),
        name="network_forward",
    )


def span(t, k):
    return (slice(t * SUB, (t + 1) * SUB), slice(k * LANE, (k + 1) * LANE))


class Shifts:
    def __init__(self, tiles, lanes):
        self.tiles, self.lanes = tiles, lanes
        sub = lax.broadcasted_iota(jnp.int32, (SUB, LANE), 0)
        lane = lax.broadcasted_iota(jnp.int32, (SUB, LANE), 1)
        self.first_sub, self.last_sub = sub == 0, sub == SUB - 1
        self.first_lane, self.last_lane = lane == 0, lane == LANE - 1

    def row(self, ref, lead, t):
        t = min(max(t, 0), self.tiles - 1)
        return [ref[lead + span(t, k)] for k in range(self.lanes)]

    def above(self, rows, k):
        return pltpu.roll(jnp.where(self.last_sub, rows[0][k], rows[1][k]), 1, 0)

    def below(self, rows, k):
        return pltpu.roll(jnp.where(self.first_sub, rows[2][k], rows[1][k]), SUB - 1, 0)

    def left(self, rows, k):
        return pltpu.roll(jnp.where(self.last_lane, rows[1][(k - 1) % self.lanes], rows[1][k]), 1, 1)

    def right(self, rows, k):
        other = rows[1][(k + 1) % self.lanes]
        return pltpu.roll(jnp.where(self.first_lane, other, rows[1][k]), LANE - 1, 1)

    def around(self, ref, lead, t, k_count):
        rows = [self.row(ref, lead, t + o) for o in (-1, 0, 1)]
        moves = (self.above, self.below, self.left, self.right)
        return [[move(rows, k) for move in moves] for k in range(k_count)]


def extend(src, cpl, inverse, north, south, col_halos, shifts, raw, src_x, cpl_x):
    nv, rows, cols = src.shape
    nc = cpl.shape[0]
    tall = rows + 2 * EDGE
    inner = slice(EDGE, EDGE + rows)
    lane = lax.broadcasted_iota(jnp.int32, (tall, LANE), 1)
    from_east, from_west = lane < DEPTH, lane >= LANE - DEPTH
    west, east = ordered("gy", *(x[...] for x in col_halos))
    for f in range(nv + nc + 1):
        if f < nv:
            raw[f, inner, 0:cols] = src[f].astype(F32)
        elif f < nv + nc:
            raw[f, inner, 0:cols] = cpl[f - nv].astype(F32)
        else:
            raw[f, inner, 0:cols] = inverse[...]
        raw[f, 0:EDGE, 0:cols] = north[f]
        raw[f, EDGE + rows :, 0:cols] = south[f]
        low, high = (-DEPTH * f) % LANE, (LANE // 2 - DEPTH * f) % LANE
        e = jnp.concatenate([pltpu.roll(east, at, 1) for at in (low, high)], axis=0)
        w = jnp.concatenate([pltpu.roll(west, (at - DEPTH) % LANE, 1) for at in (low, high)], axis=0)
        raw[f, :, cols:] = jnp.where(from_east, e, jnp.where(from_west, w, 0.0))
    for t in range(shifts.tiles):
        inv = shifts.row(raw, (nv + nc,), t)
        for k in range(shifts.lanes):
            for v in range(nv):
                src_x[(v,) + span(t, k)] = inv[k] * raw[(v,) + span(t, k)]
        for d, move in enumerate((shifts.above, shifts.below, shifts.left, shifts.right)):
            rows_d = [shifts.row(raw, (nv + d,), t + o) for o in (-1, 0, 1)]
            for k in range(shifts.lanes):
                cpl_x[(d,) + span(t, k)] = inv[k] * move(rows_d, k)


def adjoint_kernel(
    num_feat, src, cpl, inverse, prod, beta_a, beta_b, north, south, col_first, col_second,
    wmid, wtop, acts_a, slopes_a, acts_b, slopes_b, mix,
    packed, adj_out, beta_out,
    raw, src_x, cpl_x, adj, done, sums, g_mid, g_top, g_in, sems,
):
    nv, rows, cols = src.shape
    nc = cpl.shape[0]
    hidden, blk = wmid.shape[0], SUB
    half = beta_a.shape[0]
    tiles, lanes = (rows + 2 * EDGE) // SUB, cols // LANE + 1
    copies = [
        pltpu.make_async_copy(beta_a, beta_out.at[0:half], sems.at[0]),
        pltpu.make_async_copy(beta_b, beta_out.at[half:rows], sems.at[1]),
        pltpu.make_async_copy(done, adj_out, sems.at[2]),
    ]
    copies[0].start()
    copies[1].start()
    shifts = Shifts(tiles, lanes)
    extend(src, cpl, inverse, north, south, (col_first, col_second), shifts, raw, src_x, cpl_x)
    weights = [[mix[b, a] for a in range(nv)] for b in range(nv)]

    def sweep(number, t):
        last = number == SWEEPS
        count = lanes - 1 if last else lanes
        couple = [[cpl_x[(d,) + span(t, k)] for d in range(nc)] for k in range(count)]
        total = [[src_x[(a,) + span(t, k)] for a in range(nv)] for k in range(count)]
        for b in range(nv):
            old, lead = (src_x, (b,)) if number == 1 else (adj, (number - 2, b))
            around = shifts.around(old, lead, t, count)
            for k in range(count):
                terms = [couple[k][d] * around[k][d] for d in range(nc)]
                inc = (terms[0] + terms[1]) + (terms[2] + terms[3])
                total[k] = [total[k][a] + weights[b][a] * inc for a in range(nv)]
        for k in range(count):
            for a in range(nv):
                if last:
                    done[(a,) + span(t - EDGE // SUB, k)] = total[k][a]
                else:
                    adj[(number - 1, a) + span(t, k)] = total[k][a]

    def fold(x):
        parts = [x[:, k * LANE : (k + 1) * LANE] for k in range(cols // LANE)]
        return functools.reduce(jnp.add, parts)

    def joined(xs):
        return jnp.concatenate(xs, axis=1)

    def outer(x, d):
        return lax.dot_general(x, d, NT, preferred_element_type=F32)

    def backward(first):
        if first < half:
            acts, slopes, beta, start = acts_a, slopes_a, beta_a, first
        else:
            acts, slopes, beta, start = acts_b, slopes_b, beta_b, first - half
        here = slice(first, first + blk)
        sens = done[nv - 1, here] * prod[here] + REG_WEIGHT * (beta[start : start + blk] - 1.0)

        def layer(lo, high):
            return joined([acts[start + q, lo:high] for q in range(blk)])

        def add(ref, part):
            ref[...] = part if first == 0 else ref[...] + part

        def slanted(number, product, lo):
            total, out = jnp.zeros((hidden, LANE), F32), []
            for q in range(blk):
                d = product[:, q * cols : (q + 1) * cols] * slopes[start + q, lo : lo + hidden]
                total = total + fold(d)
                out.append(d.astype(BF16))
            add(sums.at[number], total)
            return joined(out)

        out_sum, sens_rows = jnp.zeros((hidden, LANE), F32), []
        for q in range(blk):
            sen = jnp.broadcast_to(sens[q : q + 1], (hidden, cols))
            out_sum = out_sum + fold(acts[start + q, 2 * hidden + 16 :].astype(F32) * sen)
            sens_rows.append(sen)
        add(sums.at[0], out_sum)
        d3 = slanted(3, joined(sens_rows), 2 * hidden)
        yield
        product = jnp.dot(wtop[...], d3, preferred_element_type=F32)
        yield
        d2 = slanted(2, product, hidden)
        add(g_top, outer(layer(hidden, 2 * hidden), d3))
        yield
        product = jnp.dot(wmid[...], d2, preferred_element_type=F32)
        yield
        d1 = slanted(1, product, 0)
        add(g_mid, outer(layer(0, hidden), d2))
        yield
        add(g_in, outer(d1, layer(2 * hidden, 2 * hidden + 16)))

    for number in range(1, SWEEPS):
        for t in range(SWEEPS + 1 - number):
            sweep(number, t)
    stages = iter(())
    for t in range(1, tiles - 1):
        for number in range(1, SWEEPS + 1):
            if t + SWEEPS - number < tiles:
                sweep(number, t + SWEEPS - number)
            next(stages, None)
        stages = backward((t - 1) * blk)
    copies[2].start()
    for _ in stages:
        pass

    turned = jnp.transpose(joined([g_in[...], jnp.zeros((hidden, LANE - 16), F32)]))
    tail = turned[SUB : 2 * SUB]
    row = lax.broadcasted_iota(jnp.int32, (SUB, hidden), 0)
    for k in range(4):
        line = jnp.sum(jnp.transpose(sums[k]), axis=0, keepdims=True)
        tail = tail + jnp.where(row == k + num_feat - SUB, jnp.broadcast_to(line, (SUB, hidden)), 0.0)
    packed[0:hidden, :] = joined([g_mid[...], g_top[...]])
    packed[hidden : hidden + SUB, :] = joined([turned[0:SUB], tail])
    for copy in copies:
        copy.wait()


def sweeps_and_backward(num_feat, source, coupling, inverse, production, betas, halos, weights, nets, mixing):
    nv, rows, cols = source.shape
    nc = coupling.shape[0]
    hidden = weights[0].shape[0]
    tall, wide = rows + 2 * EDGE, cols + LANE
    near, far = pl.BlockSpec(memory_space=pltpu.VMEM), pl.BlockSpec(memory_space=pltpu.HBM)
    operands = [source, coupling, inverse, production, *betas, *halos, *weights, *nets]
    return pl.pallas_call(
        functools.partial(adjoint_kernel, num_feat),
        in_specs=[near] * len(operands) + [pl.BlockSpec(memory_space=pltpu.SMEM)],
        out_specs=[near, far, far],
        out_shape=[
            pltpu.VMEM((hidden + SUB, LANE), F32),
            pltpu.HBM((nv, rows, cols), F32),
            pltpu.HBM((rows, cols), F32),
        ],
        scratch_shapes=[
            pltpu.VMEM((nv + nc + 1, tall, wide), F32),
            pltpu.VMEM((nv, tall, wide), F32),
            pltpu.VMEM((nc, tall, wide), F32),
            pltpu.VMEM((SWEEPS - 1, nv, tall, wide), F32),
            pltpu.VMEM((nv, rows, cols), F32),
            pltpu.VMEM((4, hidden, LANE), F32),
            pltpu.VMEM((hidden, hidden), F32),
            pltpu.VMEM((hidden, hidden), F32),
            pltpu.VMEM((hidden, 16), F32),
            pltpu.SemaphoreType.DMA((3,)),
        ],
        compiler_params=params(),
        name="sweeps_backward",
    )(*operands, mixing)


def clip_kernel(summed, gin, gmid, gtop, gout, gbias):
    hidden = gmid.shape[0]
    total = summed[...]
    squares = jnp.sum(jnp.sum(total * total, axis=0, keepdims=True), axis=1, keepdims=True)
    total = total * (CLIP_NORM / jnp.maximum(jnp.sqrt(squares), CLIP_NORM))
    gmid[...] = total[:hidden, :hidden]
    gtop[...] = total[:hidden, hidden:]
    low, high = total[hidden:, :hidden], total[hidden:, hidden:]
    gin[0:SUB] = low
    gin[SUB:] = high[: gin.shape[0] - SUB]
    at = gin.shape[0] - SUB
    gout[...] = high[at : at + 1]
    gbias[...] = high[at + 1 : at + 4]


def clip_all(summed, num_feat, hidden):
    shapes = [(num_feat, hidden), (hidden, hidden), (hidden, hidden), (1, hidden), (3, hidden)]
    return pl.pallas_call(
        clip_kernel,
        grid=(1,),
        in_specs=[whole(summed.shape)],
        out_specs=[whole(s) for s in shapes],
        out_shape=[jax.ShapeDtypeStruct(s, F32) for s in shapes],
        compiler_params=params(),
        name="clip",
    )(summed)


def sum_over_case(packed):
    for axis, radix in (("gy", 2), ("gx", 4)):
        count = lax.axis_size(axis)
        step = 1
        while step < count:
            parts = [packed]
            for k in range(1, min(radix, count // step)):
                parts.append(lax.ppermute(packed, axis, [(i, i ^ (k * step)) for i in range(count)]))
            while len(parts) > 1:
                parts = [a + b for a, b in zip(parts[::2], parts[1::2])]
            packed = parts[0]
            step *= radix
    return packed


def row_swaps(first, second):
    num_x, num_y = lax.axis_size("gx"), lax.axis_size("gy")
    out = []
    for start, slab in ((1, second), (0, first)):
        partner = {}
        for i in range(num_x):
            j = i + 1 if i % 2 == start else i - 1
            for y in range(num_y):
                if 0 <= j < num_x:
                    partner[i * num_y + y] = j * num_y + y
                elif num_y % 2 == 0:
                    partner[i * num_y + y] = i * num_y + (y ^ 1)
        out.append(lax.ppermute(slab, ("gx", "gy"), sorted(partner.items())))
    return out[::-1]


def col_swaps(first, second):
    count = lax.axis_size("gy")
    out = []
    for start, slab in ((0, first), (1, second)):
        low = [(i, i + 1) for i in range(start, count - 1, 2)]
        if count % 2 == 0 and start == 1:
            low.append((0, count - 1))
        out.append(lax.ppermute(slab, "gy", low + [(b, a) for a, b in low]))
    return out


def shards(
    features, source, coupling, diagonal, production, bc_code, mixing,
    weight_in, weight_mid, weight_top, weight_out, biases,
):
    num_feat, rows, _ = features.shape
    hidden = weight_mid.shape[0]
    loaded = load([
        source, coupling, diagonal, bc_code, production, features,
        weight_in, weight_mid, weight_top, weight_out.reshape(1, hidden), biases,
    ])
    source, coupling, _, _, production, features, weight_in, weight_mid, weight_top, wout, biases = loaded[:11]
    inverse, *row_slabs = loaded[11:]
    row_halos = row_swaps(*row_slabs)
    prepared = prepare(weight_in, weight_mid, weight_top, wout, biases)
    half = rows - 32
    *net_a, beta_a = forward(features, prepared, 0, half)
    *row_halos, beta_a = lax.optimization_barrier((*row_halos, beta_a))
    first, second, *row_halos = col_slabs(source, coupling, inverse, row_halos)
    col_halos = col_swaps(first, second)
    *net_b, beta_b = forward(features, prepared, half, rows - half)
    packed, adjoint, beta = sweeps_and_backward(
        num_feat, source, coupling, inverse, production, (beta_a, beta_b), (*row_halos, *col_halos),
        (weight_mid, weight_top), (*net_a, *net_b), mixing,
    )
    grad_in, grad_mid, grad_top, grad_out, grad_bias = clip_all(sum_over_case(packed), num_feat, hidden)
    return (adjoint, beta, grad_in, grad_mid, grad_top, grad_out.reshape(hidden), grad_bias)


def solution(mesh):
    cells3 = P(None, ("case", "gx"), "gy")
    cells2 = P(("case", "gx"), "gy")
    return jax.shard_map(
        shards,
        mesh=mesh,
        in_specs=(cells3,) * 3 + (cells2,) * 3 + (P(),) * 6,
        out_specs=(cells3, cells2, P("case"), P("case"), P("case"), P("case"), P("case")),
        check_vma=False,
    )
```

```python
import functools
import itertools

import jax
import jax.numpy as jnp
from jax import lax
from jax.experimental import pallas as pl
from jax.experimental.pallas import tpu as pltpu
from jax.sharding import PartitionSpec as P

SWEEPS = 6
WALL_EXTRA = 0.2
FAR_EXTRA = 0.6
REG_WEIGHT = 0.5
CLIP_NORM = 64.0
DEPTH = SWEEPS
EDGE = 8
SUB, LANE = 8, 128
F32, BF16 = jnp.float32, jnp.bfloat16
NT = (((1,), (1,)), ((), ()))
TN = (((0,), (0,)), ((), ()))
VMEM_BYTES = 16 * 1024 * 1024


def whole(shape):
    return pl.BlockSpec(shape, lambda *_: (0,) * len(shape))


def in_hbm(x):
    return pltpu.with_memory_space_constraint(x, pltpu.HBM)


def on_chip(kernel, operands, outs, scratch=(), far=(), far_outs=(), **kwargs):
    here, there = pl.BlockSpec(memory_space=pltpu.VMEM), pl.BlockSpec(memory_space=pltpu.HBM)
    return pl.pallas_call(
        kernel,
        in_specs=[here] * len(operands) + [there] * len(far),
        out_specs=[here] * len(outs) + [there] * len(far_outs),
        out_shape=[pltpu.VMEM(*o) for o in outs] + [pltpu.HBM(*o) for o in far_outs],
        scratch_shapes=list(scratch),
        compiler_params=params(),
        **kwargs,
    )(*operands, *[in_hbm(x) for x in far])


def like(x):
    return (x.shape, x.dtype)


def params():
    return pltpu.CompilerParams(vmem_limit_bytes=VMEM_BYTES)


def inverse_diag(diag, code):
    total = diag + jnp.where(code == 1, WALL_EXTRA, 0.0) + jnp.where(code == 2, FAR_EXTRA, 0.0)
    return 1.0 / total


def is_odd(axis):
    return lax.axis_index(axis) % 2 == 1


def load_kernel(count, *refs):
    far, near = refs[:count], refs[count : 2 * count]
    inv, second, first, sems = refs[2 * count :]
    copies = [pltpu.make_async_copy(far[k], near[k], sems.at[k]) for k in range(count)]
    for copy in copies:
        copy.start()
    src, cpl, dia, bc = near[:4]
    for copy in copies[:4]:
        copy.wait()
    nv, rows, _ = src.shape
    nc = cpl.shape[0]
    inv[...] = inverse_diag(dia[...], bc[...])
    odd = is_odd("gx")
    for f in range(nv + nc + 1):
        if f < nv + nc:
            ref, k = (src, f) if f < nv else (cpl, f - nv)
            top, bottom = ref[k, 0:16].astype(F32)[:DEPTH], ref[k, rows - 16 :].astype(F32)[16 - DEPTH :]
        else:
            top, bottom = inv[0:DEPTH], inv[rows - DEPTH :]
        first[f * DEPTH : (f + 1) * DEPTH] = jnp.where(odd, top, bottom)
        second[f * DEPTH : (f + 1) * DEPTH] = jnp.where(odd, bottom, top)
    for copy in copies[4:]:
        copy.wait()


def load(arrays):
    source, coupling = arrays[:2]
    nv, rows, cols = source.shape
    slab = (((nv + coupling.shape[0] + 1) * DEPTH, cols), F32)
    return on_chip(
        functools.partial(load_kernel, len(arrays)),
        [],
        [like(x) for x in arrays] + [((rows, cols), F32), slab, slab],
        [pltpu.SemaphoreType.DMA((len(arrays),))],
        far=arrays,
        name="load",
    )


def ordered(axis, first, second):
    odd, at = is_odd(axis), lax.axis_index(axis)
    before, after = jnp.where(odd, first, second), jnp.where(odd, second, first)
    return jnp.where(at == 0, 0.0, before), jnp.where(at == lax.axis_size(axis) - 1, 0.0, after)


def cols_kernel(src, cpl, inv, row_first, row_second, col_first, col_second, north, south):
    nv, rows, cols = src.shape
    nc = cpl.shape[0]
    half = col_first.shape[0]
    north[...] = jnp.zeros(north.shape, F32)
    south[...] = jnp.zeros(south.shape, F32)
    for f in range(nv + nc + 1):
        here = slice(f * DEPTH, (f + 1) * DEPTH)
        before, after = ordered("gx", row_first[here], row_second[here])
        north[f, EDGE - DEPTH :] = before
        south[f, 0:DEPTH] = after
    lane = lax.broadcasted_iota(jnp.int32, (half, LANE), 1)
    slabs = []
    for window, extra in ((slice(0, LANE), 0), (slice(cols - LANE, cols), DEPTH)):
        slab = jnp.zeros((half, LANE), F32)
        for f in range(nv + nc + 1):
            if f < nv:
                x = src[f, :, window].astype(F32)
            elif f < nv + nc:
                x = cpl[f - nv, :, window].astype(F32)
            else:
                x = inv[:, window]
            x = jnp.concatenate([north[f, :, window], x, south[f, :, window]], axis=0)
            for part, at in ((x[:half], DEPTH * f), (x[half:], DEPTH * f + LANE // 2)):
                own = jnp.logical_and(lane >= at, lane < at + DEPTH)
                slab = jnp.where(own, pltpu.roll(part, (at + extra) % LANE, 1), slab)
        slabs.append(slab)
    odd = is_odd("gy")
    col_first[...] = jnp.where(odd, slabs[0], slabs[1])
    col_second[...] = jnp.where(odd, slabs[1], slabs[0])


def col_slabs(source, coupling, inv, row_halos):
    nv, rows, cols = source.shape
    slab = (((rows + 2 * EDGE) // 2, LANE), F32)
    halo = ((nv + coupling.shape[0] + 1, EDGE, cols), F32)
    return on_chip(
        cols_kernel, [source, coupling, inv, *row_halos], [slab, slab, halo, halo], name="col_slabs"
    )


def column_of(row):
    hidden = row.shape[1]
    wide = jnp.concatenate([row, jnp.zeros((1, LANE - hidden), F32)], axis=1)
    return jnp.transpose(jnp.broadcast_to(wide, (LANE, LANE)))[:hidden]


def across(block, width):
    return jnp.concatenate([block] * (width // LANE), axis=1)


def weights_kernel(win, wmid, wtop, wout, bias, w1, w2, w3, cst):
    nf, hidden = win.shape
    step_rows, blk = hidden + 16, 16
    depth = w1.shape[1]
    feat_of = lax.broadcasted_iota(jnp.int32, (nf, depth), 1) // blk
    pick = (feat_of == lax.broadcasted_iota(jnp.int32, (nf, depth), 0)).astype(F32).astype(BF16)
    spread = lax.dot_general(win[...], pick, TN, preferred_element_type=F32)
    col = lax.broadcasted_iota(jnp.int32, (hidden, depth), 1)
    col_f = lax.broadcasted_iota(jnp.int32, (16, depth), 1)
    row_f = lax.broadcasted_iota(jnp.int32, (16, depth), 0)
    for r in range(blk):
        base = r * step_rows
        w1[base : base + hidden] = jnp.where(col % blk == r, spread, 0.0).astype(BF16)
        same = jnp.logical_and(col_f == row_f * blk + r, row_f < nf)
        w1[base + hidden : base + step_rows] = jnp.where(same, 1.0, 0.0).astype(BF16)
    w2[...] = jnp.transpose(wmid[...].astype(F32)).astype(BF16)
    w3[...] = jnp.transpose(wtop[...].astype(F32)).astype(BF16)
    for k in range(3):
        cst[k] = column_of(bias[k : k + 1, :])
    cst[3] = column_of(wout[...])


def prepare(weight_in, weight_mid, weight_top, weight_out, biases):
    nf, hidden = weight_in.shape
    depth = -(-nf * 16 // LANE) * LANE
    return on_chip(
        weights_kernel,
        [weight_in, weight_mid, weight_top, weight_out, biases],
        [
            ((16 * (hidden + 16), depth), BF16),
            ((hidden, hidden), BF16),
            ((hidden, hidden), BF16),
            ((4, hidden, LANE), F32),
        ],
        name="weights",
    )


def slope(act):
    return 1.0 - act * act


def forward_kernel(first_row, feat, w1, w2, w3, cst, acts, slopes, beta, x1):
    nf, _, cols = feat.shape
    hidden = w2.shape[0]
    step_rows, blk, per = hidden + 16, 16, 4
    x1[...] = jnp.zeros(x1.shape, BF16)

    @pl.loop(0, acts.shape[0] // blk)
    def _(block):
        start = pl.multiple_of(block * blk, blk)
        x1[0 : nf * blk] = feat[:, pl.ds(first_row + start, blk), :].reshape(nf * blk, cols)
        b1, b2, b3, wo = (across(cst[k], cols) for k in range(4))
        lines = []
        first = jnp.dot(w1[...], x1[...], preferred_element_type=F32)
        for g in range(blk // per):
            ones = []
            for q in range(g * per, (g + 1) * per):
                part = first[q * step_rows : (q + 1) * step_rows]
                one = jnp.tanh(part[:hidden] + b1).astype(BF16)
                slopes[start + q, 0:hidden] = slope(one.astype(F32))
                acts[start + q, 0:hidden] = one
                acts[start + q, 2 * hidden : 2 * hidden + 16] = part[hidden:].astype(BF16)
                ones.append(one)
            second = jnp.dot(w2[...], jnp.concatenate(ones, axis=1), preferred_element_type=F32)
            twos = []
            for q in range(per):
                two = jnp.tanh(second[:, q * cols : (q + 1) * cols] + b2).astype(BF16)
                slopes[start + (g * per + q), hidden : 2 * hidden] = slope(two.astype(F32))
                acts[start + (g * per + q), hidden : 2 * hidden] = two
                twos.append(two)
            third = jnp.dot(w3[...], jnp.concatenate(twos, axis=1), preferred_element_type=F32)
            for q in range(per):
                three = jnp.tanh(third[:, q * cols : (q + 1) * cols] + b3).astype(BF16)
                acts[start + (g * per + q), 2 * hidden + 16 :] = three
                three = three.astype(F32)
                slopes[start + (g * per + q), 2 * hidden :] = wo * slope(three)
                lines.append(1.0 + jnp.sum(three * wo, axis=0, keepdims=True))
        beta[pl.ds(start, blk), :] = jnp.concatenate(lines, axis=0)


def forward(features, prepared, first_row, count):
    nf, _, cols = features.shape
    w1, w2 = prepared[:2]
    hidden = w2.shape[0]
    high = 3 * hidden + 16
    return on_chip(
        functools.partial(forward_kernel, first_row),
        [features, *prepared],
        [((count, high, cols), BF16), ((count, 3 * hidden, cols), F32), ((count, cols), F32)],
        [pltpu.VMEM((w1.shape[1], cols), BF16)],
        cost_estimate=pl.CostEstimate(
            flops=2 * count * cols * (nf + 2 * hidden) * hidden,
            bytes_accessed=2 * count * cols * (high + nf),
            transcendentals=3 * count * cols * hidden,
        ),
        name="network_forward",
    )


def span(t, k):
    return (slice(t * SUB, (t + 1) * SUB), slice(k * LANE, (k + 1) * LANE))


class Shifts:
    def __init__(self, tiles, lanes):
        self.tiles, self.lanes = tiles, lanes
        sub = lax.broadcasted_iota(jnp.int32, (SUB, LANE), 0)
        lane = lax.broadcasted_iota(jnp.int32, (SUB, LANE), 1)
        self.first_sub, self.last_sub = sub == 0, sub == SUB - 1
        self.first_lane, self.last_lane = lane == 0, lane == LANE - 1

    def row(self, ref, lead, t):
        t = min(max(t, 0), self.tiles - 1)
        return [ref[lead + span(t, k)] for k in range(self.lanes)]

    def above(self, rows, k):
        return pltpu.roll(jnp.where(self.last_sub, rows[0][k], rows[1][k]), 1, 0)

    def below(self, rows, k):
        return pltpu.roll(jnp.where(self.first_sub, rows[2][k], rows[1][k]), SUB - 1, 0)

    def left(self, rows, k):
        return pltpu.roll(jnp.where(self.last_lane, rows[1][(k - 1) % self.lanes], rows[1][k]), 1, 1)

    def right(self, rows, k):
        other = rows[1][(k + 1) % self.lanes]
        return pltpu.roll(jnp.where(self.first_lane, other, rows[1][k]), LANE - 1, 1)

    def around(self, ref, lead, t, k_count):
        rows = [self.row(ref, lead, t + o) for o in (-1, 0, 1)]
        moves = (self.above, self.below, self.left, self.right)
        return [[move(rows, k) for move in moves] for k in range(k_count)]


def extend(src, cpl, inverse, north, south, col_halos, shifts, raw, src_x, cpl_x):
    nv, rows, cols = src.shape
    nc = cpl.shape[0]
    tall = rows + 2 * EDGE
    inner = slice(EDGE, EDGE + rows)
    lane = lax.broadcasted_iota(jnp.int32, (tall, LANE), 1)
    from_east, from_west = lane < DEPTH, lane >= LANE - DEPTH
    west, east = ordered("gy", *(x[...] for x in col_halos))
    for f in range(nv + nc + 1):
        if f < nv:
            raw[f, inner, 0:cols] = src[f].astype(F32)
        elif f < nv + nc:
            raw[f, inner, 0:cols] = cpl[f - nv].astype(F32)
        else:
            raw[f, inner, 0:cols] = inverse[...]
        raw[f, 0:EDGE, 0:cols] = north[f]
        raw[f, EDGE + rows :, 0:cols] = south[f]
        low, high = (-DEPTH * f) % LANE, (LANE // 2 - DEPTH * f) % LANE
        e = jnp.concatenate([pltpu.roll(east, at, 1) for at in (low, high)], axis=0)
        w = jnp.concatenate([pltpu.roll(west, (at - DEPTH) % LANE, 1) for at in (low, high)], axis=0)
        raw[f, :, cols:] = jnp.where(from_east, e, jnp.where(from_west, w, 0.0))
    for t in range(shifts.tiles):
        inv = shifts.row(raw, (nv + nc,), t)
        for k in range(shifts.lanes):
            for v in range(nv):
                src_x[(v,) + span(t, k)] = inv[k] * raw[(v,) + span(t, k)]
        for d, move in enumerate((shifts.above, shifts.below, shifts.left, shifts.right)):
            rows_d = [shifts.row(raw, (nv + d,), t + o) for o in (-1, 0, 1)]
            for k in range(shifts.lanes):
                cpl_x[(d,) + span(t, k)] = inv[k] * move(rows_d, k)


def adjoint_kernel(
    num_feat, src, cpl, inverse, prod, beta_a, beta_b, north, south, col_first, col_second,
    wmid, wtop, acts_a, slopes_a, acts_b, slopes_b, mix,
    packed, adj_out, beta_out,
    raw, src_x, cpl_x, adj, done, sums, g_mid, g_top, g_in, sems,
):
    nv, rows, cols = src.shape
    nc = cpl.shape[0]
    hidden, blk = wmid.shape[0], SUB
    half = beta_a.shape[0]
    tiles, lanes = (rows + 2 * EDGE) // SUB, cols // LANE + 1
    copies = [
        pltpu.make_async_copy(beta_a, beta_out.at[0:half], sems.at[0]),
        pltpu.make_async_copy(beta_b, beta_out.at[half:rows], sems.at[1]),
        pltpu.make_async_copy(done, adj_out, sems.at[2]),
    ]
    copies[0].start()
    copies[1].start()
    shifts = Shifts(tiles, lanes)
    extend(src, cpl, inverse, north, south, (col_first, col_second), shifts, raw, src_x, cpl_x)
    weights = [[mix[b, a] for a in range(nv)] for b in range(nv)]

    def sweep(number, t):
        last = number == SWEEPS
        count = lanes - 1 if last else lanes
        couple = [[cpl_x[(d,) + span(t, k)] for d in range(nc)] for k in range(count)]
        total = [[src_x[(a,) + span(t, k)] for a in range(nv)] for k in range(count)]
        for b in range(nv):
            old, lead = (src_x, (b,)) if number == 1 else (adj, (number - 2, b))
            around = shifts.around(old, lead, t, count)
            for k in range(count):
                terms = [couple[k][d] * around[k][d] for d in range(nc)]
                inc = (terms[0] + terms[1]) + (terms[2] + terms[3])
                total[k] = [total[k][a] + weights[b][a] * inc for a in range(nv)]
            yield
        for k in range(count):
            for a in range(nv):
                if last:
                    done[(a,) + span(t - EDGE // SUB, k)] = total[k][a]
                else:
                    adj[(number - 1, a) + span(t, k)] = total[k][a]

    def fold(x):
        parts = [x[:, k * LANE : (k + 1) * LANE] for k in range(cols // LANE)]
        return functools.reduce(jnp.add, parts)

    def joined(xs):
        return jnp.concatenate(xs, axis=1)

    def outer(x, d):
        return lax.dot_general(x, d, NT, preferred_element_type=F32)

    def backward(first):
        if first < half:
            acts, slopes, beta, start = acts_a, slopes_a, beta_a, first
        else:
            acts, slopes, beta, start = acts_b, slopes_b, beta_b, first - half
        here = slice(first, first + blk)
        sens = done[nv - 1, here] * prod[here] + REG_WEIGHT * (beta[start : start + blk] - 1.0)

        def layer(lo, high):
            return joined([acts[start + q, lo:high] for q in range(blk)])

        def add(ref, part):
            ref[...] = part if first == 0 else ref[...] + part

        def slanted(number, product, lo, out):
            total = jnp.zeros((hidden, LANE), F32)
            for q in range(blk):
                d = product[:, q * cols : (q + 1) * cols] * slopes[start + q, lo : lo + hidden]
                total = total + fold(d)
                out.append(d.astype(BF16))
                yield
            add(sums.at[number], total)

        out_sum, sens_rows, d3, d2, d1 = jnp.zeros((hidden, LANE), F32), [], [], [], []
        for q in range(blk):
            sen = jnp.broadcast_to(sens[q : q + 1], (hidden, cols))
            out_sum = out_sum + fold(acts[start + q, 2 * hidden + 16 :].astype(F32) * sen)
            sens_rows.append(sen)
            yield
        add(sums.at[0], out_sum)
        yield from slanted(3, joined(sens_rows), 2 * hidden, d3)
        d3 = joined(d3)
        product = jnp.dot(wtop[...], d3, preferred_element_type=F32)
        yield
        add(g_top, outer(layer(hidden, 2 * hidden), d3))
        yield
        yield from slanted(2, product, hidden, d2)
        d2 = joined(d2)
        product = jnp.dot(wmid[...], d2, preferred_element_type=F32)
        yield
        add(g_mid, outer(layer(0, hidden), d2))
        yield
        yield from slanted(1, product, 0, d1)
        add(g_in, outer(joined(d1), layer(2 * hidden, 2 * hidden + 16)))

    backward_turns = 4 * blk + 4

    def together(sweeps, back):
        turns = max(nv * len(sweeps), 1)
        sweeps = itertools.chain(*(sweep(*x) for x in sweeps))
        for turn in range(turns):
            next(sweeps, None)
            for _ in range(backward_turns * turn // turns, backward_turns * (turn + 1) // turns):
                next(back, None)
        for _ in itertools.chain(sweeps, back):
            pass

    ahead = [2 * (SWEEPS - number) for number in range(SWEEPS + 1)]
    for number in range(1, SWEEPS):
        together([(number, t) for t in range(min(ahead[number] + 1, tiles))], iter(()))
    for t in range(1, tiles - 1):
        step = [(n, t + ahead[n]) for n in range(1, SWEEPS + 1) if t + ahead[n] < tiles]
        together(step, backward((t - 2) * blk) if t > 1 else iter(()))
    copies[2].start()
    together([], backward(rows - blk))

    turned = jnp.transpose(joined([g_in[...], jnp.zeros((hidden, LANE - 16), F32)]))
    tail = turned[SUB : 2 * SUB]
    row = lax.broadcasted_iota(jnp.int32, (SUB, hidden), 0)
    for k in range(4):
        line = jnp.sum(jnp.transpose(sums[k]), axis=0, keepdims=True)
        tail = tail + jnp.where(row == k + num_feat - SUB, jnp.broadcast_to(line, (SUB, hidden)), 0.0)
    packed[0:hidden, :] = joined([g_mid[...], g_top[...]])
    packed[hidden : hidden + SUB, :] = joined([turned[0:SUB], tail])
    for copy in copies:
        copy.wait()


def sweeps_and_backward(num_feat, source, coupling, inverse, production, betas, halos, weights, nets, mixing):
    nv, rows, cols = source.shape
    nc = coupling.shape[0]
    hidden = weights[0].shape[0]
    tall, wide = rows + 2 * EDGE, cols + LANE
    near, far = pl.BlockSpec(memory_space=pltpu.VMEM), pl.BlockSpec(memory_space=pltpu.HBM)
    operands = [source, coupling, inverse, production, *betas, *halos, *weights, *nets]
    return pl.pallas_call(
        functools.partial(adjoint_kernel, num_feat),
        in_specs=[near] * len(operands) + [pl.BlockSpec(memory_space=pltpu.SMEM)],
        out_specs=[near, far, far],
        out_shape=[
            pltpu.VMEM((hidden + SUB, LANE), F32),
            pltpu.HBM((nv, rows, cols), F32),
            pltpu.HBM((rows, cols), F32),
        ],
        scratch_shapes=[
            pltpu.VMEM((nv + nc + 1, tall, wide), F32),
            pltpu.VMEM((nv, tall, wide), F32),
            pltpu.VMEM((nc, tall, wide), F32),
            pltpu.VMEM((SWEEPS - 1, nv, tall, wide), F32),
            pltpu.VMEM((nv, rows, cols), F32),
            pltpu.VMEM((4, hidden, LANE), F32),
            pltpu.VMEM((hidden, hidden), F32),
            pltpu.VMEM((hidden, hidden), F32),
            pltpu.VMEM((hidden, 16), F32),
            pltpu.SemaphoreType.DMA((3,)),
        ],
        compiler_params=params(),
        name="sweeps_backward",
    )(*operands, mixing)


def clip_kernel(summed, gin, gmid, gtop, gout, gbias):
    hidden = gmid.shape[0]
    total = summed[...]
    squares = jnp.sum(jnp.sum(total * total, axis=0, keepdims=True), axis=1, keepdims=True)
    total = total * (CLIP_NORM / jnp.maximum(jnp.sqrt(squares), CLIP_NORM))
    gmid[...] = total[:hidden, :hidden]
    gtop[...] = total[:hidden, hidden:]
    low, high = total[hidden:, :hidden], total[hidden:, hidden:]
    gin[0:SUB] = low
    gin[SUB:] = high[: gin.shape[0] - SUB]
    at = gin.shape[0] - SUB
    gout[...] = high[at : at + 1]
    gbias[...] = high[at + 1 : at + 4]


def clip_all(summed, num_feat, hidden):
    shapes = [(num_feat, hidden), (hidden, hidden), (hidden, hidden), (1, hidden), (3, hidden)]
    return pl.pallas_call(
        clip_kernel,
        grid=(1,),
        in_specs=[whole(summed.shape)],
        out_specs=[whole(s) for s in shapes],
        out_shape=[jax.ShapeDtypeStruct(s, F32) for s in shapes],
        compiler_params=params(),
        name="clip",
    )(summed)


def sum_over_case(packed):
    for axis, radix in (("gy", 2), ("gx", 4)):
        count = lax.axis_size(axis)
        step = 1
        while step < count:
            parts = [packed]
            for k in range(1, min(radix, count // step)):
                parts.append(lax.ppermute(packed, axis, [(i, i ^ (k * step)) for i in range(count)]))
            while len(parts) > 1:
                parts = [a + b for a, b in zip(parts[::2], parts[1::2])]
            packed = parts[0]
            step *= radix
    return packed


def row_swaps(first, second):
    num_x, num_y = lax.axis_size("gx"), lax.axis_size("gy")
    out = []
    for start, slab in ((1, second), (0, first)):
        partner = {}
        for i in range(num_x):
            j = i + 1 if i % 2 == start else i - 1
            for y in range(num_y):
                if 0 <= j < num_x:
                    partner[i * num_y + y] = j * num_y + y
                elif num_y % 2 == 0:
                    partner[i * num_y + y] = i * num_y + (y ^ 1)
        out.append(lax.ppermute(slab, ("gx", "gy"), sorted(partner.items())))
    return out[::-1]


def col_swaps(first, second):
    count = lax.axis_size("gy")
    out = []
    for start, slab in ((0, first), (1, second)):
        low = [(i, i + 1) for i in range(start, count - 1, 2)]
        if count % 2 == 0 and start == 1:
            low.append((0, count - 1))
        out.append(lax.ppermute(slab, "gy", low + [(b, a) for a, b in low]))
    return out


def shards(
    features, source, coupling, diagonal, production, bc_code, mixing,
    weight_in, weight_mid, weight_top, weight_out, biases,
):
    num_feat, rows, _ = features.shape
    hidden = weight_mid.shape[0]
    loaded = load([
        source, coupling, diagonal, bc_code, production, features,
        weight_in, weight_mid, weight_top, weight_out.reshape(1, hidden), biases,
    ])
    source, coupling, _, _, production, features, weight_in, weight_mid, weight_top, wout, biases = loaded[:11]
    inverse, second, first = loaded[11:]
    row_halos = row_swaps(first, second)
    prepared = prepare(weight_in, weight_mid, weight_top, wout, biases)
    half = rows - 32
    *net_a, beta_a = forward(features, prepared, 0, half)
    *row_halos, beta_a = lax.optimization_barrier((*row_halos, beta_a))
    first, second, *row_halos = col_slabs(source, coupling, inverse, row_halos)
    col_halos = col_swaps(first, second)
    *net_b, beta_b = forward(features, prepared, half, rows - half)
    packed, adjoint, beta = sweeps_and_backward(
        num_feat, source, coupling, inverse, production, (beta_a, beta_b), (*row_halos, *col_halos),
        (weight_mid, weight_top), (*net_a, *net_b), mixing,
    )
    grad_in, grad_mid, grad_top, grad_out, grad_bias = clip_all(sum_over_case(packed), num_feat, hidden)
    return (adjoint, beta, grad_in, grad_mid, grad_top, grad_out.reshape(hidden), grad_bias)


def solution(mesh):
    cells3 = P(None, ("case", "gx"), "gy")
    cells2 = P(("case", "gx"), "gy")
    return jax.shard_map(
        shards,
        mesh=mesh,
        in_specs=(cells3,) * 3 + (cells2,) * 3 + (P(),) * 6,
        out_specs=(cells3, cells2, P("case"), P("case"), P("case"), P("case"), P("case")),
        check_vma=False,
    )
```

```python
import functools
import itertools

import jax
import jax.numpy as jnp
from jax import lax
from jax.experimental import pallas as pl
from jax.experimental.pallas import tpu as pltpu
from jax.sharding import PartitionSpec as P

SWEEPS = 6
WALL_EXTRA = 0.2
FAR_EXTRA = 0.6
REG_WEIGHT = 0.5
CLIP_NORM = 64.0
DEPTH = SWEEPS
EDGE = 8
SUB, LANE = 8, 128
F32, BF16 = jnp.float32, jnp.bfloat16
NT = (((1,), (1,)), ((), ()))
TN = (((0,), (0,)), ((), ()))
VMEM_BYTES = 16 * 1024 * 1024


def whole(shape):
    return pl.BlockSpec(shape, lambda *_: (0,) * len(shape))


def in_hbm(x):
    return pltpu.with_memory_space_constraint(x, pltpu.HBM)


def on_chip(kernel, operands, outs, scratch=(), far=(), far_outs=(), **kwargs):
    here, there = pl.BlockSpec(memory_space=pltpu.VMEM), pl.BlockSpec(memory_space=pltpu.HBM)
    return pl.pallas_call(
        kernel,
        in_specs=[here] * len(operands) + [there] * len(far),
        out_specs=[here] * len(outs) + [there] * len(far_outs),
        out_shape=[pltpu.VMEM(*o) for o in outs] + [pltpu.HBM(*o) for o in far_outs],
        scratch_shapes=list(scratch),
        compiler_params=params(),
        **kwargs,
    )(*operands, *[in_hbm(x) for x in far])


def like(x):
    return (x.shape, x.dtype)


def params():
    return pltpu.CompilerParams(vmem_limit_bytes=VMEM_BYTES)


def inverse_diag(diag, code):
    total = diag + jnp.where(code == 1, WALL_EXTRA, 0.0) + jnp.where(code == 2, FAR_EXTRA, 0.0)
    return 1.0 / total


def is_odd(axis):
    return lax.axis_index(axis) % 2 == 1


def load_kernel(count, *refs):
    far, near = refs[:count], refs[count : 2 * count]
    inv, second, first, sems = refs[2 * count :]
    copies = [pltpu.make_async_copy(far[k], near[k], sems.at[k]) for k in range(count)]
    for copy in copies:
        copy.start()
    src, cpl, dia, bc = near[:4]
    for copy in copies[:4]:
        copy.wait()
    nv, rows, _ = src.shape
    nc = cpl.shape[0]
    inv[...] = inverse_diag(dia[...], bc[...])
    odd = is_odd("gx")
    for f in range(nv + nc + 1):
        if f < nv + nc:
            ref, k = (src, f) if f < nv else (cpl, f - nv)
            top, bottom = ref[k, 0:16].astype(F32)[:DEPTH], ref[k, rows - 16 :].astype(F32)[16 - DEPTH :]
        else:
            top, bottom = inv[0:DEPTH], inv[rows - DEPTH :]
        first[f * DEPTH : (f + 1) * DEPTH] = jnp.where(odd, top, bottom)
        second[f * DEPTH : (f + 1) * DEPTH] = jnp.where(odd, bottom, top)
    for copy in copies[4:]:
        copy.wait()


def load(arrays):
    source, coupling = arrays[:2]
    nv, rows, cols = source.shape
    slab = (((nv + coupling.shape[0] + 1) * DEPTH, cols), F32)
    return on_chip(
        functools.partial(load_kernel, len(arrays)),
        [],
        [like(x) for x in arrays] + [((rows, cols), F32), slab, slab],
        [pltpu.SemaphoreType.DMA((len(arrays),))],
        far=arrays,
        name="load",
    )


def ordered(axis, first, second):
    odd, at = is_odd(axis), lax.axis_index(axis)
    before, after = jnp.where(odd, first, second), jnp.where(odd, second, first)
    return jnp.where(at == 0, 0.0, before), jnp.where(at == lax.axis_size(axis) - 1, 0.0, after)


def cols_kernel(src, cpl, inv, row_first, row_second, col_first, col_second, north, south):
    nv, rows, cols = src.shape
    nc = cpl.shape[0]
    half = col_first.shape[0]
    north[...] = jnp.zeros(north.shape, F32)
    south[...] = jnp.zeros(south.shape, F32)
    for f in range(nv + nc + 1):
        here = slice(f * DEPTH, (f + 1) * DEPTH)
        before, after = ordered("gx", row_first[here], row_second[here])
        north[f, EDGE - DEPTH :] = before
        south[f, 0:DEPTH] = after
    lane = lax.broadcasted_iota(jnp.int32, (half, LANE), 1)
    slabs = []
    for window, extra in ((slice(0, LANE), 0), (slice(cols - LANE, cols), DEPTH)):
        slab = jnp.zeros((half, LANE), F32)
        for f in range(nv + nc + 1):
            if f < nv:
                x = src[f, :, window].astype(F32)
            elif f < nv + nc:
                x = cpl[f - nv, :, window].astype(F32)
            else:
                x = inv[:, window]
            x = jnp.concatenate([north[f, :, window], x, south[f, :, window]], axis=0)
            for part, at in ((x[:half], DEPTH * f), (x[half:], DEPTH * f + LANE // 2)):
                own = jnp.logical_and(lane >= at, lane < at + DEPTH)
                slab = jnp.where(own, pltpu.roll(part, (at + extra) % LANE, 1), slab)
        slabs.append(slab)
    odd = is_odd("gy")
    col_first[...] = jnp.where(odd, slabs[0], slabs[1])
    col_second[...] = jnp.where(odd, slabs[1], slabs[0])


def col_slabs(source, coupling, inv, row_halos):
    nv, rows, cols = source.shape
    slab = (((rows + 2 * EDGE) // 2, LANE), F32)
    halo = ((nv + coupling.shape[0] + 1, EDGE, cols), F32)
    return on_chip(
        cols_kernel, [source, coupling, inv, *row_halos], [slab, slab, halo, halo], name="col_slabs"
    )


def column_of(row):
    hidden = row.shape[1]
    wide = jnp.concatenate([row, jnp.zeros((1, LANE - hidden), F32)], axis=1)
    return jnp.transpose(jnp.broadcast_to(wide, (LANE, LANE)))[:hidden]


def across(block, width):
    return jnp.concatenate([block] * (width // LANE), axis=1)


def weights_kernel(win, wmid, wtop, wout, bias, w1, w2, w3, cst):
    nf, hidden = win.shape
    step_rows, blk = hidden + 16, 16
    depth = w1.shape[1]
    feat_of = lax.broadcasted_iota(jnp.int32, (nf, depth), 1) // blk
    pick = (feat_of == lax.broadcasted_iota(jnp.int32, (nf, depth), 0)).astype(F32).astype(BF16)
    spread = lax.dot_general(win[...], pick, TN, preferred_element_type=F32)
    col = lax.broadcasted_iota(jnp.int32, (hidden, depth), 1)
    col_f = lax.broadcasted_iota(jnp.int32, (16, depth), 1)
    row_f = lax.broadcasted_iota(jnp.int32, (16, depth), 0)
    for r in range(blk):
        base = r * step_rows
        w1[base : base + hidden] = jnp.where(col % blk == r, spread, 0.0).astype(BF16)
        same = jnp.logical_and(col_f == row_f * blk + r, row_f < nf)
        w1[base + hidden : base + step_rows] = jnp.where(same, 1.0, 0.0).astype(BF16)
    w2[...] = jnp.transpose(wmid[...].astype(F32)).astype(BF16)
    w3[...] = jnp.transpose(wtop[...].astype(F32)).astype(BF16)
    for k in range(3):
        cst[k] = column_of(bias[k : k + 1, :])
    cst[3] = column_of(wout[...])


def prepare(weight_in, weight_mid, weight_top, weight_out, biases):
    nf, hidden = weight_in.shape
    depth = -(-nf * 16 // LANE) * LANE
    return on_chip(
        weights_kernel,
        [weight_in, weight_mid, weight_top, weight_out, biases],
        [
            ((16 * (hidden + 16), depth), BF16),
            ((hidden, hidden), BF16),
            ((hidden, hidden), BF16),
            ((4, hidden, LANE), F32),
        ],
        name="weights",
    )


def slope(act):
    return 1.0 - act * act


def forward_kernel(first_row, feat, w1, w2, w3, cst, acts, turned, slopes, beta, x1):
    nf, _, cols = feat.shape
    hidden = w2.shape[0]
    step_rows, blk, per = hidden + 16, 16, 4
    x1[...] = jnp.zeros(x1.shape, BF16)

    @pl.loop(0, acts.shape[0] // blk)
    def _(block):
        start = pl.multiple_of(block * blk, blk)
        x1[0 : nf * blk] = feat[:, pl.ds(first_row + start, blk), :].reshape(nf * blk, cols)
        b1, b2, b3, wo = (across(cst[k], cols) for k in range(4))
        lines = []
        first = jnp.dot(w1[...], x1[...], preferred_element_type=F32)
        for g in range(blk // per):
            ones = []
            for q in range(g * per, (g + 1) * per):
                part = first[q * step_rows : (q + 1) * step_rows]
                one = jnp.tanh(part[:hidden] + b1).astype(BF16)
                slopes[start + q, 0:hidden] = slope(one.astype(F32))
                acts[start + q, 0:16] = part[hidden:].astype(BF16)
                ones.append(one)
            second = jnp.dot(w2[...], jnp.concatenate(ones, axis=1), preferred_element_type=F32)
            twos = []
            for q in range(per):
                two = jnp.tanh(second[:, q * cols : (q + 1) * cols] + b2).astype(BF16)
                slopes[start + (g * per + q), hidden : 2 * hidden] = slope(two.astype(F32))
                turned[start + (g * per + q)] = jnp.transpose(jnp.concatenate([ones[q], two], axis=0))
                twos.append(two)
            third = jnp.dot(w3[...], jnp.concatenate(twos, axis=1), preferred_element_type=F32)
            for q in range(per):
                three = jnp.tanh(third[:, q * cols : (q + 1) * cols] + b3).astype(BF16)
                acts[start + (g * per + q), 16:] = three
                three = three.astype(F32)
                slopes[start + (g * per + q), 2 * hidden :] = wo * slope(three)
                lines.append(1.0 + jnp.sum(three * wo, axis=0, keepdims=True))
        beta[pl.ds(start, blk), :] = jnp.concatenate(lines, axis=0)


def forward(features, prepared, first_row, count):
    nf, _, cols = features.shape
    w1, w2 = prepared[:2]
    hidden = w2.shape[0]
    high = hidden + 16
    return on_chip(
        functools.partial(forward_kernel, first_row),
        [features, *prepared],
        [
            ((count, high, cols), BF16),
            ((count, cols, 2 * hidden), BF16),
            ((count, 3 * hidden, cols), F32),
            ((count, cols), F32),
        ],
        [pltpu.VMEM((w1.shape[1], cols), BF16)],
        cost_estimate=pl.CostEstimate(
            flops=2 * count * cols * (nf + 2 * hidden) * hidden,
            bytes_accessed=2 * count * cols * (high + nf),
            transcendentals=3 * count * cols * hidden,
        ),
        name="network_forward",
    )


def span(t, k):
    return (slice(t * SUB, (t + 1) * SUB), slice(k * LANE, (k + 1) * LANE))


class Shifts:
    def __init__(self, tiles, lanes):
        self.tiles, self.lanes = tiles, lanes
        sub = lax.broadcasted_iota(jnp.int32, (SUB, LANE), 0)
        lane = lax.broadcasted_iota(jnp.int32, (SUB, LANE), 1)
        self.first_sub, self.last_sub = sub == 0, sub == SUB - 1
        self.first_lane, self.last_lane = lane == 0, lane == LANE - 1

    def row(self, ref, lead, t):
        t = min(max(t, 0), self.tiles - 1)
        return [ref[lead + span(t, k)] for k in range(self.lanes)]

    def above(self, rows, k):
        return pltpu.roll(jnp.where(self.last_sub, rows[0][k], rows[1][k]), 1, 0)

    def below(self, rows, k):
        return pltpu.roll(jnp.where(self.first_sub, rows[2][k], rows[1][k]), SUB - 1, 0)

    def left(self, rows, k):
        return pltpu.roll(jnp.where(self.last_lane, rows[1][(k - 1) % self.lanes], rows[1][k]), 1, 1)

    def right(self, rows, k):
        other = rows[1][(k + 1) % self.lanes]
        return pltpu.roll(jnp.where(self.first_lane, other, rows[1][k]), LANE - 1, 1)

    def around(self, ref, lead, t, k_count):
        rows = [self.row(ref, lead, t + o) for o in (-1, 0, 1)]
        moves = (self.above, self.below, self.left, self.right)
        return [[move(rows, k) for move in moves] for k in range(k_count)]


def extend(src, cpl, inverse, north, south, col_halos, shifts, raw, src_x, cpl_x):
    nv, rows, cols = src.shape
    nc = cpl.shape[0]
    tall = rows + 2 * EDGE
    inner = slice(EDGE, EDGE + rows)
    lane = lax.broadcasted_iota(jnp.int32, (tall, LANE), 1)
    from_east, from_west = lane < DEPTH, lane >= LANE - DEPTH
    west, east = ordered("gy", *(x[...] for x in col_halos))
    for f in range(nv + nc + 1):
        if f < nv:
            raw[f, inner, 0:cols] = src[f].astype(F32)
        elif f < nv + nc:
            raw[f, inner, 0:cols] = cpl[f - nv].astype(F32)
        else:
            raw[f, inner, 0:cols] = inverse[...]
        raw[f, 0:EDGE, 0:cols] = north[f]
        raw[f, EDGE + rows :, 0:cols] = south[f]
        low, high = (-DEPTH * f) % LANE, (LANE // 2 - DEPTH * f) % LANE
        e = jnp.concatenate([pltpu.roll(east, at, 1) for at in (low, high)], axis=0)
        w = jnp.concatenate([pltpu.roll(west, (at - DEPTH) % LANE, 1) for at in (low, high)], axis=0)
        raw[f, :, cols:] = jnp.where(from_east, e, jnp.where(from_west, w, 0.0))
    for t in range(shifts.tiles):
        inv = shifts.row(raw, (nv + nc,), t)
        for k in range(shifts.lanes):
            for v in range(nv):
                src_x[(v,) + span(t, k)] = inv[k] * raw[(v,) + span(t, k)]
        for d, move in enumerate((shifts.above, shifts.below, shifts.left, shifts.right)):
            rows_d = [shifts.row(raw, (nv + d,), t + o) for o in (-1, 0, 1)]
            for k in range(shifts.lanes):
                cpl_x[(d,) + span(t, k)] = inv[k] * move(rows_d, k)


def adjoint_kernel(
    num_feat, src, cpl, inverse, prod, beta_a, beta_b, north, south, col_first, col_second,
    wmid, wtop, acts_a, turned_a, slopes_a, acts_b, turned_b, slopes_b, mix,
    packed, adj_out, beta_out,
    raw, src_x, cpl_x, adj, done, sums, g_two, g_in, sems,
):
    nv, rows, cols = src.shape
    nc = cpl.shape[0]
    hidden, blk = wmid.shape[0], SUB
    half = beta_a.shape[0]
    tiles, lanes = (rows + 2 * EDGE) // SUB, cols // LANE + 1
    copies = [
        pltpu.make_async_copy(beta_a, beta_out.at[0:half], sems.at[0]),
        pltpu.make_async_copy(beta_b, beta_out.at[half:rows], sems.at[1]),
        pltpu.make_async_copy(done, adj_out, sems.at[2]),
    ]
    copies[0].start()
    copies[1].start()
    shifts = Shifts(tiles, lanes)
    extend(src, cpl, inverse, north, south, (col_first, col_second), shifts, raw, src_x, cpl_x)
    weights = [[mix[b, a] for a in range(nv)] for b in range(nv)]

    def sweep(number, t):
        last = number == SWEEPS
        count = lanes - 1 if last else lanes
        couple = [[cpl_x[(d,) + span(t, k)] for d in range(nc)] for k in range(count)]
        total = [[src_x[(a,) + span(t, k)] for a in range(nv)] for k in range(count)]
        for b in range(nv):
            old, lead = (src_x, (b,)) if number == 1 else (adj, (number - 2, b))
            around = shifts.around(old, lead, t, count)
            for k in range(count):
                terms = [couple[k][d] * around[k][d] for d in range(nc)]
                inc = (terms[0] + terms[1]) + (terms[2] + terms[3])
                total[k] = [total[k][a] + weights[b][a] * inc for a in range(nv)]
            yield
        for k in range(count):
            for a in range(nv):
                if last:
                    done[(a,) + span(t - EDGE // SUB, k)] = total[k][a]
                else:
                    adj[(number - 1, a) + span(t, k)] = total[k][a]

    def fold(x):
        parts = [x[:, k * LANE : (k + 1) * LANE] for k in range(cols // LANE)]
        return functools.reduce(jnp.add, parts)

    def joined(xs):
        return jnp.concatenate(xs, axis=1)

    def outer(x, d):
        return lax.dot_general(x, d, NT, preferred_element_type=F32)

    def backward(first):
        if first < half:
            acts, turned, slopes, beta, start = acts_a, turned_a, slopes_a, beta_a, first
        else:
            acts, turned, slopes, beta, start = acts_b, turned_b, slopes_b, beta_b, first - half
        here = slice(first, first + blk)
        sens = done[nv - 1, here] * prod[here] + REG_WEIGHT * (beta[start : start + blk] - 1.0)

        def add(ref, part):
            ref[...] = part if first == 0 else ref[...] + part

        def slanted(number, product, lo, out):
            total = jnp.zeros((hidden, LANE), F32)
            for q in range(blk):
                d = product[:, q * cols : (q + 1) * cols] * slopes[start + q, lo : lo + hidden]
                total = total + fold(d)
                out.append(d.astype(BF16))
                yield
            add(sums.at[number], total)

        out_sum, sens_rows, d3, d2, d1 = jnp.zeros((hidden, LANE), F32), [], [], [], []
        for q in range(blk):
            sen = jnp.broadcast_to(sens[q : q + 1], (hidden, cols))
            out_sum = out_sum + fold(acts[start + q, 16:].astype(F32) * sen)
            sens_rows.append(sen)
            yield
        add(sums.at[0], out_sum)
        yield from slanted(3, joined(sens_rows), 2 * hidden, d3)
        d3 = joined(d3)
        product = jnp.dot(wtop[...], d3, preferred_element_type=F32)
        yield
        yield from slanted(2, product, hidden, d2)
        d2 = joined(d2)
        product = jnp.dot(wmid[...], d2, preferred_element_type=F32)
        yield
        add(
            g_two,
            jnp.dot(
                jnp.concatenate([d2, d3], axis=0),
                turned[start : start + blk].reshape(blk * cols, 2 * hidden),
                preferred_element_type=F32,
            ),
        )
        yield
        yield from slanted(1, product, 0, d1)
        add(g_in, outer(joined(d1), joined([acts[start + q, 0:16] for q in range(blk)])))

    backward_turns = 4 * blk + 3

    def together(sweeps, back):
        turns = max(nv * len(sweeps), 1)
        sweeps = itertools.chain(*(sweep(*x) for x in sweeps))
        for turn in range(turns):
            next(sweeps, None)
            for _ in range(backward_turns * turn // turns, backward_turns * (turn + 1) // turns):
                next(back, None)
        for _ in itertools.chain(sweeps, back):
            pass

    ahead = [2 * (SWEEPS - number) for number in range(SWEEPS + 1)]
    for number in range(1, SWEEPS):
        together([(number, t) for t in range(min(ahead[number] + 1, tiles))], iter(()))
    for t in range(1, tiles - 1):
        step = [(n, t + ahead[n]) for n in range(1, SWEEPS + 1) if t + ahead[n] < tiles]
        together(step, backward((t - 2) * blk) if t > 1 else iter(()))
    copies[2].start()
    together([], backward(rows - blk))

    from_features = jnp.transpose(joined([g_in[...], jnp.zeros((hidden, LANE - 16), F32)]))
    tail = from_features[SUB : 2 * SUB]
    row = lax.broadcasted_iota(jnp.int32, (SUB, hidden), 0)
    for k in range(4):
        line = jnp.sum(jnp.transpose(sums[k]), axis=0, keepdims=True)
        tail = tail + jnp.where(row == k + num_feat - SUB, jnp.broadcast_to(line, (SUB, hidden)), 0.0)
    both = jnp.transpose(g_two[...])
    lane = lax.broadcasted_iota(jnp.int32, (hidden, 2 * hidden), 1)
    packed[0:hidden, :] = jnp.where(lane < hidden, both[:hidden], both[hidden:])
    packed[hidden : hidden + SUB, :] = joined([from_features[0:SUB], tail])
    for copy in copies:
        copy.wait()


def sweeps_and_backward(num_feat, source, coupling, inverse, production, betas, halos, weights, nets, mixing):
    nv, rows, cols = source.shape
    nc = coupling.shape[0]
    hidden = weights[0].shape[0]
    tall, wide = rows + 2 * EDGE, cols + LANE
    near, far = pl.BlockSpec(memory_space=pltpu.VMEM), pl.BlockSpec(memory_space=pltpu.HBM)
    operands = [source, coupling, inverse, production, *betas, *halos, *weights, *nets]
    return pl.pallas_call(
        functools.partial(adjoint_kernel, num_feat),
        in_specs=[near] * len(operands) + [pl.BlockSpec(memory_space=pltpu.SMEM)],
        out_specs=[near, far, far],
        out_shape=[
            pltpu.VMEM((hidden + SUB, LANE), F32),
            pltpu.HBM((nv, rows, cols), F32),
            pltpu.HBM((rows, cols), F32),
        ],
        scratch_shapes=[
            pltpu.VMEM((nv + nc + 1, tall, wide), F32),
            pltpu.VMEM((nv, tall, wide), F32),
            pltpu.VMEM((nc, tall, wide), F32),
            pltpu.VMEM((SWEEPS - 1, nv, tall, wide), F32),
            pltpu.VMEM((nv, rows, cols), F32),
            pltpu.VMEM((4, hidden, LANE), F32),
            pltpu.VMEM((2 * hidden, 2 * hidden), F32),
            pltpu.VMEM((hidden, 16), F32),
            pltpu.SemaphoreType.DMA((3,)),
        ],
        compiler_params=params(),
        name="sweeps_backward",
    )(*operands, mixing)


def clip_kernel(summed, gin, gmid, gtop, gout, gbias):
    hidden = gmid.shape[0]
    total = summed[...]
    squares = jnp.sum(jnp.sum(total * total, axis=0, keepdims=True), axis=1, keepdims=True)
    total = total * (CLIP_NORM / jnp.maximum(jnp.sqrt(squares), CLIP_NORM))
    gmid[...] = total[:hidden, :hidden]
    gtop[...] = total[:hidden, hidden:]
    low, high = total[hidden:, :hidden], total[hidden:, hidden:]
    gin[0:SUB] = low
    gin[SUB:] = high[: gin.shape[0] - SUB]
    at = gin.shape[0] - SUB
    gout[...] = high[at : at + 1]
    gbias[...] = high[at + 1 : at + 4]


def clip_all(summed, num_feat, hidden):
    shapes = [(num_feat, hidden), (hidden, hidden), (hidden, hidden), (1, hidden), (3, hidden)]
    return pl.pallas_call(
        clip_kernel,
        grid=(1,),
        in_specs=[whole(summed.shape)],
        out_specs=[whole(s) for s in shapes],
        out_shape=[jax.ShapeDtypeStruct(s, F32) for s in shapes],
        compiler_params=params(),
        name="clip",
    )(summed)


def sum_over_case(packed):
    num_x, num_y = lax.axis_size("gx"), lax.axis_size("gy")

    def swapped(x, dx, dy):
        pairs = [(i * num_y + j, (i ^ dx) * num_y + (j ^ dy)) for i in range(num_x) for j in range(num_y)]
        return lax.ppermute(x, ("gx", "gy"), pairs)

    cross = 1 if num_y > 1 else 0
    if num_y > 1:
        packed = packed + swapped(packed, 0, 1)
    step = 2
    while step < num_y:
        packed = packed + swapped(packed, 0, step ^ cross)
        step *= 2
    step = 1
    while step < num_x:
        parts = [packed] + [swapped(packed, k * step, cross) for k in range(1, min(4, num_x // step))]
        while len(parts) > 1:
            parts = [a + b for a, b in zip(parts[::2], parts[1::2])]
        packed = parts[0]
        step *= 4
    return packed


def row_swaps(first, second):
    num_x, num_y = lax.axis_size("gx"), lax.axis_size("gy")
    out = []
    for start, slab in ((1, second), (0, first)):
        partner = {}
        for i in range(num_x):
            j = i + 1 if i % 2 == start else i - 1
            for y in range(num_y):
                if 0 <= j < num_x:
                    partner[i * num_y + y] = j * num_y + y
                elif num_y % 2 == 0:
                    partner[i * num_y + y] = i * num_y + (y ^ 1)
        out.append(lax.ppermute(slab, ("gx", "gy"), sorted(partner.items())))
    return out[::-1]


def col_swaps(first, second):
    count = lax.axis_size("gy")
    out = []
    for start, slab in ((0, first), (1, second)):
        low = [(i, i + 1) for i in range(start, count - 1, 2)]
        if count % 2 == 0 and start == 1:
            low.append((0, count - 1))
        out.append(lax.ppermute(slab, "gy", low + [(b, a) for a, b in low]))
    return out


def shards(
    features, source, coupling, diagonal, production, bc_code, mixing,
    weight_in, weight_mid, weight_top, weight_out, biases,
):
    num_feat, rows, _ = features.shape
    hidden = weight_mid.shape[0]
    loaded = load([
        source, coupling, diagonal, bc_code, production, features,
        weight_in, weight_mid, weight_top, weight_out.reshape(1, hidden), biases,
    ])
    source, coupling, _, _, production, features, weight_in, weight_mid, weight_top, wout, biases = loaded[:11]
    inverse, second, first = loaded[11:]
    row_halos = row_swaps(first, second)
    prepared = prepare(weight_in, weight_mid, weight_top, wout, biases)
    half = rows - 32
    *net_a, beta_a = forward(features, prepared, 0, half)
    *row_halos, beta_a = lax.optimization_barrier((*row_halos, beta_a))
    first, second, *row_halos = col_slabs(source, coupling, inverse, row_halos)
    col_halos = col_swaps(first, second)
    *net_b, beta_b = forward(features, prepared, half, rows - half)
    packed, adjoint, beta = sweeps_and_backward(
        num_feat, source, coupling, inverse, production, (beta_a, beta_b), (*row_halos, *col_halos),
        (weight_mid, weight_top), (*net_a, *net_b), mixing,
    )
    grad_in, grad_mid, grad_top, grad_out, grad_bias = clip_all(sum_over_case(packed), num_feat, hidden)
    return (adjoint, beta, grad_in, grad_mid, grad_top, grad_out.reshape(hidden), grad_bias)


def solution(mesh):
    cells3 = P(None, ("case", "gx"), "gy")
    cells2 = P(("case", "gx"), "gy")
    return jax.shard_map(
        shards,
        mesh=mesh,
        in_specs=(cells3,) * 3 + (cells2,) * 3 + (P(),) * 6,
        out_specs=(cells3, cells2, P("case"), P("case"), P("case"), P("case"), P("case")),
        check_vma=False,
    )
```

```python
import functools
import itertools

import jax
import jax.numpy as jnp
from jax import lax
from jax.experimental import pallas as pl
from jax.experimental.pallas import tpu as pltpu
from jax.sharding import PartitionSpec as P

SWEEPS = 6
WALL_EXTRA = 0.2
FAR_EXTRA = 0.6
REG_WEIGHT = 0.5
CLIP_NORM = 64.0
DEPTH = SWEEPS
EDGE = 8
SUB, LANE = 8, 128
F32, BF16 = jnp.float32, jnp.bfloat16
NT = (((1,), (1,)), ((), ()))
TN = (((0,), (0,)), ((), ()))
VMEM_BYTES = 16 * 1024 * 1024


def whole(shape):
    return pl.BlockSpec(shape, lambda *_: (0,) * len(shape))


def in_hbm(x):
    return pltpu.with_memory_space_constraint(x, pltpu.HBM)


def on_chip(kernel, operands, outs, scratch=(), far=(), far_outs=(), **kwargs):
    here, there = pl.BlockSpec(memory_space=pltpu.VMEM), pl.BlockSpec(memory_space=pltpu.HBM)
    return pl.pallas_call(
        kernel,
        in_specs=[here] * len(operands) + [there] * len(far),
        out_specs=[here] * len(outs) + [there] * len(far_outs),
        out_shape=[pltpu.VMEM(*o) for o in outs] + [pltpu.HBM(*o) for o in far_outs],
        scratch_shapes=list(scratch),
        compiler_params=params(),
        **kwargs,
    )(*operands, *[in_hbm(x) for x in far])


def like(x):
    return (x.shape, x.dtype)


def params():
    return pltpu.CompilerParams(vmem_limit_bytes=VMEM_BYTES)


def inverse_diag(diag, code):
    total = diag + jnp.where(code == 1, WALL_EXTRA, 0.0) + jnp.where(code == 2, FAR_EXTRA, 0.0)
    return 1.0 / total


def is_odd(axis):
    return lax.axis_index(axis) % 2 == 1


def load_kernel(count, *refs):
    far, kept = refs[:count], refs[count : 2 * count - 2]
    inv, second, first, dia, bc, sems = refs[2 * count - 2 :]
    near = (*kept[:2], dia, bc, *kept[2:])
    copies = [pltpu.make_async_copy(far[k], near[k], sems.at[k]) for k in range(count)]
    for copy in copies:
        copy.start()
    src, cpl = near[:2]
    for copy in copies[:4]:
        copy.wait()
    nv, rows, _ = src.shape
    nc = cpl.shape[0]
    inv[...] = inverse_diag(dia[...], bc[...])
    odd = is_odd("gx")
    for f in range(nv + nc + 1):
        if f < nv + nc:
            ref, k = (src, f) if f < nv else (cpl, f - nv)
            top, bottom = ref[k, 0:16].astype(F32)[:DEPTH], ref[k, rows - 16 :].astype(F32)[16 - DEPTH :]
        else:
            top, bottom = inv[0:DEPTH], inv[rows - DEPTH :]
        first[f * DEPTH : (f + 1) * DEPTH] = jnp.where(odd, top, bottom)
        second[f * DEPTH : (f + 1) * DEPTH] = jnp.where(odd, bottom, top)
    for copy in copies[4:]:
        copy.wait()


def load(arrays):
    source, coupling, diagonal, bc_code = arrays[:4]
    nv, rows, cols = source.shape
    slab = (((nv + coupling.shape[0] + 1) * DEPTH, cols), F32)
    return on_chip(
        functools.partial(load_kernel, len(arrays)),
        [],
        [like(x) for x in (*arrays[:2], *arrays[4:])] + [((rows, cols), F32), slab, slab],
        [pltpu.VMEM(*like(diagonal)), pltpu.VMEM(*like(bc_code)), pltpu.SemaphoreType.DMA((len(arrays),))],
        far=arrays,
        name="load",
    )


def ordered(axis, first, second):
    odd, at = is_odd(axis), lax.axis_index(axis)
    before, after = jnp.where(odd, first, second), jnp.where(odd, second, first)
    return jnp.where(at == 0, 0.0, before), jnp.where(at == lax.axis_size(axis) - 1, 0.0, after)


def cols_kernel(src, cpl, inv, row_second, row_first, col_first, col_second, north, south):
    nv, rows, cols = src.shape
    nc = cpl.shape[0]
    half = col_first.shape[0]
    north[...] = jnp.zeros(north.shape, F32)
    south[...] = jnp.zeros(south.shape, F32)
    for f in range(nv + nc + 1):
        here = slice(f * DEPTH, (f + 1) * DEPTH)
        before, after = ordered("gx", row_first[here], row_second[here])
        north[f, EDGE - DEPTH :] = before
        south[f, 0:DEPTH] = after
    lane = lax.broadcasted_iota(jnp.int32, (half, LANE), 1)
    slabs = []
    for window, extra in ((slice(0, LANE), 0), (slice(cols - LANE, cols), DEPTH)):
        slab = jnp.zeros((half, LANE), F32)
        for f in range(nv + nc + 1):
            if f < nv:
                x = src[f, :, window].astype(F32)
            elif f < nv + nc:
                x = cpl[f - nv, :, window].astype(F32)
            else:
                x = inv[:, window]
            x = jnp.concatenate([north[f, :, window], x, south[f, :, window]], axis=0)
            for part, at in ((x[:half], DEPTH * f), (x[half:], DEPTH * f + LANE // 2)):
                own = jnp.logical_and(lane >= at, lane < at + DEPTH)
                slab = jnp.where(own, pltpu.roll(part, (at + extra) % LANE, 1), slab)
        slabs.append(slab)
    odd = is_odd("gy")
    col_first[...] = jnp.where(odd, slabs[0], slabs[1])
    col_second[...] = jnp.where(odd, slabs[1], slabs[0])


def col_slabs(source, coupling, inv, row_halos):
    nv, rows, cols = source.shape
    slab = (((rows + 2 * EDGE) // 2, LANE), F32)
    halo = ((nv + coupling.shape[0] + 1, EDGE, cols), F32)
    return on_chip(
        cols_kernel, [source, coupling, inv, *row_halos], [slab, slab, halo, halo], name="col_slabs"
    )


def column_of(row):
    hidden = row.shape[1]
    wide = jnp.concatenate([row, jnp.zeros((1, LANE - hidden), F32)], axis=1)
    return jnp.transpose(jnp.broadcast_to(wide, (LANE, LANE)))[:hidden]


def across(block, width):
    return jnp.concatenate([block] * (width // LANE), axis=1)


def weights_kernel(win, wmid, wtop, wout, bias, w1, w2, w3, cst):
    nf, hidden = win.shape
    step_rows, blk = hidden + 16, 16
    depth = w1.shape[1]
    feat_of = lax.broadcasted_iota(jnp.int32, (nf, depth), 1) // blk
    pick = (feat_of == lax.broadcasted_iota(jnp.int32, (nf, depth), 0)).astype(F32).astype(BF16)
    spread = lax.dot_general(win[...], pick, TN, preferred_element_type=F32)
    col = lax.broadcasted_iota(jnp.int32, (hidden, depth), 1)
    col_f = lax.broadcasted_iota(jnp.int32, (16, depth), 1)
    row_f = lax.broadcasted_iota(jnp.int32, (16, depth), 0)
    for r in range(blk):
        base = r * step_rows
        w1[base : base + hidden] = jnp.where(col % blk == r, spread, 0.0).astype(BF16)
        same = jnp.logical_and(col_f == row_f * blk + r, row_f < nf)
        w1[base + hidden : base + step_rows] = jnp.where(same, 1.0, 0.0).astype(BF16)
    w2[...] = jnp.transpose(wmid[...].astype(F32)).astype(BF16)
    w3[...] = jnp.transpose(wtop[...].astype(F32)).astype(BF16)
    for k in range(3):
        cst[k] = column_of(bias[k : k + 1, :])
    cst[3] = column_of(wout[...])


def prepare(weight_in, weight_mid, weight_top, weight_out, biases):
    nf, hidden = weight_in.shape
    depth = -(-nf * 16 // LANE) * LANE
    return on_chip(
        weights_kernel,
        [weight_in, weight_mid, weight_top, weight_out, biases],
        [
            ((16 * (hidden + 16), depth), BF16),
            ((hidden, hidden), BF16),
            ((hidden, hidden), BF16),
            ((4, hidden, LANE), F32),
        ],
        name="weights",
    )


def slope(act):
    return 1.0 - act * act


def forward_kernel(first_row, feat, w1, w2, w3, cst, acts, slopes, beta, x1):
    nf, _, cols = feat.shape
    hidden = w2.shape[0]
    step_rows, blk, per = hidden + 16, 16, 4
    x1[...] = jnp.zeros(x1.shape, BF16)

    @pl.loop(0, acts.shape[0] // blk)
    def _(block):
        start = pl.multiple_of(block * blk, blk)
        x1[0 : nf * blk] = feat[:, pl.ds(first_row + start, blk), :].reshape(nf * blk, cols)
        b1, b2, b3, wo = (across(cst[k], cols) for k in range(4))
        lines = []
        first = jnp.dot(w1[...], x1[...], preferred_element_type=F32)
        for g in range(blk // per):
            ones = []
            for q in range(g * per, (g + 1) * per):
                part = first[q * step_rows : (q + 1) * step_rows]
                one = jnp.tanh(part[:hidden] + b1).astype(BF16)
                slopes[start + q, 0:hidden] = slope(one.astype(F32))
                acts[start + q, 0:hidden] = one
                acts[start + q, 2 * hidden : 2 * hidden + 16] = part[hidden:].astype(BF16)
                ones.append(one)
            second = jnp.dot(w2[...], jnp.concatenate(ones, axis=1), preferred_element_type=F32)
            twos = []
            for q in range(per):
                two = jnp.tanh(second[:, q * cols : (q + 1) * cols] + b2).astype(BF16)
                slopes[start + (g * per + q), hidden : 2 * hidden] = slope(two.astype(F32))
                acts[start + (g * per + q), hidden : 2 * hidden] = two
                twos.append(two)
            third = jnp.dot(w3[...], jnp.concatenate(twos, axis=1), preferred_element_type=F32)
            for q in range(per):
                three = jnp.tanh(third[:, q * cols : (q + 1) * cols] + b3).astype(BF16)
                acts[start + (g * per + q), 2 * hidden + 16 :] = three
                three = three.astype(F32)
                slopes[start + (g * per + q), 2 * hidden :] = wo * slope(three)
                lines.append(1.0 + jnp.sum(three * wo, axis=0, keepdims=True))
        beta[pl.ds(start, blk), :] = jnp.concatenate(lines, axis=0)


def forward(features, prepared, first_row, count):
    nf, _, cols = features.shape
    w1, w2 = prepared[:2]
    hidden = w2.shape[0]
    high = 3 * hidden + 16
    return on_chip(
        functools.partial(forward_kernel, first_row),
        [features, *prepared],
        [((count, high, cols), BF16), ((count, 3 * hidden, cols), F32), ((count, cols), F32)],
        [pltpu.VMEM((w1.shape[1], cols), BF16)],
        cost_estimate=pl.CostEstimate(
            flops=2 * count * cols * (nf + 2 * hidden) * hidden,
            bytes_accessed=2 * count * cols * (high + nf),
            transcendentals=3 * count * cols * hidden,
        ),
        name="network_forward",
    )


def span(t, k):
    return (slice(t * SUB, (t + 1) * SUB), slice(k * LANE, (k + 1) * LANE))


class Shifts:
    def __init__(self, tiles, lanes):
        self.tiles, self.lanes = tiles, lanes
        sub = lax.broadcasted_iota(jnp.int32, (SUB, LANE), 0)
        lane = lax.broadcasted_iota(jnp.int32, (SUB, LANE), 1)
        self.first_sub, self.last_sub = sub == 0, sub == SUB - 1
        self.first_lane, self.last_lane = lane == 0, lane == LANE - 1

    def row(self, ref, lead, t):
        t = min(max(t, 0), self.tiles - 1)
        return [ref[lead + span(t, k)] for k in range(self.lanes)]

    def above(self, rows, k):
        return pltpu.roll(jnp.where(self.last_sub, rows[0][k], rows[1][k]), 1, 0)

    def below(self, rows, k):
        return pltpu.roll(jnp.where(self.first_sub, rows[2][k], rows[1][k]), SUB - 1, 0)

    def left(self, rows, k):
        return pltpu.roll(jnp.where(self.last_lane, rows[1][(k - 1) % self.lanes], rows[1][k]), 1, 1)

    def right(self, rows, k):
        other = rows[1][(k + 1) % self.lanes]
        return pltpu.roll(jnp.where(self.first_lane, other, rows[1][k]), LANE - 1, 1)

    def around(self, ref, lead, t, k_count):
        rows = [self.row(ref, lead, t + o) for o in (-1, 0, 1)]
        moves = (self.above, self.below, self.left, self.right)
        return [[move(rows, k) for move in moves] for k in range(k_count)]


def extend(src, cpl, inverse, north, south, col_halos, shifts, raw, src_x, cpl_x):
    nv, rows, cols = src.shape
    nc = cpl.shape[0]
    tall = rows + 2 * EDGE
    inner = slice(EDGE, EDGE + rows)
    lane = lax.broadcasted_iota(jnp.int32, (tall, LANE), 1)
    from_east, from_west = lane < DEPTH, lane >= LANE - DEPTH
    west, east = ordered("gy", *(x[...] for x in col_halos))
    for f in range(nv + nc + 1):
        if f < nv:
            raw[f, inner, 0:cols] = src[f].astype(F32)
        elif f < nv + nc:
            raw[f, inner, 0:cols] = cpl[f - nv].astype(F32)
        else:
            raw[f, inner, 0:cols] = inverse[...]
        raw[f, 0:EDGE, 0:cols] = north[f]
        raw[f, EDGE + rows :, 0:cols] = south[f]
        low, high = (-DEPTH * f) % LANE, (LANE // 2 - DEPTH * f) % LANE
        e = jnp.concatenate([pltpu.roll(east, at, 1) for at in (low, high)], axis=0)
        w = jnp.concatenate([pltpu.roll(west, (at - DEPTH) % LANE, 1) for at in (low, high)], axis=0)
        raw[f, :, cols:] = jnp.where(from_east, e, jnp.where(from_west, w, 0.0))
    for t in range(shifts.tiles):
        inv = shifts.row(raw, (nv + nc,), t)
        for k in range(shifts.lanes):
            for v in range(nv):
                src_x[(v,) + span(t, k)] = inv[k] * raw[(v,) + span(t, k)]
        for d, move in enumerate((shifts.above, shifts.below, shifts.left, shifts.right)):
            rows_d = [shifts.row(raw, (nv + d,), t + o) for o in (-1, 0, 1)]
            for k in range(shifts.lanes):
                cpl_x[(d,) + span(t, k)] = inv[k] * move(rows_d, k)


def adjoint_kernel(
    num_feat, src, cpl, inverse, prod, beta_a, beta_b, north, south, col_first, col_second,
    wmid, wtop, acts_a, slopes_a, acts_b, slopes_b, mix,
    packed, adj_out, beta_out,
    raw, src_x, cpl_x, adj, done, sums, g_mid, g_top, g_in, sems,
):
    nv, rows, cols = src.shape
    nc = cpl.shape[0]
    hidden, blk = wmid.shape[0], SUB
    half = beta_a.shape[0]
    tiles, lanes = (rows + 2 * EDGE) // SUB, cols // LANE + 1
    copies = [
        pltpu.make_async_copy(beta_a, beta_out.at[0:half], sems.at[0]),
        pltpu.make_async_copy(beta_b, beta_out.at[half:rows], sems.at[1]),
        pltpu.make_async_copy(done, adj_out, sems.at[2]),
    ]
    copies[0].start()
    copies[1].start()
    shifts = Shifts(tiles, lanes)
    extend(src, cpl, inverse, north, south, (col_first, col_second), shifts, raw, src_x, cpl_x)
    weights = [[mix[b, a] for a in range(nv)] for b in range(nv)]

    def sweep(number, t):
        last = number == SWEEPS
        count = lanes - 1 if last else lanes
        couple = [[cpl_x[(d,) + span(t, k)] for d in range(nc)] for k in range(count)]
        total = [[src_x[(a,) + span(t, k)] for a in range(nv)] for k in range(count)]
        for b in range(nv):
            old, lead = (src_x, (b,)) if number == 1 else (adj, (number - 2, b))
            around = shifts.around(old, lead, t, count)
            for k in range(count):
                terms = [couple[k][d] * around[k][d] for d in range(nc)]
                inc = (terms[0] + terms[1]) + (terms[2] + terms[3])
                total[k] = [total[k][a] + weights[b][a] * inc for a in range(nv)]
            yield
        for k in range(count):
            for a in range(nv):
                if last:
                    done[(a,) + span(t - EDGE // SUB, k)] = total[k][a]
                else:
                    adj[(number - 1, a) + span(t, k)] = total[k][a]

    def fold(x):
        parts = [x[:, k * LANE : (k + 1) * LANE] for k in range(cols // LANE)]
        return functools.reduce(jnp.add, parts)

    def joined(xs):
        return jnp.concatenate(xs, axis=1)

    def outer(x, d):
        return lax.dot_general(x, d, NT, preferred_element_type=F32)

    def backward(first):
        if first < half:
            acts, slopes, beta, start = acts_a, slopes_a, beta_a, first
        else:
            acts, slopes, beta, start = acts_b, slopes_b, beta_b, first - half
        here = slice(first, first + blk)
        sens = done[nv - 1, here] * prod[here] + REG_WEIGHT * (beta[start : start + blk] - 1.0)

        def layer(lo, high):
            return joined([acts[start + q, lo:high] for q in range(blk)])

        def add(ref, part):
            ref[...] = part if first == 0 else ref[...] + part

        def slanted(number, product, lo, out):
            total = jnp.zeros((hidden, LANE), F32)
            for q in range(blk):
                d = product[:, q * cols : (q + 1) * cols] * slopes[start + q, lo : lo + hidden]
                total = total + fold(d)
                out.append(d.astype(BF16))
                yield
            add(sums.at[number], total)

        out_sum, sens_rows, d3, d2, d1 = jnp.zeros((hidden, LANE), F32), [], [], [], []
        for q in range(blk):
            sen = jnp.broadcast_to(sens[q : q + 1], (hidden, cols))
            out_sum = out_sum + fold(acts[start + q, 2 * hidden + 16 :].astype(F32) * sen)
            sens_rows.append(sen)
            yield
        add(sums.at[0], out_sum)
        yield from slanted(3, joined(sens_rows), 2 * hidden, d3)
        d3 = joined(d3)
        product = jnp.dot(wtop[...], d3, preferred_element_type=F32)
        yield
        add(g_top, outer(layer(hidden, 2 * hidden), d3))
        yield
        yield from slanted(2, product, hidden, d2)
        d2 = joined(d2)
        product = jnp.dot(wmid[...], d2, preferred_element_type=F32)
        yield
        add(g_mid, outer(layer(0, hidden), d2))
        yield
        yield from slanted(1, product, 0, d1)
        add(g_in, outer(joined(d1), layer(2 * hidden, 2 * hidden + 16)))

    backward_turns = 4 * blk + 4

    def together(sweeps, back):
        turns = max(nv * len(sweeps), 1)
        sweeps = itertools.chain(*(sweep(*x) for x in sweeps))
        for turn in range(turns):
            next(sweeps, None)
            for _ in range(backward_turns * turn // turns, backward_turns * (turn + 1) // turns):
                next(back, None)
        for _ in itertools.chain(sweeps, back):
            pass

    ahead = [2 * (SWEEPS - number) for number in range(SWEEPS + 1)]
    for number in range(1, SWEEPS):
        together([(number, t) for t in range(min(ahead[number] + 1, tiles))], iter(()))
    for t in range(1, tiles - 1):
        step = [(n, t + ahead[n]) for n in range(1, SWEEPS + 1) if t + ahead[n] < tiles]
        together(step, backward((t - 2) * blk) if t > 1 else iter(()))
    copies[2].start()
    together([], backward(rows - blk))

    turned = jnp.transpose(joined([g_in[...], jnp.zeros((hidden, LANE - 16), F32)]))
    tail = turned[SUB : 2 * SUB]
    row = lax.broadcasted_iota(jnp.int32, (SUB, hidden), 0)
    for k in range(4):
        line = jnp.sum(jnp.transpose(sums[k]), axis=0, keepdims=True)
        tail = tail + jnp.where(row == k + num_feat - SUB, jnp.broadcast_to(line, (SUB, hidden)), 0.0)
    packed[0:hidden, :] = joined([g_mid[...], g_top[...]])
    packed[hidden : hidden + SUB, :] = joined([turned[0:SUB], tail])
    for copy in copies:
        copy.wait()


def sweeps_and_backward(num_feat, source, coupling, inverse, production, betas, halos, weights, nets, mixing):
    nv, rows, cols = source.shape
    nc = coupling.shape[0]
    hidden = weights[0].shape[0]
    tall, wide = rows + 2 * EDGE, cols + LANE
    near, far = pl.BlockSpec(memory_space=pltpu.VMEM), pl.BlockSpec(memory_space=pltpu.HBM)
    operands = [source, coupling, inverse, production, *betas, *halos, *weights, *nets]
    return pl.pallas_call(
        functools.partial(adjoint_kernel, num_feat),
        in_specs=[near] * len(operands) + [pl.BlockSpec(memory_space=pltpu.SMEM)],
        out_specs=[near, far, far],
        out_shape=[
            pltpu.VMEM((hidden + SUB, LANE), F32),
            pltpu.HBM((nv, rows, cols), F32),
            pltpu.HBM((rows, cols), F32),
        ],
        scratch_shapes=[
            pltpu.VMEM((nv + nc + 1, tall, wide), F32),
            pltpu.VMEM((nv, tall, wide), F32),
            pltpu.VMEM((nc, tall, wide), F32),
            pltpu.VMEM((SWEEPS - 1, nv, tall, wide), F32),
            pltpu.VMEM((nv, rows, cols), F32),
            pltpu.VMEM((4, hidden, LANE), F32),
            pltpu.VMEM((hidden, hidden), F32),
            pltpu.VMEM((hidden, hidden), F32),
            pltpu.VMEM((hidden, 16), F32),
            pltpu.SemaphoreType.DMA((3,)),
        ],
        compiler_params=params(),
        name="sweeps_backward",
    )(*operands, mixing)


def clip_kernel(summed, gin, gmid, gtop, gout, gbias):
    hidden = gmid.shape[0]
    total = summed[...]
    squares = jnp.sum(jnp.sum(total * total, axis=0, keepdims=True), axis=1, keepdims=True)
    total = total * (CLIP_NORM / jnp.maximum(jnp.sqrt(squares), CLIP_NORM))
    gmid[...] = total[:hidden, :hidden]
    gtop[...] = total[:hidden, hidden:]
    low, high = total[hidden:, :hidden], total[hidden:, hidden:]
    gin[0:SUB] = low
    gin[SUB:] = high[: gin.shape[0] - SUB]
    at = gin.shape[0] - SUB
    gout[...] = high[at : at + 1]
    gbias[...] = high[at + 1 : at + 4]


def clip_all(summed, num_feat, hidden):
    shapes = [(num_feat, hidden), (hidden, hidden), (hidden, hidden), (1, hidden), (3, hidden)]
    return pl.pallas_call(
        clip_kernel,
        grid=(1,),
        in_specs=[whole(summed.shape)],
        out_specs=[whole(s) for s in shapes],
        out_shape=[jax.ShapeDtypeStruct(s, F32) for s in shapes],
        compiler_params=params(),
        name="clip",
    )(summed)


def sum_over_case(packed):
    num_x, num_y = lax.axis_size("gx"), lax.axis_size("gy")

    def swapped(x, dx, dy):
        pairs = [(i * num_y + j, (i ^ dx) * num_y + (j ^ dy)) for i in range(num_x) for j in range(num_y)]
        return lax.ppermute(x, ("gx", "gy"), pairs)

    cross = 1 if num_y > 1 else 0
    if num_y > 1:
        packed = packed + swapped(packed, 0, 1)
    step = 2
    while step < num_y:
        packed = packed + swapped(packed, 0, step ^ cross)
        step *= 2
    step = 1
    while step < num_x:
        parts = [packed] + [swapped(packed, k * step, cross) for k in range(1, min(4, num_x // step))]
        while len(parts) > 1:
            parts = [a + b for a, b in zip(parts[::2], parts[1::2])]
        packed = parts[0]
        step *= 4
    return packed


def row_swaps(first, second):
    num_x, num_y = lax.axis_size("gx"), lax.axis_size("gy")
    out = []
    for start, slab in ((1, second), (0, first)):
        partner = {}
        for i in range(num_x):
            j = i + 1 if i % 2 == start else i - 1
            for y in range(num_y):
                if 0 <= j < num_x:
                    partner[i * num_y + y] = j * num_y + y
                elif num_y % 2 == 0:
                    partner[i * num_y + y] = i * num_y + (y ^ 1)
        out.append(lax.ppermute(slab, ("gx", "gy"), sorted(partner.items())))
    return out


def col_swaps(first, second):
    count = lax.axis_size("gy")
    out = []
    for start, slab in ((0, first), (1, second)):
        low = [(i, i + 1) for i in range(start, count - 1, 2)]
        if count % 2 == 0 and start == 1:
            low.append((0, count - 1))
        out.append(lax.ppermute(slab, "gy", low + [(b, a) for a, b in low]))
    return out


def shards(
    features, source, coupling, diagonal, production, bc_code, mixing,
    weight_in, weight_mid, weight_top, weight_out, biases,
):
    num_feat, rows, _ = features.shape
    hidden = weight_mid.shape[0]
    loaded = load([
        source, coupling, diagonal, bc_code, production, features,
        weight_in, weight_mid, weight_top, weight_out.reshape(1, hidden), biases,
    ])
    source, coupling, production, features, weight_in, weight_mid, weight_top, wout, biases = loaded[:9]
    inverse, second, first = loaded[9:]
    row_halos = row_swaps(first, second)
    prepared = prepare(weight_in, weight_mid, weight_top, wout, biases)
    half = rows - 32
    *net_a, beta_a = forward(features, prepared, 0, half)
    *row_halos, beta_a = lax.optimization_barrier((*row_halos, beta_a))
    first, second, *row_halos = col_slabs(source, coupling, inverse, row_halos)
    col_halos = col_swaps(first, second)
    *net_b, beta_b = forward(features, prepared, half, rows - half)
    packed, adjoint, beta = sweeps_and_backward(
        num_feat, source, coupling, inverse, production, (beta_a, beta_b), (*row_halos, *col_halos),
        (weight_mid, weight_top), (*net_a, *net_b), mixing,
    )
    grad_in, grad_mid, grad_top, grad_out, grad_bias = clip_all(sum_over_case(packed), num_feat, hidden)
    return (adjoint, beta, grad_in, grad_mid, grad_top, grad_out.reshape(hidden), grad_bias)


def solution(mesh):
    cells3 = P(None, ("case", "gx"), "gy")
    cells2 = P(("case", "gx"), "gy")
    return jax.shard_map(
        shards,
        mesh=mesh,
        in_specs=(cells3,) * 3 + (cells2,) * 3 + (P(),) * 6,
        out_specs=(cells3, cells2, P("case"), P("case"), P("case"), P("case"), P("case")),
        check_vma=False,
    )
```

```python
import functools
import itertools

import jax
import jax.numpy as jnp
from jax import lax
from jax.experimental import pallas as pl
from jax.experimental.pallas import tpu as pltpu
from jax.sharding import PartitionSpec as P

SWEEPS = 6
WALL_EXTRA = 0.2
FAR_EXTRA = 0.6
REG_WEIGHT = 0.5
CLIP_NORM = 64.0
DEPTH = SWEEPS
EDGE = 8
SUB, LANE = 8, 128
F32, BF16 = jnp.float32, jnp.bfloat16
NT = (((1,), (1,)), ((), ()))
TN = (((0,), (0,)), ((), ()))
VMEM_BYTES = 16 * 1024 * 1024


def whole(shape):
    return pl.BlockSpec(shape, lambda *_: (0,) * len(shape))


def in_hbm(x):
    return pltpu.with_memory_space_constraint(x, pltpu.HBM)


def on_chip(kernel, operands, outs, scratch=(), far=(), far_outs=(), **kwargs):
    here, there = pl.BlockSpec(memory_space=pltpu.VMEM), pl.BlockSpec(memory_space=pltpu.HBM)
    return pl.pallas_call(
        kernel,
        in_specs=[here] * len(operands) + [there] * len(far),
        out_specs=[here] * len(outs) + [there] * len(far_outs),
        out_shape=[pltpu.VMEM(*o) for o in outs] + [pltpu.HBM(*o) for o in far_outs],
        scratch_shapes=list(scratch),
        compiler_params=params(),
        **kwargs,
    )(*operands, *[in_hbm(x) for x in far])


def like(x):
    return (x.shape, x.dtype)


def params():
    return pltpu.CompilerParams(vmem_limit_bytes=VMEM_BYTES)


def inverse_diag(diag, code):
    total = diag + jnp.where(code == 1, WALL_EXTRA, 0.0) + jnp.where(code == 2, FAR_EXTRA, 0.0)
    return 1.0 / total


def is_odd(axis):
    return lax.axis_index(axis) % 2 == 1


def load_kernel(count, *refs):
    far, kept = refs[:count], refs[count : 2 * count - 2]
    inv, second, first, dia, bc, sems = refs[2 * count - 2 :]
    near = (*kept[:2], dia, bc, *kept[2:])
    copies = [pltpu.make_async_copy(far[k], near[k], sems.at[k]) for k in range(count)]
    for copy in copies:
        copy.start()
    src, cpl = near[:2]
    for copy in copies[:4]:
        copy.wait()
    nv, rows, _ = src.shape
    nc = cpl.shape[0]
    inv[...] = inverse_diag(dia[...], bc[...])
    odd = is_odd("gx")
    for f in range(nv + nc + 1):
        if f < nv + nc:
            ref, k = (src, f) if f < nv else (cpl, f - nv)
            top, bottom = ref[k, 0:16].astype(F32)[:DEPTH], ref[k, rows - 16 :].astype(F32)[16 - DEPTH :]
        else:
            top, bottom = inv[0:DEPTH], inv[rows - DEPTH :]
        first[f * DEPTH : (f + 1) * DEPTH] = jnp.where(odd, top, bottom)
        second[f * DEPTH : (f + 1) * DEPTH] = jnp.where(odd, bottom, top)
    for copy in copies[4:]:
        copy.wait()


def load(arrays):
    source, coupling, diagonal, bc_code = arrays[:4]
    nv, rows, cols = source.shape
    slab = (((nv + coupling.shape[0] + 1) * DEPTH, cols), F32)
    return on_chip(
        functools.partial(load_kernel, len(arrays)),
        [],
        [like(x) for x in (*arrays[:2], *arrays[4:])] + [((rows, cols), F32), slab, slab],
        [pltpu.VMEM(*like(diagonal)), pltpu.VMEM(*like(bc_code)), pltpu.SemaphoreType.DMA((len(arrays),))],
        far=arrays,
        name="load",
    )


def ordered(axis, first, second):
    odd, at = is_odd(axis), lax.axis_index(axis)
    before, after = jnp.where(odd, first, second), jnp.where(odd, second, first)
    return jnp.where(at == 0, 0.0, before), jnp.where(at == lax.axis_size(axis) - 1, 0.0, after)


def cols_kernel(src, cpl, inv, row_second, row_first, col_first, col_second, north, south):
    nv, rows, cols = src.shape
    nc = cpl.shape[0]
    half = col_first.shape[0]
    north[...] = jnp.zeros(north.shape, F32)
    south[...] = jnp.zeros(south.shape, F32)
    for f in range(nv + nc + 1):
        here = slice(f * DEPTH, (f + 1) * DEPTH)
        before, after = ordered("gx", row_first[here], row_second[here])
        north[f, EDGE - DEPTH :] = before
        south[f, 0:DEPTH] = after
    lane = lax.broadcasted_iota(jnp.int32, (half, LANE), 1)
    slabs = []
    for window, extra in ((slice(0, LANE), 0), (slice(cols - LANE, cols), DEPTH)):
        slab = jnp.zeros((half, LANE), F32)
        for f in range(nv + nc + 1):
            if f < nv:
                x = src[f, :, window].astype(F32)
            elif f < nv + nc:
                x = cpl[f - nv, :, window].astype(F32)
            else:
                x = inv[:, window]
            x = jnp.concatenate([north[f, :, window], x, south[f, :, window]], axis=0)
            for part, at in ((x[:half], DEPTH * f), (x[half:], DEPTH * f + LANE // 2)):
                own = jnp.logical_and(lane >= at, lane < at + DEPTH)
                slab = jnp.where(own, pltpu.roll(part, (at + extra) % LANE, 1), slab)
        slabs.append(slab)
    odd = is_odd("gy")
    col_first[...] = jnp.where(odd, slabs[0], slabs[1])
    col_second[...] = jnp.where(odd, slabs[1], slabs[0])


def col_slabs(source, coupling, inv, row_halos):
    nv, rows, cols = source.shape
    slab = (((rows + 2 * EDGE) // 2, LANE), F32)
    halo = ((nv + coupling.shape[0] + 1, EDGE, cols), F32)
    return on_chip(
        cols_kernel, [source, coupling, inv, *row_halos], [slab, slab, halo, halo], name="col_slabs"
    )


def column_of(row):
    hidden = row.shape[1]
    wide = jnp.concatenate([row, jnp.zeros((1, LANE - hidden), F32)], axis=1)
    return jnp.transpose(jnp.broadcast_to(wide, (LANE, LANE)))[:hidden]


def across(block, width):
    return jnp.concatenate([block] * (width // LANE), axis=1)


def weights_kernel(win, wmid, wtop, wout, bias, w1, w2, w3, cst):
    nf, hidden = win.shape
    step_rows, blk = hidden + 16, 16
    depth = w1.shape[1]
    feat_of = lax.broadcasted_iota(jnp.int32, (nf, depth), 1) // blk
    pick = (feat_of == lax.broadcasted_iota(jnp.int32, (nf, depth), 0)).astype(F32).astype(BF16)
    spread = lax.dot_general(win[...], pick, TN, preferred_element_type=F32)
    col = lax.broadcasted_iota(jnp.int32, (hidden, depth), 1)
    col_f = lax.broadcasted_iota(jnp.int32, (16, depth), 1)
    row_f = lax.broadcasted_iota(jnp.int32, (16, depth), 0)
    for r in range(blk):
        base = r * step_rows
        w1[base : base + hidden] = jnp.where(col % blk == r, spread, 0.0).astype(BF16)
        same = jnp.logical_and(col_f == row_f * blk + r, row_f < nf)
        w1[base + hidden : base + step_rows] = jnp.where(same, 1.0, 0.0).astype(BF16)
    w2[...] = jnp.transpose(wmid[...].astype(F32)).astype(BF16)
    w3[...] = jnp.transpose(wtop[...].astype(F32)).astype(BF16)
    for k in range(3):
        cst[k] = column_of(bias[k : k + 1, :])
    cst[3] = column_of(wout[...])


def prepare(weight_in, weight_mid, weight_top, weight_out, biases):
    nf, hidden = weight_in.shape
    depth = -(-nf * 16 // LANE) * LANE
    return on_chip(
        weights_kernel,
        [weight_in, weight_mid, weight_top, weight_out, biases],
        [
            ((16 * (hidden + 16), depth), BF16),
            ((hidden, hidden), BF16),
            ((hidden, hidden), BF16),
            ((4, hidden, LANE), F32),
        ],
        name="weights",
    )


def slope(act):
    return 1.0 - act * act


def forward_kernel(first_row, feat, w1, w2, w3, cst, acts, slopes, beta, x1):
    nf, _, cols = feat.shape
    hidden = w2.shape[0]
    step_rows, blk, per = hidden + 16, 16, 4
    x1[...] = jnp.zeros(x1.shape, BF16)

    @pl.loop(0, acts.shape[0] // blk)
    def _(block):
        start = pl.multiple_of(block * blk, blk)
        x1[0 : nf * blk] = feat[:, pl.ds(first_row + start, blk), :].reshape(nf * blk, cols)
        b1, b2, b3, wo = (across(cst[k], cols) for k in range(4))
        lines = []
        first = jnp.dot(w1[...], x1[...], preferred_element_type=F32)
        for g in range(blk // per):
            ones = []
            for q in range(g * per, (g + 1) * per):
                part = first[q * step_rows : (q + 1) * step_rows]
                one = jnp.tanh(part[:hidden] + b1).astype(BF16)
                slopes[start + q, 0:hidden] = slope(one.astype(F32))
                acts[start + q, 0:hidden] = one
                acts[start + q, 2 * hidden : 2 * hidden + 16] = part[hidden:].astype(BF16)
                ones.append(one)
            second = jnp.dot(w2[...], jnp.concatenate(ones, axis=1), preferred_element_type=F32)
            twos = []
            for q in range(per):
                two = jnp.tanh(second[:, q * cols : (q + 1) * cols] + b2).astype(BF16)
                slopes[start + (g * per + q), hidden : 2 * hidden] = slope(two.astype(F32))
                acts[start + (g * per + q), hidden : 2 * hidden] = two
                twos.append(two)
            third = jnp.dot(w3[...], jnp.concatenate(twos, axis=1), preferred_element_type=F32)
            for q in range(per):
                three = jnp.tanh(third[:, q * cols : (q + 1) * cols] + b3).astype(BF16)
                acts[start + (g * per + q), 2 * hidden + 16 :] = three
                three = three.astype(F32)
                slopes[start + (g * per + q), 2 * hidden :] = wo * slope(three)
                lines.append(1.0 + jnp.sum(three * wo, axis=0, keepdims=True))
        beta[pl.ds(start, blk), :] = jnp.concatenate(lines, axis=0)


def forward(features, prepared, first_row, count):
    nf, _, cols = features.shape
    w1, w2 = prepared[:2]
    hidden = w2.shape[0]
    high = 3 * hidden + 16
    return on_chip(
        functools.partial(forward_kernel, first_row),
        [features, *prepared],
        [((count, high, cols), BF16), ((count, 3 * hidden, cols), F32), ((count, cols), F32)],
        [pltpu.VMEM((w1.shape[1], cols), BF16)],
        cost_estimate=pl.CostEstimate(
            flops=2 * count * cols * (nf + 2 * hidden) * hidden,
            bytes_accessed=2 * count * cols * (high + nf),
            transcendentals=3 * count * cols * hidden,
        ),
        name="network_forward",
    )


def span(t, k):
    return (slice(t * SUB, (t + 1) * SUB), slice(k * LANE, (k + 1) * LANE))


class Shifts:
    def __init__(self, tiles, lanes):
        self.tiles, self.lanes = tiles, lanes
        sub = lax.broadcasted_iota(jnp.int32, (SUB, LANE), 0)
        lane = lax.broadcasted_iota(jnp.int32, (SUB, LANE), 1)
        self.first_sub, self.last_sub = sub == 0, sub == SUB - 1
        self.first_lane, self.last_lane = lane == 0, lane == LANE - 1

    def row(self, ref, lead, t):
        t = min(max(t, 0), self.tiles - 1)
        return [ref[lead + span(t, k)] for k in range(self.lanes)]

    def above(self, rows, k):
        return pltpu.roll(jnp.where(self.last_sub, rows[0][k], rows[1][k]), 1, 0)

    def below(self, rows, k):
        return pltpu.roll(jnp.where(self.first_sub, rows[2][k], rows[1][k]), SUB - 1, 0)

    def left(self, rows, k):
        return pltpu.roll(jnp.where(self.last_lane, rows[1][(k - 1) % self.lanes], rows[1][k]), 1, 1)

    def right(self, rows, k):
        other = rows[1][(k + 1) % self.lanes]
        return pltpu.roll(jnp.where(self.first_lane, other, rows[1][k]), LANE - 1, 1)

    def around(self, ref, lead, t, k_count):
        rows = [self.row(ref, lead, t + o) for o in (-1, 0, 1)]
        moves = (self.above, self.below, self.left, self.right)
        return [[move(rows, k) for move in moves] for k in range(k_count)]


def extend(src, cpl, inverse, north, south, col_halos, shifts, raw, src_x, cpl_x):
    nv, rows, cols = src.shape
    nc = cpl.shape[0]
    tall = rows + 2 * EDGE
    inner = slice(EDGE, EDGE + rows)
    lane = lax.broadcasted_iota(jnp.int32, (tall, LANE), 1)
    from_east, from_west = lane < DEPTH, lane >= LANE - DEPTH
    west, east = ordered("gy", *(x[...] for x in col_halos))
    for f in range(nv + nc + 1):
        if f < nv:
            raw[f, inner, 0:cols] = src[f].astype(F32)
        elif f < nv + nc:
            raw[f, inner, 0:cols] = cpl[f - nv].astype(F32)
        else:
            raw[f, inner, 0:cols] = inverse[...]
        raw[f, 0:EDGE, 0:cols] = north[f]
        raw[f, EDGE + rows :, 0:cols] = south[f]
        low, high = (-DEPTH * f) % LANE, (LANE // 2 - DEPTH * f) % LANE
        e = jnp.concatenate([pltpu.roll(east, at, 1) for at in (low, high)], axis=0)
        w = jnp.concatenate([pltpu.roll(west, (at - DEPTH) % LANE, 1) for at in (low, high)], axis=0)
        raw[f, :, cols:] = jnp.where(from_east, e, jnp.where(from_west, w, 0.0))
    for t in range(shifts.tiles):
        inv = shifts.row(raw, (nv + nc,), t)
        for k in range(shifts.lanes):
            for v in range(nv):
                src_x[(v,) + span(t, k)] = inv[k] * raw[(v,) + span(t, k)]
        for d, move in enumerate((shifts.above, shifts.below, shifts.left, shifts.right)):
            rows_d = [shifts.row(raw, (nv + d,), t + o) for o in (-1, 0, 1)]
            for k in range(shifts.lanes):
                cpl_x[(d,) + span(t, k)] = inv[k] * move(rows_d, k)


def adjoint_kernel(
    num_feat, src, cpl, inverse, prod, beta_a, beta_b, north, south, col_first, col_second,
    wmid, wtop, acts_a, slopes_a, acts_b, slopes_b, mix,
    packed, adj_out, beta_out,
    raw, src_x, cpl_x, adj, done, sums, g_mid, g_top, g_in, sems,
):
    nv, rows, cols = src.shape
    nc = cpl.shape[0]
    hidden, blk = wmid.shape[0], SUB
    half = beta_a.shape[0]
    tiles, lanes = (rows + 2 * EDGE) // SUB, cols // LANE + 1
    copies = [
        pltpu.make_async_copy(beta_a, beta_out.at[0:half], sems.at[0]),
        pltpu.make_async_copy(beta_b, beta_out.at[half:rows], sems.at[1]),
        pltpu.make_async_copy(done, adj_out, sems.at[2]),
    ]
    copies[0].start()
    copies[1].start()
    shifts = Shifts(tiles, lanes)
    extend(src, cpl, inverse, north, south, (col_first, col_second), shifts, raw, src_x, cpl_x)
    weights = [[mix[b, a] for a in range(nv)] for b in range(nv)]

    def sweep(number, t):
        last = number == SWEEPS
        count = lanes - 1 if last else lanes
        couple = [[cpl_x[(d,) + span(t, k)] for d in range(nc)] for k in range(count)]
        total = [[src_x[(a,) + span(t, k)] for a in range(nv)] for k in range(count)]
        for b in range(nv):
            old, lead = (src_x, (b,)) if number == 1 else (adj, (number - 2, b))
            around = shifts.around(old, lead, t, count)
            for k in range(count):
                terms = [couple[k][d] * around[k][d] for d in range(nc)]
                inc = (terms[0] + terms[1]) + (terms[2] + terms[3])
                total[k] = [total[k][a] + weights[b][a] * inc for a in range(nv)]
            yield
        for k in range(count):
            for a in range(nv):
                if last:
                    done[(a,) + span(t - EDGE // SUB, k)] = total[k][a]
                else:
                    adj[(number - 1, a) + span(t, k)] = total[k][a]

    def fold(x):
        parts = [x[:, k * LANE : (k + 1) * LANE] for k in range(cols // LANE)]
        return functools.reduce(jnp.add, parts)

    def joined(xs):
        return jnp.concatenate(xs, axis=1)

    def outer(x, d):
        return lax.dot_general(x, d, NT, preferred_element_type=F32)

    def backward(first):
        if first < half:
            acts, slopes, beta, start = acts_a, slopes_a, beta_a, first
        else:
            acts, slopes, beta, start = acts_b, slopes_b, beta_b, first - half
        here = slice(first, first + blk)
        sens = done[nv - 1, here] * prod[here] + REG_WEIGHT * (beta[start : start + blk] - 1.0)

        def layer(lo, high):
            return joined([acts[start + q, lo:high] for q in range(blk)])

        def add(ref, part):
            ref[...] = part if first == 0 else ref[...] + part

        def slanted(number, product, lo, out):
            total = jnp.zeros((hidden, LANE), F32)
            for q in range(blk):
                d = product[:, q * cols : (q + 1) * cols] * slopes[start + q, lo : lo + hidden]
                total = total + fold(d)
                out.append(d.astype(BF16))
                yield
            add(sums.at[number], total)

        out_sum, sens_rows, d3, d2, d1 = jnp.zeros((hidden, LANE), F32), [], [], [], []
        for q in range(blk):
            sen = jnp.broadcast_to(sens[q : q + 1], (hidden, cols))
            out_sum = out_sum + fold(acts[start + q, 2 * hidden + 16 :].astype(F32) * sen)
            sens_rows.append(sen)
            yield
        add(sums.at[0], out_sum)
        yield from slanted(3, joined(sens_rows), 2 * hidden, d3)
        d3 = joined(d3)
        product = jnp.dot(wtop[...], d3, preferred_element_type=F32)
        yield
        add(g_top, outer(layer(hidden, 2 * hidden), d3))
        yield
        yield from slanted(2, product, hidden, d2)
        d2 = joined(d2)
        product = jnp.dot(wmid[...], d2, preferred_element_type=F32)
        yield
        add(g_mid, outer(layer(0, hidden), d2))
        yield
        yield from slanted(1, product, 0, d1)
        add(g_in, outer(joined(d1), layer(2 * hidden, 2 * hidden + 16)))

    backward_turns = 4 * blk + 4

    def together(sweeps, back):
        turns = max(nv * len(sweeps), 1)
        sweeps = itertools.chain(*(sweep(*x) for x in sweeps))
        for turn in range(turns):
            next(sweeps, None)
            for _ in range(backward_turns * turn // turns, backward_turns * (turn + 1) // turns):
                next(back, None)
        for _ in itertools.chain(sweeps, back):
            pass

    ahead = [SWEEPS - number for number in range(SWEEPS + 1)]
    for number in range(1, SWEEPS):
        together([(number, t) for t in range(min(ahead[number] + 1, tiles))], iter(()))
    for t in range(1, tiles - 1):
        step = [(n, t + ahead[n]) for n in range(1, SWEEPS + 1) if t + ahead[n] < tiles]
        together(step, backward((t - 2) * blk) if t > 1 else iter(()))
    copies[2].start()
    together([], backward(rows - blk))

    turned = jnp.transpose(joined([g_in[...], jnp.zeros((hidden, LANE - 16), F32)]))
    tail = turned[SUB : 2 * SUB]
    row = lax.broadcasted_iota(jnp.int32, (SUB, hidden), 0)
    for k in range(4):
        line = jnp.sum(jnp.transpose(sums[k]), axis=0, keepdims=True)
        tail = tail + jnp.where(row == k + num_feat - SUB, jnp.broadcast_to(line, (SUB, hidden)), 0.0)
    packed[0:hidden, :] = joined([g_mid[...], g_top[...]])
    packed[hidden : hidden + SUB, :] = joined([turned[0:SUB], tail])
    for copy in copies:
        copy.wait()


def sweeps_and_backward(num_feat, source, coupling, inverse, production, betas, halos, weights, nets, mixing):
    nv, rows, cols = source.shape
    nc = coupling.shape[0]
    hidden = weights[0].shape[0]
    tall, wide = rows + 2 * EDGE, cols + LANE
    near, far = pl.BlockSpec(memory_space=pltpu.VMEM), pl.BlockSpec(memory_space=pltpu.HBM)
    operands = [source, coupling, inverse, production, *betas, *halos, *weights, *nets]
    return pl.pallas_call(
        functools.partial(adjoint_kernel, num_feat),
        in_specs=[near] * len(operands) + [pl.BlockSpec(memory_space=pltpu.SMEM)],
        out_specs=[near, far, far],
        out_shape=[
            pltpu.VMEM((hidden + SUB, LANE), F32),
            pltpu.HBM((nv, rows, cols), F32),
            pltpu.HBM((rows, cols), F32),
        ],
        scratch_shapes=[
            pltpu.VMEM((nv + nc + 1, tall, wide), F32),
            pltpu.VMEM((nv, tall, wide), F32),
            pltpu.VMEM((nc, tall, wide), F32),
            pltpu.VMEM((SWEEPS - 1, nv, tall, wide), F32),
            pltpu.VMEM((nv, rows, cols), F32),
            pltpu.VMEM((4, hidden, LANE), F32),
            pltpu.VMEM((hidden, hidden), F32),
            pltpu.VMEM((hidden, hidden), F32),
            pltpu.VMEM((hidden, 16), F32),
            pltpu.SemaphoreType.DMA((3,)),
        ],
        compiler_params=params(),
        name="sweeps_backward",
    )(*operands, mixing)


def clip_kernel(summed, gin, gmid, gtop, gout, gbias):
    hidden = gmid.shape[0]
    total = summed[...]
    squares = jnp.sum(jnp.sum(total * total, axis=0, keepdims=True), axis=1, keepdims=True)
    total = total * (CLIP_NORM / jnp.maximum(jnp.sqrt(squares), CLIP_NORM))
    gmid[...] = total[:hidden, :hidden]
    gtop[...] = total[:hidden, hidden:]
    low, high = total[hidden:, :hidden], total[hidden:, hidden:]
    gin[0:SUB] = low
    gin[SUB:] = high[: gin.shape[0] - SUB]
    at = gin.shape[0] - SUB
    gout[...] = high[at : at + 1]
    gbias[...] = high[at + 1 : at + 4]


def clip_all(summed, num_feat, hidden):
    shapes = [(num_feat, hidden), (hidden, hidden), (hidden, hidden), (1, hidden), (3, hidden)]
    return pl.pallas_call(
        clip_kernel,
        grid=(1,),
        in_specs=[whole(summed.shape)],
        out_specs=[whole(s) for s in shapes],
        out_shape=[jax.ShapeDtypeStruct(s, F32) for s in shapes],
        compiler_params=params(),
        name="clip",
    )(summed)


def sum_over_case(packed):
    num_x, num_y = lax.axis_size("gx"), lax.axis_size("gy")

    def swapped(x, dx, dy):
        pairs = [(i * num_y + j, (i ^ dx) * num_y + (j ^ dy)) for i in range(num_x) for j in range(num_y)]
        return lax.ppermute(x, ("gx", "gy"), pairs)

    cross = 0
    for along_y, count in ((1, num_y), (0, num_x)):
        step = 1
        while step < count:
            shifts = [k * step for k in range(1, min(4, count // step))]
            parts = [packed] + [swapped(packed, 0, k ^ cross) if along_y else swapped(packed, k, cross) for k in shifts]
            while len(parts) > 1:
                parts = [a + b for a, b in zip(parts[::2], parts[1::2])]
            packed = parts[0]
            step *= 4
            cross = cross or along_y
    return packed


def row_swaps(first, second):
    num_x, num_y = lax.axis_size("gx"), lax.axis_size("gy")
    out = []
    for start, slab in ((1, second), (0, first)):
        partner = {}
        for i in range(num_x):
            j = i + 1 if i % 2 == start else i - 1
            for y in range(num_y):
                if 0 <= j < num_x:
                    partner[i * num_y + y] = j * num_y + y
                elif num_y % 2 == 0:
                    partner[i * num_y + y] = i * num_y + (y ^ 1)
        out.append(lax.ppermute(slab, ("gx", "gy"), sorted(partner.items())))
    return out


def col_swaps(first, second):
    count = lax.axis_size("gy")
    out = []
    for start, slab in ((0, first), (1, second)):
        low = [(i, i + 1) for i in range(start, count - 1, 2)]
        if count % 2 == 0 and start == 1:
            low.append((0, count - 1))
        out.append(lax.ppermute(slab, "gy", low + [(b, a) for a, b in low]))
    return out


def shards(
    features, source, coupling, diagonal, production, bc_code, mixing,
    weight_in, weight_mid, weight_top, weight_out, biases,
):
    num_feat, rows, _ = features.shape
    hidden = weight_mid.shape[0]
    loaded = load([
        source, coupling, diagonal, bc_code, production, features,
        weight_in, weight_mid, weight_top, weight_out.reshape(1, hidden), biases,
    ])
    source, coupling, production, features, weight_in, weight_mid, weight_top, wout, biases = loaded[:9]
    inverse, second, first = loaded[9:]
    row_halos = row_swaps(first, second)
    prepared = prepare(weight_in, weight_mid, weight_top, wout, biases)
    half = rows - 32
    *net_a, beta_a = forward(features, prepared, 0, half)
    *row_halos, beta_a = lax.optimization_barrier((*row_halos, beta_a))
    first, second, *row_halos = col_slabs(source, coupling, inverse, row_halos)
    col_halos = col_swaps(first, second)
    *net_b, beta_b = forward(features, prepared, half, rows - half)
    packed, adjoint, beta = sweeps_and_backward(
        num_feat, source, coupling, inverse, production, (beta_a, beta_b), (*row_halos, *col_halos),
        (weight_mid, weight_top), (*net_a, *net_b), mixing,
    )
    grad_in, grad_mid, grad_top, grad_out, grad_bias = clip_all(sum_over_case(packed), num_feat, hidden)
    return (adjoint, beta, grad_in, grad_mid, grad_top, grad_out.reshape(hidden), grad_bias)


def solution(mesh):
    cells3 = P(None, ("case", "gx"), "gy")
    cells2 = P(("case", "gx"), "gy")
    return jax.shard_map(
        shards,
        mesh=mesh,
        in_specs=(cells3,) * 3 + (cells2,) * 3 + (P(),) * 6,
        out_specs=(cells3, cells2, P("case"), P("case"), P("case"), P("case"), P("case")),
        check_vma=False,
    )
```

```python
import functools
import itertools

import jax
import jax.numpy as jnp
from jax import lax
from jax.experimental import pallas as pl
from jax.experimental.pallas import tpu as pltpu
from jax.sharding import PartitionSpec as P

SWEEPS = 6
WALL_EXTRA = 0.2
FAR_EXTRA = 0.6
REG_WEIGHT = 0.5
CLIP_NORM = 64.0
DEPTH = SWEEPS
EDGE = 8
SUB, LANE = 8, 128
F32, BF16 = jnp.float32, jnp.bfloat16
NT = (((1,), (1,)), ((), ()))
TN = (((0,), (0,)), ((), ()))
VMEM_BYTES = 16 * 1024 * 1024


def whole(shape):
    return pl.BlockSpec(shape, lambda *_: (0,) * len(shape))


def in_hbm(x):
    return pltpu.with_memory_space_constraint(x, pltpu.HBM)


def on_chip(kernel, operands, outs, scratch=(), far=(), far_outs=(), **kwargs):
    here, there = pl.BlockSpec(memory_space=pltpu.VMEM), pl.BlockSpec(memory_space=pltpu.HBM)
    return pl.pallas_call(
        kernel,
        in_specs=[here] * len(operands) + [there] * len(far),
        out_specs=[here] * len(outs) + [there] * len(far_outs),
        out_shape=[pltpu.VMEM(*o) for o in outs] + [pltpu.HBM(*o) for o in far_outs],
        scratch_shapes=list(scratch),
        compiler_params=params(),
        **kwargs,
    )(*operands, *[in_hbm(x) for x in far])


def like(x):
    return (x.shape, x.dtype)


def params():
    return pltpu.CompilerParams(vmem_limit_bytes=VMEM_BYTES)


def inverse_diag(diag, code):
    total = diag + jnp.where(code == 1, WALL_EXTRA, 0.0) + jnp.where(code == 2, FAR_EXTRA, 0.0)
    return 1.0 / total


def is_odd(axis):
    return lax.axis_index(axis) % 2 == 1


def load_kernel(count, *refs):
    far, kept = refs[:count], refs[count : 2 * count - 2]
    inv, second, first, dia, bc, sems = refs[2 * count - 2 :]
    near = (*kept[:2], dia, bc, *kept[2:])
    copies = [pltpu.make_async_copy(far[k], near[k], sems.at[k]) for k in range(count)]
    for copy in copies:
        copy.start()
    src, cpl = near[:2]
    for copy in copies[:4]:
        copy.wait()
    nv, rows, _ = src.shape
    nc = cpl.shape[0]
    inv[...] = inverse_diag(dia[...], bc[...])
    odd = is_odd("gx")
    for f in range(nv + nc + 1):
        if f < nv + nc:
            ref, k = (src, f) if f < nv else (cpl, f - nv)
            top, bottom = ref[k, 0:16].astype(F32)[:DEPTH], ref[k, rows - 16 :].astype(F32)[16 - DEPTH :]
        else:
            top, bottom = inv[0:DEPTH], inv[rows - DEPTH :]
        first[f * DEPTH : (f + 1) * DEPTH] = jnp.where(odd, top, bottom)
        second[f * DEPTH : (f + 1) * DEPTH] = jnp.where(odd, bottom, top)
    for copy in copies[4:]:
        copy.wait()


def load(arrays):
    source, coupling, diagonal, bc_code = arrays[:4]
    nv, rows, cols = source.shape
    slab = (((nv + coupling.shape[0] + 1) * DEPTH, cols), F32)
    return on_chip(
        functools.partial(load_kernel, len(arrays)),
        [],
        [like(x) for x in (*arrays[:2], *arrays[4:])] + [((rows, cols), F32), slab, slab],
        [pltpu.VMEM(*like(diagonal)), pltpu.VMEM(*like(bc_code)), pltpu.SemaphoreType.DMA((len(arrays),))],
        far=arrays,
        name="load",
    )


def ordered(axis, first, second):
    odd, at = is_odd(axis), lax.axis_index(axis)
    before, after = jnp.where(odd, first, second), jnp.where(odd, second, first)
    return jnp.where(at == 0, 0.0, before), jnp.where(at == lax.axis_size(axis) - 1, 0.0, after)


def cols_kernel(src, cpl, inv, row_second, row_first, col_first, col_second, north, south):
    nv, rows, cols = src.shape
    nc = cpl.shape[0]
    half = col_first.shape[0]
    north[...] = jnp.zeros(north.shape, F32)
    south[...] = jnp.zeros(south.shape, F32)
    for f in range(nv + nc + 1):
        here = slice(f * DEPTH, (f + 1) * DEPTH)
        before, after = ordered("gx", row_first[here], row_second[here])
        north[f, EDGE - DEPTH :] = before
        south[f, 0:DEPTH] = after
    lane = lax.broadcasted_iota(jnp.int32, (half, LANE), 1)
    slabs = []
    for window, extra in ((slice(0, LANE), 0), (slice(cols - LANE, cols), DEPTH)):
        slab = jnp.zeros((half, LANE), F32)
        for f in range(nv + nc + 1):
            if f < nv:
                x = src[f, :, window].astype(F32)
            elif f < nv + nc:
                x = cpl[f - nv, :, window].astype(F32)
            else:
                x = inv[:, window]
            x = jnp.concatenate([north[f, :, window], x, south[f, :, window]], axis=0)
            for part, at in ((x[:half], DEPTH * f), (x[half:], DEPTH * f + LANE // 2)):
                own = jnp.logical_and(lane >= at, lane < at + DEPTH)
                slab = jnp.where(own, pltpu.roll(part, (at + extra) % LANE, 1), slab)
        slabs.append(slab)
    odd = is_odd("gy")
    col_first[...] = jnp.where(odd, slabs[0], slabs[1])
    col_second[...] = jnp.where(odd, slabs[1], slabs[0])


def col_slabs(source, coupling, inv, row_halos):
    nv, rows, cols = source.shape
    slab = (((rows + 2 * EDGE) // 2, LANE), F32)
    halo = ((nv + coupling.shape[0] + 1, EDGE, cols), F32)
    return on_chip(
        cols_kernel, [source, coupling, inv, *row_halos], [slab, slab, halo, halo], name="col_slabs"
    )


def column_of(row):
    hidden = row.shape[1]
    wide = jnp.concatenate([row, jnp.zeros((1, LANE - hidden), F32)], axis=1)
    return jnp.transpose(jnp.broadcast_to(wide, (LANE, LANE)))[:hidden]


def across(block, width):
    return jnp.concatenate([block] * (width // LANE), axis=1)


def weights_kernel(win, wmid, wtop, wout, bias, w1, w2, w3, cst):
    nf, hidden = win.shape
    step_rows, blk = hidden + 16, 16
    depth = w1.shape[1]
    feat_of = lax.broadcasted_iota(jnp.int32, (nf, depth), 1) // blk
    pick = (feat_of == lax.broadcasted_iota(jnp.int32, (nf, depth), 0)).astype(F32).astype(BF16)
    spread = lax.dot_general(win[...], pick, TN, preferred_element_type=F32)
    col = lax.broadcasted_iota(jnp.int32, (hidden, depth), 1)
    col_f = lax.broadcasted_iota(jnp.int32, (16, depth), 1)
    row_f = lax.broadcasted_iota(jnp.int32, (16, depth), 0)
    for r in range(blk):
        base = r * step_rows
        w1[base : base + hidden] = jnp.where(col % blk == r, spread, 0.0).astype(BF16)
        same = jnp.logical_and(col_f == row_f * blk + r, row_f < nf)
        w1[base + hidden : base + step_rows] = jnp.where(same, 1.0, 0.0).astype(BF16)
    w2[...] = jnp.transpose(wmid[...].astype(F32)).astype(BF16)
    w3[...] = jnp.transpose(wtop[...].astype(F32)).astype(BF16)
    for k in range(3):
        cst[k] = column_of(bias[k : k + 1, :])
    cst[3] = column_of(wout[...])


def prepare(weight_in, weight_mid, weight_top, weight_out, biases):
    nf, hidden = weight_in.shape
    depth = -(-nf * 16 // LANE) * LANE
    return on_chip(
        weights_kernel,
        [weight_in, weight_mid, weight_top, weight_out, biases],
        [
            ((16 * (hidden + 16), depth), BF16),
            ((hidden, hidden), BF16),
            ((hidden, hidden), BF16),
            ((4, hidden, LANE), F32),
        ],
        name="weights",
    )


def slope(act):
    return 1.0 - act * act


def forward_kernel(first_row, feat, w1, w2, w3, cst, acts, slopes, beta, x1):
    nf, _, cols = feat.shape
    hidden = w2.shape[0]
    step_rows, blk, per = hidden + 16, 16, 4
    x1[...] = jnp.zeros(x1.shape, BF16)
    b1, b2, b3, wo = (across(cst[k], cols) for k in range(4))

    def product(weight, parts):
        return jnp.dot(weight, jnp.concatenate(parts, axis=1), preferred_element_type=F32)

    groups = acts.shape[0] // per
    ones, twos, lines = {}, {}, []
    for s in range(groups + 2):
        rows = [range((s - lag) * per, (s - lag + 1) * per) for lag in range(3)]
        if s < groups and s * per % blk == 0:
            block = s * per // blk
            cells = feat[:, first_row + s * per : first_row + s * per + blk, :]
            x1[block, 0 : nf * blk] = cells.reshape(nf * blk, cols)
            first = jnp.dot(w1[...], x1[block], preferred_element_type=F32)
        second = product(w2[...], ones.pop(s - 1)) if 1 <= s <= groups else None
        third = product(w3[...], twos.pop(s - 2)) if s >= 2 else None
        if s < groups:
            ones[s] = []
            for r in rows[0]:
                part = first[r % blk * step_rows : (r % blk + 1) * step_rows]
                one = jnp.tanh(part[:hidden] + b1).astype(BF16)
                slopes[r, 0:hidden] = slope(one.astype(F32))
                acts[r, 0:hidden] = one
                acts[r, 2 * hidden : 2 * hidden + 16] = part[hidden:].astype(BF16)
                ones[s].append(one)
        if second is not None:
            twos[s - 1] = []
            for q, r in enumerate(rows[1]):
                two = jnp.tanh(second[:, q * cols : (q + 1) * cols] + b2).astype(BF16)
                slopes[r, hidden : 2 * hidden] = slope(two.astype(F32))
                acts[r, hidden : 2 * hidden] = two
                twos[s - 1].append(two)
        if third is not None:
            for q, r in enumerate(rows[2]):
                three = jnp.tanh(third[:, q * cols : (q + 1) * cols] + b3).astype(BF16)
                acts[r, 2 * hidden + 16 :] = three
                three = three.astype(F32)
                slopes[r, 2 * hidden :] = wo * slope(three)
                lines.append(1.0 + jnp.sum(three * wo, axis=0, keepdims=True))
                if len(lines) == SUB:
                    beta[r + 1 - SUB : r + 1, :] = jnp.concatenate(lines, axis=0)
                    lines = []


def forward(features, prepared, first_row, count):
    nf, _, cols = features.shape
    w1, w2 = prepared[:2]
    hidden = w2.shape[0]
    high = 3 * hidden + 16
    return on_chip(
        functools.partial(forward_kernel, first_row),
        [features, *prepared],
        [((count, high, cols), BF16), ((count, 3 * hidden, cols), F32), ((count, cols), F32)],
        [pltpu.VMEM((count // 16, w1.shape[1], cols), BF16)],
        cost_estimate=pl.CostEstimate(
            flops=2 * count * cols * (nf + 2 * hidden) * hidden,
            bytes_accessed=2 * count * cols * (high + nf),
            transcendentals=3 * count * cols * hidden,
        ),
        name="network_forward",
    )


def span(t, k):
    return (slice(t * SUB, (t + 1) * SUB), slice(k * LANE, (k + 1) * LANE))


class Shifts:
    def __init__(self, tiles, lanes):
        self.tiles, self.lanes = tiles, lanes
        sub = lax.broadcasted_iota(jnp.int32, (SUB, LANE), 0)
        lane = lax.broadcasted_iota(jnp.int32, (SUB, LANE), 1)
        self.first_sub, self.last_sub = sub == 0, sub == SUB - 1
        self.first_lane, self.last_lane = lane == 0, lane == LANE - 1

    def row(self, ref, lead, t):
        t = min(max(t, 0), self.tiles - 1)
        return [ref[lead + span(t, k)] for k in range(self.lanes)]

    def above(self, rows, k):
        return pltpu.roll(jnp.where(self.last_sub, rows[0][k], rows[1][k]), 1, 0)

    def below(self, rows, k):
        return pltpu.roll(jnp.where(self.first_sub, rows[2][k], rows[1][k]), SUB - 1, 0)

    def left(self, rows, k):
        return pltpu.roll(jnp.where(self.last_lane, rows[1][(k - 1) % self.lanes], rows[1][k]), 1, 1)

    def right(self, rows, k):
        other = rows[1][(k + 1) % self.lanes]
        return pltpu.roll(jnp.where(self.first_lane, other, rows[1][k]), LANE - 1, 1)

    def around(self, ref, lead, t, k_count):
        rows = [self.row(ref, lead, t + o) for o in (-1, 0, 1)]
        moves = (self.above, self.below, self.left, self.right)
        return [[move(rows, k) for move in moves] for k in range(k_count)]


def extend(src, cpl, inverse, north, south, col_halos, shifts, raw, src_x, cpl_x):
    nv, rows, cols = src.shape
    nc = cpl.shape[0]
    tall = rows + 2 * EDGE
    inner = slice(EDGE, EDGE + rows)
    lane = lax.broadcasted_iota(jnp.int32, (tall, LANE), 1)
    from_east, from_west = lane < DEPTH, lane >= LANE - DEPTH
    west, east = ordered("gy", *(x[...] for x in col_halos))
    for f in range(nv + nc + 1):
        if f < nv:
            raw[f, inner, 0:cols] = src[f].astype(F32)
        elif f < nv + nc:
            raw[f, inner, 0:cols] = cpl[f - nv].astype(F32)
        else:
            raw[f, inner, 0:cols] = inverse[...]
        raw[f, 0:EDGE, 0:cols] = north[f]
        raw[f, EDGE + rows :, 0:cols] = south[f]
        low, high = (-DEPTH * f) % LANE, (LANE // 2 - DEPTH * f) % LANE
        e = jnp.concatenate([pltpu.roll(east, at, 1) for at in (low, high)], axis=0)
        w = jnp.concatenate([pltpu.roll(west, (at - DEPTH) % LANE, 1) for at in (low, high)], axis=0)
        raw[f, :, cols:] = jnp.where(from_east, e, jnp.where(from_west, w, 0.0))
    for t in range(shifts.tiles):
        inv = shifts.row(raw, (nv + nc,), t)
        for k in range(shifts.lanes):
            for v in range(nv):
                src_x[(v,) + span(t, k)] = inv[k] * raw[(v,) + span(t, k)]
        for d, move in enumerate((shifts.above, shifts.below, shifts.left, shifts.right)):
            rows_d = [shifts.row(raw, (nv + d,), t + o) for o in (-1, 0, 1)]
            for k in range(shifts.lanes):
                cpl_x[(d,) + span(t, k)] = inv[k] * move(rows_d, k)


def adjoint_kernel(
    num_feat, src, cpl, inverse, prod, beta_a, beta_b, north, south, col_first, col_second,
    wmid, wtop, acts_a, slopes_a, acts_b, slopes_b, mix,
    packed, adj_out, beta_out,
    raw, src_x, cpl_x, adj, done, sums, g_mid, g_top, g_in, sems,
):
    nv, rows, cols = src.shape
    nc = cpl.shape[0]
    hidden, blk = wmid.shape[0], SUB
    half = beta_a.shape[0]
    tiles, lanes = (rows + 2 * EDGE) // SUB, cols // LANE + 1
    copies = [
        pltpu.make_async_copy(beta_a, beta_out.at[0:half], sems.at[0]),
        pltpu.make_async_copy(beta_b, beta_out.at[half:rows], sems.at[1]),
        pltpu.make_async_copy(done, adj_out, sems.at[2]),
    ]
    copies[0].start()
    copies[1].start()
    shifts = Shifts(tiles, lanes)
    extend(src, cpl, inverse, north, south, (col_first, col_second), shifts, raw, src_x, cpl_x)
    weights = [[mix[b, a] for a in range(nv)] for b in range(nv)]

    def sweep(number, t):
        last = number == SWEEPS
        count = lanes - 1 if last else lanes
        couple = [[cpl_x[(d,) + span(t, k)] for d in range(nc)] for k in range(count)]
        total = [[src_x[(a,) + span(t, k)] for a in range(nv)] for k in range(count)]
        for b in range(nv):
            old, lead = (src_x, (b,)) if number == 1 else (adj, (number - 2, b))
            around = shifts.around(old, lead, t, count)
            for k in range(count):
                terms = [couple[k][d] * around[k][d] for d in range(nc)]
                inc = (terms[0] + terms[1]) + (terms[2] + terms[3])
                total[k] = [total[k][a] + weights[b][a] * inc for a in range(nv)]
            yield
        for k in range(count):
            for a in range(nv):
                if last:
                    done[(a,) + span(t - EDGE // SUB, k)] = total[k][a]
                else:
                    adj[(number - 1, a) + span(t, k)] = total[k][a]

    def fold(x):
        parts = [x[:, k * LANE : (k + 1) * LANE] for k in range(cols // LANE)]
        return functools.reduce(jnp.add, parts)

    def joined(xs):
        return jnp.concatenate(xs, axis=1)

    def outer(x, d):
        return lax.dot_general(x, d, NT, preferred_element_type=F32)

    def backward(first):
        if first < half:
            acts, slopes, beta, start = acts_a, slopes_a, beta_a, first
        else:
            acts, slopes, beta, start = acts_b, slopes_b, beta_b, first - half
        here = slice(first, first + blk)
        sens = done[nv - 1, here] * prod[here] + REG_WEIGHT * (beta[start : start + blk] - 1.0)

        def layer(lo, high):
            return joined([acts[start + q, lo:high] for q in range(blk)])

        def add(ref, part):
            ref[...] = part if first == 0 else ref[...] + part

        def slanted(number, product, lo, out):
            total = jnp.zeros((hidden, LANE), F32)
            for q in range(blk):
                d = product[:, q * cols : (q + 1) * cols] * slopes[start + q, lo : lo + hidden]
                total = total + fold(d)
                out.append(d.astype(BF16))
                yield
            add(sums.at[number], total)

        out_sum, sens_rows, d3, d2, d1 = jnp.zeros((hidden, LANE), F32), [], [], [], []
        for q in range(blk):
            sen = jnp.broadcast_to(sens[q : q + 1], (hidden, cols))
            out_sum = out_sum + fold(acts[start + q, 2 * hidden + 16 :].astype(F32) * sen)
            sens_rows.append(sen)
            yield
        add(sums.at[0], out_sum)
        yield from slanted(3, joined(sens_rows), 2 * hidden, d3)
        d3 = joined(d3)
        product = jnp.dot(wtop[...], d3, preferred_element_type=F32)
        yield
        add(g_top, outer(layer(hidden, 2 * hidden), d3))
        yield
        yield from slanted(2, product, hidden, d2)
        d2 = joined(d2)
        product = jnp.dot(wmid[...], d2, preferred_element_type=F32)
        yield
        add(g_mid, outer(layer(0, hidden), d2))
        yield
        yield from slanted(1, product, 0, d1)
        add(g_in, outer(joined(d1), layer(2 * hidden, 2 * hidden + 16)))

    backward_turns = 4 * blk + 4

    def together(sweeps, back):
        turns = max(nv * len(sweeps), 1)
        sweeps = itertools.chain(*(sweep(*x) for x in sweeps))
        for turn in range(turns):
            next(sweeps, None)
            for _ in range(backward_turns * turn // turns, backward_turns * (turn + 1) // turns):
                next(back, None)
        for _ in itertools.chain(sweeps, back):
            pass

    ahead = [SWEEPS - number for number in range(SWEEPS + 1)]
    for number in range(1, SWEEPS):
        together([(number, t) for t in range(min(ahead[number] + 1, tiles))], iter(()))
    for t in range(1, tiles - 1):
        step = [(n, t + ahead[n]) for n in range(1, SWEEPS + 1) if t + ahead[n] < tiles]
        together(step, backward((t - 2) * blk) if t > 1 else iter(()))
    copies[2].start()
    together([], backward(rows - blk))

    turned = jnp.transpose(joined([g_in[...], jnp.zeros((hidden, LANE - 16), F32)]))
    tail = turned[SUB : 2 * SUB]
    row = lax.broadcasted_iota(jnp.int32, (SUB, hidden), 0)
    for k in range(4):
        line = jnp.sum(jnp.transpose(sums[k]), axis=0, keepdims=True)
        tail = tail + jnp.where(row == k + num_feat - SUB, jnp.broadcast_to(line, (SUB, hidden)), 0.0)
    packed[0:hidden, :] = joined([g_mid[...], g_top[...]])
    packed[hidden : hidden + SUB, :] = joined([turned[0:SUB], tail])
    for copy in copies:
        copy.wait()


def sweeps_and_backward(num_feat, source, coupling, inverse, production, betas, halos, weights, nets, mixing):
    nv, rows, cols = source.shape
    nc = coupling.shape[0]
    hidden = weights[0].shape[0]
    tall, wide = rows + 2 * EDGE, cols + LANE
    near, far = pl.BlockSpec(memory_space=pltpu.VMEM), pl.BlockSpec(memory_space=pltpu.HBM)
    operands = [source, coupling, inverse, production, *betas, *halos, *weights, *nets]
    return pl.pallas_call(
        functools.partial(adjoint_kernel, num_feat),
        in_specs=[near] * len(operands) + [pl.BlockSpec(memory_space=pltpu.SMEM)],
        out_specs=[near, far, far],
        out_shape=[
            pltpu.VMEM((hidden + SUB, LANE), F32),
            pltpu.HBM((nv, rows, cols), F32),
            pltpu.HBM((rows, cols), F32),
        ],
        scratch_shapes=[
            pltpu.VMEM((nv + nc + 1, tall, wide), F32),
            pltpu.VMEM((nv, tall, wide), F32),
            pltpu.VMEM((nc, tall, wide), F32),
            pltpu.VMEM((SWEEPS - 1, nv, tall, wide), F32),
            pltpu.VMEM((nv, rows, cols), F32),
            pltpu.VMEM((4, hidden, LANE), F32),
            pltpu.VMEM((hidden, hidden), F32),
            pltpu.VMEM((hidden, hidden), F32),
            pltpu.VMEM((hidden, 16), F32),
            pltpu.SemaphoreType.DMA((3,)),
        ],
        compiler_params=params(),
        name="sweeps_backward",
    )(*operands, mixing)


def clip_kernel(summed, gin, gmid, gtop, gout, gbias):
    hidden = gmid.shape[0]
    total = summed[...]
    squares = jnp.sum(jnp.sum(total * total, axis=0, keepdims=True), axis=1, keepdims=True)
    total = total * (CLIP_NORM / jnp.maximum(jnp.sqrt(squares), CLIP_NORM))
    gmid[...] = total[:hidden, :hidden]
    gtop[...] = total[:hidden, hidden:]
    low, high = total[hidden:, :hidden], total[hidden:, hidden:]
    gin[0:SUB] = low
    gin[SUB:] = high[: gin.shape[0] - SUB]
    at = gin.shape[0] - SUB
    gout[...] = high[at : at + 1]
    gbias[...] = high[at + 1 : at + 4]


def clip_all(summed, num_feat, hidden):
    shapes = [(num_feat, hidden), (hidden, hidden), (hidden, hidden), (1, hidden), (3, hidden)]
    return pl.pallas_call(
        clip_kernel,
        grid=(1,),
        in_specs=[whole(summed.shape)],
        out_specs=[whole(s) for s in shapes],
        out_shape=[jax.ShapeDtypeStruct(s, F32) for s in shapes],
        compiler_params=params(),
        name="clip",
    )(summed)


def sum_over_case(packed):
    num_x, num_y = lax.axis_size("gx"), lax.axis_size("gy")

    def swapped(x, dx, dy):
        pairs = [(i * num_y + j, (i ^ dx) * num_y + (j ^ dy)) for i in range(num_x) for j in range(num_y)]
        return lax.ppermute(x, ("gx", "gy"), pairs)

    cross = 0
    for along_y, count in ((1, num_y), (0, num_x)):
        step = 1
        while step < count:
            shifts = [k * step for k in range(1, min(4, count // step))]
            parts = [packed] + [swapped(packed, 0, k ^ cross) if along_y else swapped(packed, k, cross) for k in shifts]
            while len(parts) > 1:
                parts = [a + b for a, b in zip(parts[::2], parts[1::2])]
            packed = parts[0]
            step *= 4
            cross = cross or along_y
    return packed


def row_swaps(first, second):
    num_x, num_y = lax.axis_size("gx"), lax.axis_size("gy")
    out = []
    for start, slab in ((1, second), (0, first)):
        partner = {}
        for i in range(num_x):
            j = i + 1 if i % 2 == start else i - 1
            for y in range(num_y):
                if 0 <= j < num_x:
                    partner[i * num_y + y] = j * num_y + y
                elif num_y % 2 == 0:
                    partner[i * num_y + y] = i * num_y + (y ^ 1)
        out.append(lax.ppermute(slab, ("gx", "gy"), sorted(partner.items())))
    return out


def col_swaps(first, second):
    count = lax.axis_size("gy")
    out = []
    for start, slab in ((0, first), (1, second)):
        low = [(i, i + 1) for i in range(start, count - 1, 2)]
        if count % 2 == 0 and start == 1:
            low.append((0, count - 1))
        out.append(lax.ppermute(slab, "gy", low + [(b, a) for a, b in low]))
    return out


def shards(
    features, source, coupling, diagonal, production, bc_code, mixing,
    weight_in, weight_mid, weight_top, weight_out, biases,
):
    num_feat, rows, _ = features.shape
    hidden = weight_mid.shape[0]
    loaded = load([
        source, coupling, diagonal, bc_code, production, features,
        weight_in, weight_mid, weight_top, weight_out.reshape(1, hidden), biases,
    ])
    source, coupling, production, features, weight_in, weight_mid, weight_top, wout, biases = loaded[:9]
    inverse, second, first = loaded[9:]
    row_halos = row_swaps(first, second)
    prepared = prepare(weight_in, weight_mid, weight_top, wout, biases)
    half = rows - 32
    *net_a, beta_a = forward(features, prepared, 0, half)
    *row_halos, beta_a = lax.optimization_barrier((*row_halos, beta_a))
    first, second, *row_halos = col_slabs(source, coupling, inverse, row_halos)
    col_halos = col_swaps(first, second)
    *net_b, beta_b = forward(features, prepared, half, rows - half)
    packed, adjoint, beta = sweeps_and_backward(
        num_feat, source, coupling, inverse, production, (beta_a, beta_b), (*row_halos, *col_halos),
        (weight_mid, weight_top), (*net_a, *net_b), mixing,
    )
    grad_in, grad_mid, grad_top, grad_out, grad_bias = clip_all(sum_over_case(packed), num_feat, hidden)
    return (adjoint, beta, grad_in, grad_mid, grad_top, grad_out.reshape(hidden), grad_bias)


def solution(mesh):
    cells3 = P(None, ("case", "gx"), "gy")
    cells2 = P(("case", "gx"), "gy")
    return jax.shard_map(
        shards,
        mesh=mesh,
        in_specs=(cells3,) * 3 + (cells2,) * 3 + (P(),) * 6,
        out_specs=(cells3, cells2, P("case"), P("case"), P("case"), P("case"), P("case")),
        check_vma=False,
    )
```
